32 devices in a mesh: dp: 8 (over y, x, core), chan: 4 (over z).
Axes of the slice: x: 2, y: 2, z: 4, core: 2. Of those that a mesh axis runs over, the one named last changes fastest.
Arguments:
- images: bfloat16 [512, 64, 192], P('dp', 'chan'), may hold values from -6 to 6
- labels: int32 [512], P('dp'), may hold values from 0 to 999
- resolution: int32 [512], P('dp'), may hold values from 6 to 8
- class_weight: float32 [1000], replicated, may hold values from 0.5 to 7.5
- column_master: float32 [1826, 1152], P(None, 'chan'), may hold values from -0.4375 to 0.4375
- column_first: float32 [1826, 1152], P(None, 'chan'), may hold values from -9.536743e-06 to 9.536743e-06
- column_second: float32 [1826, 1152], P(None, 'chan'), may hold values from 2e-14 to 3.2e-13
- column_average: float32 [1826, 1152], P(None, 'chan'), may hold values from -0.4375 to 0.4375
- row_master: float32 [1152, 2800], P('chan'), may hold values from -0.1875 to 0.1875
- row_first: float32 [1152, 2800], P('chan'), may hold values from -9.536743e-06 to 9.536743e-06
- row_second: float32 [1152, 2800], P('chan'), may hold values from 2e-14 to 3.2e-13
- row_average: float32 [1152, 2800], P('chan'), may hold values from -0.1875 to 0.1875
- head_master: float32 [3560, 1280], P(None, ('dp', 'chan')), may hold values from -0.3125 to 0.3125
- head_first: float32 [3560, 1280], P(None, ('dp', 'chan')), may hold values from -9.536743e-06 to 9.536743e-06
- head_second: float32 [3560, 1280], P(None, ('dp', 'chan')), may hold values from 2e-14 to 3.2e-13
- head_average: float32 [3560, 1280], P(None, ('dp', 'chan')), may hold values from -0.3125 to 0.3125
- route_master: float32 [512, 8], replicated, may hold values from -3 to 3
- route_first: float32 [512, 8], replicated, may hold values from -9.536743e-06 to 9.536743e-06
- route_second: float32 [512, 8], replicated, may hold values from 2e-14 to 3.2e-13
- route_average: float32 [512, 8], replicated, may hold values from -3 to 3
Outputs:
- column_moment: float32 [1826, 1152], P(None, 'chan')
- column_variance: float32 [1826, 1152], P(None, 'chan')
- column_updated: float32 [1826, 1152], P(None, 'chan')
- column_smoothed: float32 [1826, 1152], P(None, 'chan')
- column_halves: bfloat16 [1826, 1152], P(None, 'chan')
- row_moment: float32 [1152, 2800], P('chan')
- row_variance: float32 [1152, 2800], P('chan')
- row_updated: float32 [1152, 2800], P('chan')
- row_smoothed: float32 [1152, 2800], P('chan')
- row_halves: bfloat16 [1152, 2800], P('chan')
- head_moment: float32 [3560, 1280], P(None, ('dp', 'chan'))
- head_variance: float32 [3560, 1280], P(None, ('dp', 'chan'))
- head_updated: float32 [3560, 1280], P(None, ('dp', 'chan'))
- head_smoothed: float32 [3560, 1280], P(None, ('dp', 'chan'))
- head_halves: bfloat16 [3560, 1280], P(None, ('dp', 'chan'))
- route_moment: float32 [512, 8], replicated
- route_variance: float32 [512, 8], replicated
- route_updated: float32 [512, 8], replicated
- route_smoothed: float32 [512, 8], replicated
- route_halves: bfloat16 [512, 8], replicated
- loss_total: float32 [], replicated
- weight_total: float32 [], replicated
- clip_norm: float32 [], replicated
The draws below stay inside these ranges and needn't reach their ends.
All inputs are finite; a program needn't handle non-finite values.
Results may differ from the reference program's by a relative error of at most 0.0059.
Values may be sent and summed in bfloat16 or wider, within the bound.
No kernel may reach another device: no remote copies, remote signals or barrier semaphores. Data moves between devices by JAX's collectives and lax.ppermute only.
A program may use at most 576 MiB of HBM per device.

```python
import math
import jax
import jax.numpy as jnp
from jax import lax

C0 = 192
E = 1152
C2 = 320
SE = 48
H = 1280
CLASSES = 1000
NE = 8
KERNEL = 5
MAP = 8
STEP = 10
IMG_DEV = 64
IMAGES = 512
COLR = 1826
ROWC = 2800
HEADR = 3560
ROUTR = 512


def draw_labels(key, part):
    band = jnp.arange(IMAGES, dtype=jnp.int32) // IMG_DEV
    devices = IMAGES // IMG_DEV
    lower = band * CLASSES // devices
    upper = (band + 1) * CLASSES // devices
    picked = jax.random.randint(key, (IMAGES,), 0, 1 << 20, dtype=jnp.int32)
    return lower + picked % (upper - lower)


def draw_class_weight(key, part):
    ranks = jnp.arange(CLASSES, dtype=jnp.float32) / CLASSES
    factor = jax.random.uniform(key, (CLASSES,), jnp.float32, 0.75, 1.25)
    rising = 1.0 + 2.0 * ranks
    return (rising * factor).astype(jnp.float32)


def with_ends(entries, rng, smallest, largest):
    spot = [jax.random.randint(jax.random.fold_in(rng, axis), (), 0, length) for axis, length in enumerate(entries.shape)]
    widest = entries.shape.index(max(entries.shape))
    neighbour = spot[:widest] + [(spot[widest] + 1) % entries.shape[widest]] + spot[widest + 1:]
    return entries.at[tuple(spot)].set(smallest).at[tuple(neighbour)].set(largest)


def block_levels(own_key, dims, shards, least, high):
    def one(axis_at, parts):
        steps = jax.random.uniform(jax.random.fold_in(jax.random.fold_in(own_key, 6), axis_at), (parts,), jnp.float32, least / len(shards), high / len(shards))
        return jnp.repeat(jnp.exp(steps), dims[axis_at] // parts).reshape((-1,) + (1,) * (len(dims) - axis_at - 1))

    factor_of = one(*shards[0])
    for cut in shards[1:]:
        factor_of = factor_of * one(*cut)
    return factor_of


def bell_draw(own_key, extent, width, limit, split=(), kind=jnp.bfloat16):
    entries = width * jax.random.normal(own_key, extent, jnp.float32)
    if split:
        entries = entries * block_levels(own_key, extent, split, -0.22, 0.18)
    return jnp.clip(entries, -limit, limit).astype(kind)


def setup_inputs(seed: int = 0) -> dict:
    streams_of = jax.random.split(jax.random.key(seed), 21)
    return {
        "images": bell_draw(streams_of[0], (IMAGES, MAP * MAP, C0), 1.0, 6.0, ((0, 8), (1, 4))),
        "labels": draw_labels(jax.random.fold_in(streams_of[20], 71), 0),
        "resolution": with_ends(jax.random.randint(streams_of[2], (IMAGES,), 6, 9), jax.random.fold_in(streams_of[2], 1), 6, 8).astype(jnp.int32),
        "class_weight": draw_class_weight(jax.random.fold_in(streams_of[20], 71), 0),
        "column_master": bell_draw(streams_of[4], (COLR, E), C0 ** -0.5, 0.4375, ((1, 4),), jnp.float32),
        "column_first": bell_draw(streams_of[5], (COLR, E), (7e-7), 9.5367431640625e-06, ((1, 4),), jnp.float32),
        "column_second": jnp.clip(jnp.exp(math.log(3.199999943845344e-13) - 2.7725887 * jax.random.uniform(streams_of[6], (COLR, E), jnp.float32) ** block_levels(streams_of[6], (COLR, E), ((1, 4),), -0.2, 0.2)), 1.99999996490334e-14, 3.199999943845344e-13),
        "column_average": bell_draw(streams_of[7], (COLR, E), C0 ** -0.5, 0.4375, ((1, 4),), jnp.float32),
        "row_master": bell_draw(streams_of[8], (E, ROWC), E ** -0.5, 0.1875, ((0, 4),), jnp.float32),
        "row_first": bell_draw(streams_of[9], (E, ROWC), (7e-7), 9.5367431640625e-06, ((0, 4),), jnp.float32),
        "row_second": jnp.clip(jnp.exp(math.log(3.199999943845344e-13) - 2.7725887 * jax.random.uniform(streams_of[10], (E, ROWC), jnp.float32) ** block_levels(streams_of[10], (E, ROWC), ((0, 4),), -0.2, 0.2)), 1.99999996490334e-14, 3.199999943845344e-13),
        "row_average": bell_draw(streams_of[11], (E, ROWC), E ** -0.5, 0.1875, ((0, 4),), jnp.float32),
        "head_master": bell_draw(streams_of[12], (HEADR, H), C2 ** -0.5, 0.3125, ((1, 32),), jnp.float32),
        "head_first": bell_draw(streams_of[13], (HEADR, H), (7e-7), 9.5367431640625e-06, ((1, 32),), jnp.float32),
        "head_second": jnp.clip(jnp.exp(math.log(3.199999943845344e-13) - 2.7725887 * jax.random.uniform(streams_of[14], (HEADR, H), jnp.float32) ** block_levels(streams_of[14], (HEADR, H), ((1, 32),), -0.2, 0.2)), 1.99999996490334e-14, 3.199999943845344e-13),
        "head_average": bell_draw(streams_of[15], (HEADR, H), C2 ** -0.5, 0.3125, ((1, 32),), jnp.float32),
        "route_master": bell_draw(streams_of[16], (ROUTR, NE), 0.4, 3.0, (), jnp.float32),
        "route_first": bell_draw(streams_of[17], (ROUTR, NE), (7e-7), 9.5367431640625e-06, (), jnp.float32),
        "route_second": jnp.clip(jnp.exp(jax.random.uniform(streams_of[18], (ROUTR, NE), jnp.float32, math.log(1.99999996490334e-14), math.log(3.199999943845344e-13))), 1.99999996490334e-14, 3.199999943845344e-13),
        "route_average": bell_draw(streams_of[19], (ROUTR, NE), 0.4, 3.0, (), jnp.float32),
    }


HIGH = lax.Precision.HIGHEST
BIG = lax.Precision.HIGHEST
BETA_ONE = 0.9
BETA_TWO = 0.999
EPSILON = 1e-08
DECAY = 0.05
RATE = 0.05
CLIP = 0.02
SMOOTH = 0.9

@jax.custom_vjp
def low(v):
    return lax.optimization_barrier(v.astype(jnp.bfloat16)).astype(jnp.float32)

@jax.custom_vjp
def low_back(v):
    return v

def low_keep(v):
    return (low(v), None)

def low_pass(kept, grad):
    return (grad,)

def back_keep(v):
    return (v, None)

def back_low(kept, grad):
    return (low(grad),)
low.defvjp(low_keep, low_pass)
low_back.defvjp(back_keep, back_low)

def swish(values):
    return values * jax.nn.sigmoid(values)

def depthwise(inputs, kernel):
    batches, channels = (inputs.shape[0], inputs.shape[-1])
    margin = KERNEL // 2
    padded = jnp.pad(inputs.reshape(batches, MAP, MAP, channels), ((0, 0), (margin, margin), (margin, margin), (0, 0)))
    summed = jnp.zeros((batches, MAP, MAP, channels), jnp.float32)
    for offset in range(KERNEL * KERNEL):
        down_step, side_step = (offset // KERNEL, offset % KERNEL)
        summed = summed + padded[:, down_step:down_step + MAP, side_step:side_step + MAP, :] * kernel[offset]
    return summed.reshape(batches, MAP * MAP, channels)

def unpack(column_pack, row_pack, head_pack, route_pack):
    taps = KERNEL * KERNEL
    begin = C0 + 2 * taps + SE
    return (column_pack[:C0], column_pack[C0:C0 + taps], row_pack[:, :C0], route_pack[:C0], column_pack[begin:].reshape(NE, C0, column_pack.shape[1]), column_pack[C0 + taps:C0 + 2 * taps], row_pack[:, C0:C0 + SE], column_pack[C0 + 2 * taps:begin], row_pack[:, C0 + SE:].reshape(row_pack.shape[0], NE, C2).transpose(1, 0, 2), route_pack[C0:], head_pack[:NE * C2].reshape(NE, C2, head_pack.shape[1]), head_pack[NE * C2:])

def mask_count(resolution):
    spots = jnp.arange(MAP * MAP, dtype=jnp.int32)
    inside = ((spots // MAP)[None, :] < resolution[:, None]) & ((spots % MAP)[None, :] < resolution[:, None])
    return (inside.astype(jnp.float32)[:, :, None], (resolution * resolution).astype(jnp.float32)[:, None])

def first_block(first_in, first_kernel, first_out, inputs, valid_mask):
    expanded = low_back(jnp.einsum('bpc,cf->bpf', low(inputs), low(first_in), precision=BIG))
    depth_out = swish(depthwise(swish(expanded) * valid_mask, first_kernel)) * valid_mask
    return jnp.einsum('bpf,fo->bpo', low(depth_out), low(first_out), precision=BIG)

def route_logits(router, hidden, valid_mask, pixel_count):
    return jnp.dot(lax.optimization_barrier(jnp.sum(hidden * valid_mask, 1)) / pixel_count, router, precision=HIGH)

def second_expand(expert_in, kernel, inputs, gating, valid_mask):
    expanded = low_back(jnp.einsum('bpc,ecf->bpef', low(inputs), low(expert_in), precision=BIG))
    mixed = jnp.einsum('bpef,be->bpf', expanded, gating, precision=HIGH)
    return swish(depthwise(swish(mixed) * valid_mask, kernel)) * valid_mask

def squeeze(excite_in, depth_out, pixel_count):
    return jnp.dot(lax.optimization_barrier(jnp.sum(depth_out, 1)) / pixel_count, excite_in, precision=HIGH)

def second_project(excite_out, expert_out, depth_out, squeezed, gating):
    excite = jax.nn.sigmoid(jnp.dot(swish(squeezed), excite_out, precision=HIGH))
    projected = low_back(jnp.einsum('bpf,efo->bpeo', low(depth_out * excite[:, None, :]), low(expert_out), precision=BIG))
    return jnp.einsum('bpeo,be->bpo', projected, gating, precision=HIGH)

def head_block(head_experts, hidden, gating, valid_mask, pixel_count):
    expanded = low_back(jnp.einsum('bpo,eoh->bpeh', low(hidden), low(head_experts), precision=BIG))
    feature = swish(jnp.einsum('bpeh,be->bph', expanded, gating, precision=HIGH)) * valid_mask
    return lax.optimization_barrier(jnp.sum(feature, 1)) / pixel_count

def class_loss(classifier, pooled, onehot, weight):
    logits = low_back(jnp.dot(low(pooled), low(classifier).T, precision=BIG))
    top = lax.optimization_barrier(jnp.max(logits, 1, keepdims=True))
    spread = top[:, 0] + jnp.log(lax.optimization_barrier(jnp.sum(jnp.exp(logits - top), 1)))
    return jnp.sum(weight * (spread - lax.optimization_barrier(jnp.sum(logits * onehot, 1))))

def block_loss(column_pack, row_pack, head_pack, route_pack, images, labels, resolution, class_weight):
    first_in, first_kernel, first_out, route_in, expert_in, second_kernel, excite_in, excite_out, expert_out, route_out, head_experts, classifier = unpack(column_pack, row_pack, head_pack, route_pack)
    valid_mask, pixel_count = mask_count(resolution)
    onehot = (labels[:, None] == jnp.arange(CLASSES, dtype=jnp.int32)[None, :]).astype(jnp.float32)
    weight = jnp.dot(onehot, class_weight, precision=HIGH)
    entry_rows = images * valid_mask
    hidden = entry_rows + low_back(first_block(first_in, first_kernel, first_out, entry_rows, valid_mask))
    gating = jax.nn.sigmoid(route_logits(route_in, hidden, valid_mask, pixel_count))
    depth_out = second_expand(expert_in, second_kernel, hidden, gating, valid_mask)
    squeezed = squeeze(excite_in, depth_out, pixel_count)
    narrow = low_back(second_project(excite_out, expert_out, depth_out, squeezed, gating))
    head_gating = jax.nn.sigmoid(route_logits(route_out, narrow, valid_mask, pixel_count))
    pooled = head_block(head_experts, narrow, head_gating, valid_mask, pixel_count)
    return class_loss(classifier, pooled, onehot, weight)

def adamw(master, first, second, average, grad):
    first = BETA_ONE * first + (1.0 - BETA_ONE) * grad
    second = BETA_TWO * second + (1.0 - BETA_TWO) * grad * grad
    ratio = first / (1.0 - BETA_ONE ** STEP) / (jnp.sqrt(second / (1.0 - BETA_TWO ** STEP)) + EPSILON)
    master = master - RATE * (ratio + DECAY * master)
    average = SMOOTH * average + (1.0 - SMOOTH) * master
    return (first, second, master, average, master.astype(jnp.bfloat16))

def reference(images, labels, resolution, class_weight, column_master, column_first, column_second, column_average, row_master, row_first, row_second, row_average, head_master, head_first, head_second, head_average, route_master, route_first, route_second, route_average):
    block = math.gcd(IMAGES, 16)
    rounds = IMAGES // block
    pictures = images.astype(jnp.float32).reshape(rounds, block, MAP * MAP, C0)
    packs = (column_master, row_master, head_master, route_master)

    def accumulate(carry, item):
        picture, label_block, size_block = item

        def loss_of(first_pack, second_pack, third_pack, fourth_pack):
            return block_loss(first_pack, second_pack, third_pack, fourth_pack, picture, label_block, size_block, class_weight)
        value, pull = jax.vjp(loss_of, column_master, row_master, head_master, route_master)
        grads = pull(jnp.ones((), jnp.float32))
        return ((carry[0] + value, tuple((left + right for left, right in zip(carry[1], grads)))), None)
    start = (jnp.zeros((), jnp.float32), tuple((jnp.zeros_like(array) for array in packs)))
    (loss_total, grads), unused = lax.scan(accumulate, start, (pictures, labels.reshape(rounds, block), resolution.reshape(rounds, block)))
    weight_total = jnp.sum(class_weight[labels])
    scaled = tuple((grad / weight_total for grad in grads))
    clip_norm = jnp.sqrt(sum((jnp.sum(grad * grad) for grad in scaled)))
    factor = jnp.minimum(1.0, CLIP / (clip_norm + 1e-06))
    column_out = adamw(column_master, column_first, column_second, column_average, scaled[0] * factor)
    row_out = adamw(row_master, row_first, row_second, row_average, scaled[1] * factor)
    head_out = adamw(head_master, head_first, head_second, head_average, scaled[2] * factor)
    route_out = adamw(route_master, route_first, route_second, route_average, scaled[3] * factor)
    return (column_out[0], column_out[1], column_out[2], column_out[3], column_out[4], row_out[0], row_out[1], row_out[2], row_out[3], row_out[4], head_out[0], head_out[1], head_out[2], head_out[3], head_out[4], route_out[0], route_out[1], route_out[2], route_out[3], route_out[4], loss_total, weight_total, clip_norm)
```

```python
import functools
import math

import jax
import jax.numpy as jnp
from jax import lax
from jax.experimental import pallas as pl
from jax.experimental.pallas import tpu as pltpu
from jax.sharding import Mesh
from jax.sharding import PartitionSpec as P

C0 = 192
C2 = 320
SE = 48
CLASSES = 1000
NE = 8
HALF = NE // 2
KERNEL = 5
TAPS = KERNEL * KERNEL
MAP = 8
STEP = 10
LANES = 128

HIGH = lax.Precision.HIGHEST
BETA_ONE = 0.9
BETA_TWO = 0.999
EPSILON = 1e-08
DECAY = 0.05
RATE = 0.05
CLIP = 0.02
SMOOTH = 0.9

F32 = jnp.float32
BF16 = jnp.bfloat16
VMEM_BYTES = 60 * 1024 * 1024


def nn(left, right):
    return jnp.dot(left, right, preferred_element_type=F32)


def nt(left, right):
    return lax.dot_general(left, right, (((1,), (1,)), ((), ())), preferred_element_type=F32)


def high_nn(left, right):
    return jnp.dot(left, right, precision=HIGH, preferred_element_type=F32)


def high_nt(left, right):
    return lax.dot_general(
        left, right, (((1,), (1,)), ((), ())), precision=HIGH, preferred_element_type=F32
    )


def high_tn(left, right):
    return lax.dot_general(
        left, right, (((0,), (0,)), ((), ())), precision=HIGH, preferred_element_type=F32
    )


def sig(values):
    return 0.5 * jnp.tanh(0.5 * values) + 0.5


def slope(values, gate):
    return gate * (1.0 + values * (1.0 - gate))


def loop(count, body):
    def step(index, carry):
        body(index)
        return carry

    lax.fori_loop(0, count, step, 0)


def rows_at(index, count):
    return pl.ds(pl.multiple_of(index * count, count), count)


def lanes_at(index):
    return pl.ds(pl.multiple_of(index * LANES, LANES), LANES)


def depthwise(source, taps, lanes, batch, flip, emit):
    parts = batch // 8
    weights = [taps[TAPS - 1 - t if flip else t, :, lanes] for t in range(TAPS)]
    for down in range(MAP):
        total = {}
        for step_y in range(-2, 3):
            line = down + step_y
            if not 0 <= line < MAP:
                continue
            for spot in range(MAP):
                for part in range(parts):
                    value = source[pl.ds((line * MAP + spot) * batch + 8 * part, 8), lanes]
                    for step_x in range(-2, 3):
                        place = spot - step_x
                        if not 0 <= place < MAP:
                            continue
                        term = value * weights[(step_y + 2) * KERNEL + step_x + 2]
                        key = (place, part)
                        total[key] = total[key] + term if key in total else term
        for (place, part), value in total.items():
            emit((down * MAP + place) * batch + 8 * part, value)


def depthwise_weight(source, grad, lanes, batch, store):
    parts = batch // 8
    total = {}
    for down in range(MAP):
        slopes = {
            (spot, part): grad[pl.ds((down * MAP + spot) * batch + 8 * part, 8), lanes]
            for spot in range(MAP)
            for part in range(parts)
        }
        for step_y in range(-2, 3):
            line = down + step_y
            if not 0 <= line < MAP:
                continue
            for spot in range(MAP):
                for part in range(parts):
                    value = source[pl.ds((line * MAP + spot) * batch + 8 * part, 8), lanes]
                    for step_x in range(-2, 3):
                        place = spot - step_x
                        if not 0 <= place < MAP:
                            continue
                        tap = (step_y + 2) * KERNEL + step_x + 2
                        term = value * slopes[(place, part)]
                        total[tap] = total[tap] + term if tap in total else term
    for tap in range(TAPS):
        store(tap, jnp.sum(total[tap], axis=0, keepdims=True))


def pair_gates(gates, width):
    batch = gates.shape[0]
    spots = lax.broadcasted_iota(jnp.int32, (batch, 2 * width), 1)
    out = []
    for pair in range(HALF):
        left = jnp.broadcast_to(gates[:, 2 * pair : 2 * pair + 1], (batch, 2 * width))
        right = jnp.broadcast_to(gates[:, 2 * pair + 1 : 2 * pair + 2], (batch, 2 * width))
        out.append(jnp.where(spots < width, left, right))
    return out


def split_sums(values, width):
    columns = []
    for value in values:
        spots = lax.broadcasted_iota(jnp.int32, value.shape, 1)
        columns.append(jnp.sum(jnp.where(spots < width, value, 0.0), axis=1, keepdims=True))
        columns.append(jnp.sum(jnp.where(spots < width, 0.0, value), axis=1, keepdims=True))
    return jnp.concatenate(columns, axis=1)


def grouped(values, batch):
    return values.reshape(values.shape[0] // batch, batch, values.shape[1])


def flat(values):
    return values.reshape(values.shape[0] * values.shape[1], values.shape[2])


def first_forward(
    x_ref, left_ref, right_ref, taps_ref, mask_ref, count_ref, route_ref,
    conv_ref, wide_ref, twice_ref, mean_ref, gate_ref, small_gates_ref, large_gates_ref,
    act, deep, total,
):
    batch, tile = count_ref.shape[0], act.shape[1]
    line = MAP * batch
    step = pl.program_id(0)

    def expand(index):
        rows = rows_at(index, line)
        value = nt(x_ref[rows, :], left_ref[:, :C0])
        for part in range(tile // LANES):
            here = value[:, part * LANES : (part + 1) * LANES]
            act[rows, part * LANES : (part + 1) * LANES] = here * sig(here) * mask_ref[rows, :]

    loop(MAP, expand)

    def conv(index):
        lanes = lanes_at(index)

        def emit(row, value):
            conv_ref[pl.ds(row, 8), lanes] = value

        depthwise(act, taps_ref, lanes, batch, False, emit)

    loop(tile // LANES, conv)

    def activate(index):
        rows = rows_at(index, line)
        for part in range(tile // LANES):
            lanes = slice(part * LANES, (part + 1) * LANES)
            here = conv_ref[rows, lanes]
            deep[rows, lanes] = (here * sig(here) * mask_ref[rows, :]).astype(BF16)

    loop(MAP, activate)
    part_sum = nn(deep[...], right_ref[:, :C0])

    @pl.when(step == 0)
    def _():
        total[...] = part_sum

    @pl.when(step > 0)
    def _():
        total[...] += part_sum

    @pl.when(step == pl.num_programs(0) - 1)
    def _():
        mean_ref[...] = jnp.zeros_like(mean_ref)

        def finish(index):
            rows = rows_at(index, line)
            value = x_ref[rows, :].astype(F32) + total[rows, :]
            low = value.astype(BF16)
            twice_ref[rows, :C0] = low
            twice_ref[rows, C0:] = low
            for part in range(2):
                lanes = slice(0, LANES) if part == 0 else slice(LANES, C0)
                kept = value[:, lanes] * mask_ref[rows, : lanes.stop - lanes.start]
                mean_ref[:, lanes] += jnp.sum(grouped(kept, batch), axis=0)

        loop(MAP, finish)
        mean_ref[...] = mean_ref[...] / count_ref[:, :1]
        gates = jax.nn.sigmoid(high_nn(mean_ref[...], route_ref[...]))
        gate_ref[...] = gates
        for pair, value in enumerate(pair_gates(gates, C0)):
            small_gates_ref[pair] = value
        for pair, value in enumerate(pair_gates(gates, C2)):
            large_gates_ref[pair] = value

        def widen(index):
            rows = rows_at(index, line)
            value = grouped(twice_ref[rows, :].astype(F32), batch)
            for pair in range(HALF):
                lanes = slice(pair * 2 * C0, (pair + 1) * 2 * C0)
                wide_ref[rows, lanes] = flat(value * small_gates_ref[pair][None]).astype(BF16)

        loop(MAP, widen)


def second_forward(
    wide_ref, own_ref, far_ref, taps_ref, mask_ref, count_ref, squeeze_ref, excite_ref,
    mixed_ref, conv_ref, mean_ref, units_ref, scale_ref,
    act,
):
    batch, tile = count_ref.shape[0], act.shape[1]
    line = MAP * batch
    step = pl.program_id(0)
    half = own_ref.shape[1]

    def expand(index):
        rows = rows_at(index, 2 * line)
        mixed_ref[rows, :] = nt(wide_ref[rows, :half], own_ref[...]) + nt(
            wide_ref[rows, half:], far_ref[...]
        )

    loop(MAP // 2, expand)

    def activate(index):
        rows = rows_at(index, line)
        for part in range(tile // LANES):
            lanes = slice(part * LANES, (part + 1) * LANES)
            here = mixed_ref[rows, lanes]
            act[rows, lanes] = here * sig(here) * mask_ref[rows, :]

    loop(MAP, activate)

    def conv(index):
        lanes = lanes_at(index)

        def emit(row, value):
            conv_ref[pl.ds(row, 8), lanes] = value

        depthwise(act, taps_ref, lanes, batch, False, emit)

    loop(tile // LANES, conv)
    mean_ref[...] = jnp.zeros_like(mean_ref)

    def pool(index):
        rows = rows_at(index, line)
        for part in range(tile // LANES):
            lanes = slice(part * LANES, (part + 1) * LANES)
            here = conv_ref[rows, lanes]
            kept = here * sig(here) * mask_ref[rows, :]
            mean_ref[:, lanes] += jnp.sum(grouped(kept, batch), axis=0)

    loop(MAP, pool)
    mean_ref[...] = mean_ref[...] / count_ref[:, :1]
    units = high_nn(mean_ref[...], squeeze_ref[...])

    @pl.when(step == 0)
    def _():
        units_ref[...] = units

    @pl.when(step > 0)
    def _():
        units_ref[...] += units

    @pl.when(step == pl.num_programs(0) - 1)
    def _():
        value = units_ref[...]
        scale_ref[...] = jax.nn.sigmoid(high_nt(value * jax.nn.sigmoid(value), excite_ref[...]))


def project(
    conv_ref, scale_ref, own_ref, far_ref, mask_ref, count_ref, gates_ref, route_ref,
    each_ref, twice_ref, wide_ref, mean_ref, gate_ref, head_gates_ref,
    scaled,
):
    batch = count_ref.shape[0]
    line = MAP * batch
    width = scaled.shape[1]

    def activate(index):
        rows = rows_at(index, line)
        for part in range(width // LANES):
            lanes = slice(part * LANES, (part + 1) * LANES)
            here = conv_ref[rows, lanes]
            kept = grouped(here * sig(here) * mask_ref[rows, :], batch)
            scaled[rows, lanes] = flat(kept * scale_ref[:, lanes][None]).astype(BF16)

    loop(MAP, activate)
    mean_ref[...] = jnp.zeros_like(mean_ref)
    pairs = HALF // 2

    def mix(index):
        rows = rows_at(index, 2 * line)
        value = scaled[rows, :]
        total = None
        for pair in range(HALF):
            weights = own_ref if pair < pairs else far_ref
            inner = slice((pair % pairs) * 2 * C2, (pair % pairs + 1) * 2 * C2)
            each = nn(value, weights[:, inner])
            each_ref[rows, pair * 2 * C2 : (pair + 1) * 2 * C2] = each.astype(BF16)
            term = grouped(each, batch) * gates_ref[pair][None]
            total = term if total is None else total + term
        total = flat(total)
        value = total[:, :C2] + total[:, C2:]
        low = value.astype(BF16)
        twice_ref[rows, :C2] = low
        twice_ref[rows, C2:] = low
        kept = grouped(value * mask_ref[rows, :1], batch)
        mean_ref[...] += jnp.sum(kept, axis=0)

    loop(MAP // 2, mix)
    mean_ref[...] = mean_ref[...] / count_ref[:, :1]
    gates = jax.nn.sigmoid(high_nn(mean_ref[...], route_ref[...]))
    gate_ref[...] = gates
    for pair, value in enumerate(pair_gates(gates, C2)):
        head_gates_ref[pair] = value

    def widen(index):
        rows = rows_at(index, line)
        value = grouped(twice_ref[rows, :].astype(F32), batch)
        for pair in range(HALF):
            lanes = slice(pair * 2 * C2, (pair + 1) * 2 * C2)
            wide_ref[rows, lanes] = flat(value * head_gates_ref[pair][None]).astype(BF16)

    loop(MAP, widen)


def head(
    wide_ref, twice_ref, own_ref, far_ref, mask_ref, count_ref, label_ref, class_ref,
    gates_ref, gate_ref, mean_ref, route_ref,
    expert_grad_ref, class_grad_ref, loss_ref, hidden_grad_ref, route_grad_ref,
    mixed, slopes, turned, pooled, total,
):
    batch = count_ref.shape[0]
    line = MAP * batch
    step = pl.program_id(0)
    half = own_ref.shape[0]
    experts = NE * C2
    columns = expert_grad_ref.shape[2]
    sides = (own_ref, far_ref)

    @pl.when(step == 0)
    def _():
        pooled[...] = jnp.zeros_like(pooled)
        for side, weights in enumerate(sides):

            def expand(index, side=side, weights=weights):
                rows = rows_at(index, 2 * line)
                mixed[rows, side * half : (side + 1) * half] = nt(
                    wide_ref[rows, :], weights[:, :experts]
                )

            loop(MAP // 2, expand)

        def pool(index):
            rows = rows_at(index, line)
            for part in range(2 * half // LANES):
                lanes = slice(part * LANES, (part + 1) * LANES)
                here = mixed[rows, lanes]
                kept = here * sig(here) * mask_ref[rows, :]
                pooled[:, lanes] += jnp.sum(grouped(kept, batch), axis=0)

        loop(MAP, pool)
        mean = (pooled[...] / count_ref[:, :1]).astype(BF16)
        logits = nn(mean[:, :half], own_ref[:, experts:]) + nn(mean[:, half:], far_ref[:, experts:])
        spots = lax.broadcasted_iota(jnp.int32, logits.shape, 1)
        onehot = (spots == label_ref[...]).astype(F32)
        weight = jnp.sum(onehot * class_ref[...], axis=1, keepdims=True)
        top = jnp.max(logits, axis=1, keepdims=True)
        powers = jnp.exp(logits - top)
        summed = jnp.sum(powers, axis=1, keepdims=True)
        loss = weight * (top + jnp.log(summed) - jnp.sum(logits * onehot, axis=1, keepdims=True))
        loss_ref[...] = jnp.concatenate([loss, weight], axis=1)
        logit_grad = (weight * (powers / summed - onehot)).astype(BF16)
        for side, weights in enumerate(sides):
            place = slice(side * half, (side + 1) * half)
            class_grad_ref[side] = lax.dot_general(
                mean[:, place], logit_grad, (((0,), (0,)), ((), ())), preferred_element_type=F32
            )
            pooled[:, place] = nt(logit_grad, weights[:, experts:]) / count_ref[:, :1]

        def back(index):
            rows = rows_at(index, line)
            for part in range(2 * half // LANES):
                lanes = slice(part * LANES, (part + 1) * LANES)
                here = mixed[rows, lanes]
                value = grouped(mask_ref[rows, :] * slope(here, sig(here)), batch)
                slopes[rows, lanes] = flat(value * pooled[:, lanes][None]).astype(BF16)

        loop(MAP, back)
        for part in range(2 * half // LANES):
            turned[part * LANES : (part + 1) * LANES, :] = slopes[
                :, part * LANES : (part + 1) * LANES
            ].T

    blocks = experts // columns
    side = 1 - step // blocks
    block = step % blocks
    expert_grad_ref[0] = nn(
        turned[pl.ds(pl.multiple_of(side * half, half), half), :],
        wide_ref[:, pl.ds(pl.multiple_of(block * columns, columns), columns)],
    )

    @pl.when(step == pl.num_programs(0) - 1)
    def _():
        sums = [jnp.zeros((batch, 2 * C2), F32)] * HALF

        def pull(index, sums):
            rows = rows_at(index, 2 * line)
            left, right = (slopes[rows, :half], slopes[rows, half:])
            hidden = grouped(twice_ref[rows, :].astype(F32), batch)
            summed = None
            sums = list(sums)
            for pair in range(HALF):
                lanes = slice(pair * 2 * C2, (pair + 1) * 2 * C2)
                each = grouped(nn(left, own_ref[:, lanes]) + nn(right, far_ref[:, lanes]), batch)
                sums[pair] = sums[pair] + jnp.sum(each * hidden, axis=0)
                term = each * gates_ref[pair][None]
                summed = term if summed is None else summed + term
            summed = flat(summed)
            total[rows, :] = summed[:, :C2] + summed[:, C2:]
            return tuple(sums)

        sums = lax.fori_loop(0, MAP // 2, pull, tuple(sums))
        gates = gate_ref[...]
        logit = split_sums(sums, C2) * gates * (1.0 - gates)
        route_grad_ref[...] = high_tn(mean_ref[...], logit)
        back_rows = high_nt(logit, route_ref[...]) / count_ref[:, :1]

        def finish(index):
            rows = rows_at(index, line)
            value = grouped(total[rows, :], batch) + back_rows[None] * grouped(
                jnp.broadcast_to(mask_ref[rows, :1], (line, C2)), batch
            )
            low = flat(value).astype(BF16)
            hidden_grad_ref[rows, :C2] = low
            hidden_grad_ref[rows, C2:] = low

        loop(MAP, finish)


def project_back(
    hidden_ref, gates_ref, each_ref, own_ref, far_ref, conv_ref, scale_ref, mask_ref,
    full_scale_ref, units_ref, mean_ref, excite_ref,
    grad_ref, own_grad_ref, far_grad_ref, gate_sum_ref, unit_grad_ref, small_ref,
    spread, scaled, sums,
):
    batch, tile = scale_ref.shape
    line = MAP * batch
    step = pl.program_id(0)
    half = own_ref.shape[1]

    @pl.when(step == 0)
    def _():
        gate_sum_ref[...] = jnp.zeros_like(gate_sum_ref)

        def widen(index):
            rows = rows_at(index, line)
            value = grouped(hidden_ref[rows, :].astype(F32), batch)
            for pair in range(HALF):
                lanes = slice(pair * 2 * C2, (pair + 1) * 2 * C2)
                spread[rows, lanes] = flat(value * gates_ref[pair][None]).astype(BF16)
                each = grouped(each_ref[rows, lanes].astype(F32), batch)
                gate_sum_ref[pair] += jnp.sum(each * value, axis=0)

        loop(MAP, widen)

    def pull(index):
        rows = rows_at(index, 2 * line)
        grad_ref[rows, :] = nt(spread[rows, :half], own_ref[...]) + nt(
            spread[rows, half:], far_ref[...]
        )

    loop(MAP // 2, pull)
    place = pl.ds(pl.multiple_of(step * tile, tile), tile)
    sums[:, place] = jnp.zeros((batch, tile), F32)

    def activate(index):
        rows = rows_at(index, line)
        for part in range(tile // LANES):
            lanes = slice(part * LANES, (part + 1) * LANES)
            here = conv_ref[rows, lanes]
            kept = here * sig(here) * mask_ref[rows, :]
            scaled[rows, lanes] = flat(grouped(kept, batch) * scale_ref[:, lanes][None]).astype(BF16)
            added = jnp.sum(grouped(grad_ref[rows, lanes] * kept, batch), axis=0)
            sums[:, pl.ds(pl.multiple_of(step * tile + part * LANES, LANES), LANES)] += added

    loop(MAP, activate)
    turned = scaled[...].T
    far_grad_ref[...] = nn(turned, spread[:, half:])
    own_grad_ref[...] = nn(turned, spread[:, :half])

    @pl.when(step == pl.num_programs(0) - 1)
    def _():
        scale = full_scale_ref[...]
        pre = sums[...] * scale * (1.0 - scale)
        units = units_ref[...]
        gate = jax.nn.sigmoid(units)
        unit_grad = high_nn(pre, excite_ref[...]) * slope(units, gate)
        unit_grad_ref[...] = unit_grad
        small_ref[:, :SE] = high_tn(pre, units * gate)
        small_ref[:, SE:] = high_tn(mean_ref[...], unit_grad)


def second_back(
    grad_ref, scale_ref, unit_grad_ref, squeeze_ref, count_ref, mask_ref, conv_ref, mixed_ref,
    taps_ref, wide_ref, own_ref, far_ref, twice_ref, gates_ref, gate_ref, gate_sum_ref,
    route_ref, mean_ref,
    own_grad_ref, far_grad_ref, tap_grad_ref, hidden_grad_ref, route_grad_ref,
    act, inner, slopes, own_all, far_all,
):
    batch, tile = scale_ref.shape
    line = MAP * batch
    step = pl.program_id(0)
    half = own_ref.shape[1]
    place = pl.ds(pl.multiple_of(step * tile, tile), tile)
    own_all[place, :] = own_ref[...]
    far_all[place, :] = far_ref[...]
    pool_grad = high_nt(unit_grad_ref[...], squeeze_ref[...]) / count_ref[:, :1]

    def activate(index):
        rows = rows_at(index, line)
        for part in range(tile // LANES):
            lanes = slice(part * LANES, (part + 1) * LANES)
            mask = mask_ref[rows, :]
            here = mixed_ref[rows, lanes]
            act[rows, lanes] = here * sig(here) * mask
            here = conv_ref[rows, lanes]
            value = grouped(grad_ref[rows, lanes], batch) * scale_ref[:, lanes][None]
            value = flat(value + pool_grad[:, lanes][None])
            inner[rows, lanes] = value * mask * slope(here, sig(here))

    loop(MAP, activate)

    def conv(index):
        lanes = lanes_at(index)

        def store(tap, value):
            tap_grad_ref[tap : tap + 1, lanes] = value

        depthwise_weight(act, inner, lanes, batch, store)

        def emit(row, value):
            act[pl.ds(row, 8), lanes] = value

        depthwise(inner, taps_ref, lanes, batch, True, emit)

    loop(tile // LANES, conv)

    def deactivate(index):
        rows = rows_at(index, line)
        for part in range(tile // LANES):
            lanes = slice(part * LANES, (part + 1) * LANES)
            here = mixed_ref[rows, lanes]
            value = act[rows, lanes] * mask_ref[rows, :] * slope(here, sig(here))
            slopes[rows, pl.ds(pl.multiple_of(step * tile + part * LANES, LANES), LANES)] = (
                value.astype(BF16)
            )

    loop(MAP, deactivate)
    turned = slopes[:, place].T
    far_grad_ref[...] = nn(turned, wide_ref[:, half:])
    own_grad_ref[...] = nn(turned, wide_ref[:, :half])

    @pl.when(step == pl.num_programs(0) - 1)
    def _():
        sums = [jnp.zeros((batch, 2 * C0), F32)] * HALF
        pairs = HALF // 2

        def pull(index, sums):
            rows = rows_at(index, 2 * line)
            value = slopes[rows, :]
            hidden = grouped(twice_ref[rows, :].astype(F32), batch)
            summed = None
            sums = list(sums)
            for pair in range(HALF):
                weights = own_all if pair < pairs else far_all
                lanes = slice((pair % pairs) * 2 * C0, (pair % pairs + 1) * 2 * C0)
                each = grouped(nn(value, weights[:, lanes]), batch)
                sums[pair] = sums[pair] + jnp.sum(each * hidden, axis=0)
                term = each * gates_ref[pair][None]
                summed = term if summed is None else summed + term
            act[rows, : 2 * C0] = flat(summed)
            return tuple(sums)

        sums = lax.fori_loop(0, MAP // 2, pull, tuple(sums))
        gates = gate_ref[...]
        logit = split_sums(sums, C0) + split_sums([gate_sum_ref[k] for k in range(HALF)], C2)
        logit = logit * gates * (1.0 - gates)
        route_grad_ref[...] = high_tn(mean_ref[...], logit)
        back_rows = high_nt(logit, route_ref[...]) / count_ref[:, :1]

        def finish(index):
            rows = rows_at(index, line)
            summed = act[rows, : 2 * C0]
            value = grouped(summed[:, :C0] + summed[:, C0:], batch) + back_rows[None] * grouped(
                jnp.broadcast_to(mask_ref[rows, :1], (line, C0)), batch
            )
            hidden_grad_ref[rows, :] = flat(value).astype(BF16)

        loop(MAP, finish)


def first_back(
    x_ref, left_ref, right_ref, taps_ref, mask_ref, conv_ref, hidden_ref,
    weight_grad_ref, tap_grad_ref,
    act, inner, wide, deep,
):
    tile = act.shape[1]
    batch = x_ref.shape[0] // (MAP * MAP)
    line = MAP * batch

    def expand(index):
        rows = rows_at(index, line)
        value = nt(x_ref[rows, :], left_ref[:, :C0])
        grad = nt(hidden_ref[rows, :], right_ref[:, :C0])
        for part in range(tile // LANES):
            lanes = slice(part * LANES, (part + 1) * LANES)
            mask = mask_ref[rows, :]
            here = value[:, lanes]
            gate = sig(here)
            act[rows, lanes] = here * gate * mask
            wide[rows, lanes] = slope(here, gate) * mask
            here = conv_ref[rows, lanes]
            gate = sig(here)
            deep[rows, lanes] = (here * gate * mask).astype(BF16)
            inner[rows, lanes] = grad[:, lanes] * mask * slope(here, gate)

    loop(MAP, expand)
    weight_grad_ref[:, C0:] = nn(deep[...].T, hidden_ref[...])

    def conv(index):
        lanes = lanes_at(index)

        def store(tap, value):
            tap_grad_ref[tap : tap + 1, lanes] = value

        depthwise_weight(act, inner, lanes, batch, store)

        def emit(row, value):
            act[pl.ds(row, 8), lanes] = value

        depthwise(inner, taps_ref, lanes, batch, True, emit)

    loop(tile // LANES, conv)

    def deactivate(index):
        rows = rows_at(index, line)
        for part in range(tile // LANES):
            lanes = slice(part * LANES, (part + 1) * LANES)
            deep[rows, lanes] = (act[rows, lanes] * wide[rows, lanes]).astype(BF16)

    loop(MAP, deactivate)
    weight_grad_ref[:, :C0] = nn(deep[...].T, x_ref[...])


def adamw_values(master, first, second, average, grad):
    first = BETA_ONE * first + (1.0 - BETA_ONE) * grad
    second = BETA_TWO * second + (1.0 - BETA_TWO) * grad * grad
    ratio = first / (1.0 - BETA_ONE**STEP) / (jnp.sqrt(second / (1.0 - BETA_TWO**STEP)) + EPSILON)
    master = master - RATE * (ratio + DECAY * master)
    average = SMOOTH * average + (1.0 - SMOOTH) * master
    return (first, second, master, average, master.astype(BF16))


def adamw_kernel(widths, factor_ref, *refs):
    pieces = refs[: len(widths)]
    master, first, second, average = refs[len(widths) : len(widths) + 4]
    outs = refs[len(widths) + 4 : len(widths) + 9]
    factor = factor_ref[0]
    if len(widths) == 1:
        grad = pieces[0][...].astype(F32) * factor
    else:
        whole = refs[-1]
        begin = 0
        for piece, width in zip(pieces, widths):
            whole[:, begin : begin + width] = piece[:, :width].astype(F32)
            begin += width
        grad = whole[...] * factor
    values = adamw_values(master[...], first[...], second[...], average[...], grad)
    for out, value in zip(outs, values):
        out[...] = value


def adamw(factor, pieces, widths, master, first, second, average):
    height, width = master.shape
    rows = 72 if height % 72 == 0 else height
    specs = [pl.BlockSpec((rows, piece.shape[1]), lambda i: (i, 0)) for piece in pieces]
    full = pl.BlockSpec((rows, width), lambda i: (i, 0))
    types = (F32, F32, F32, F32, BF16)
    return pl.pallas_call(
        functools.partial(adamw_kernel, tuple(widths)),
        grid=(height // rows,),
        in_specs=[pl.BlockSpec(memory_space=pltpu.SMEM)] + specs + [full] * 4,
        out_specs=[full] * 5,
        out_shape=[jax.ShapeDtypeStruct((height, width), kind) for kind in types],
        scratch_shapes=[pltpu.VMEM((rows, width), F32)] if len(widths) > 1 else [],
        compiler_params=pltpu.CompilerParams(vmem_limit_bytes=VMEM_BYTES),
        name="adamw",
    )(factor, *pieces, master, first, second, average)


def swap(values, axis, distance):
    size = lax.axis_size(axis)
    return lax.ppermute(values, axis, [(i, i ^ distance) for i in range(size)])


def gather(values, axis):
    parts = [values] + [swap(values, axis, k) for k in range(1, lax.axis_size(axis))]
    return jnp.concatenate(parts, axis=0)


def scatter_sum(mine, axis):
    total = mine(0)
    for k in range(1, lax.axis_size(axis)):
        total = total + swap(mine(k).astype(BF16), axis, k).astype(F32)
    return total


def reduce_shard(own, far, rows):
    came = swap(far, "core", 1)
    deep = lax.axis_size("chan")

    def block(k):
        place = slice(k * deep * rows, (k + 1) * deep * rows)
        return own[place] + came[place]

    middle = scatter_sum(block, "xy")
    return scatter_sum(lambda k: middle[k * rows : (k + 1) * rows], "chan")


def total_sum(values):
    for axis in ("core", "xy", "chan"):
        distance = 1
        while distance < lax.axis_size(axis):
            values = values + swap(values, axis, distance)
            distance *= 2
    return values


def own_order(values, rows):
    place = lax.axis_index("xy")
    return [
        lax.dynamic_slice_in_dim(values, (place ^ k) * rows, rows, 0)
        for k in range(lax.axis_size("xy"))
    ]


def spread_back(shard):
    low = shard.astype(BF16)
    place = lax.axis_index("xy")
    size = lax.axis_size("xy")
    stack = gather(low, "xy").reshape(size, *low.shape)
    mine = jnp.concatenate(
        [lax.dynamic_index_in_dim(stack, place ^ k, 0, keepdims=False) for k in range(size)], 0
    )
    return mine, swap(mine, "core", 1)


def two_parts(values):
    upper = lax.reduce_precision(values, 8, 7)
    return [upper.astype(BF16), (values - upper).astype(BF16)]


def call(kernel, grid, ins, outs, scratch, name):
    def spec(shape, block, index):
        if block is None:
            return pl.BlockSpec(memory_space=pltpu.VMEM)
        return pl.BlockSpec(block, index)

    in_specs = []
    arrays = []
    for entry in ins:
        array, block, index, *mode = entry
        arrays.append(array)
        if mode:
            in_specs.append(pl.BlockSpec(block, index, pipeline_mode=mode[0]))
        else:
            in_specs.append(spec(array.shape, block, index))
    return pl.pallas_call(
        kernel,
        grid=grid,
        in_specs=in_specs,
        out_specs=[spec(shape, block, index) for shape, kind, block, index in outs],
        out_shape=[jax.ShapeDtypeStruct(shape, kind) for shape, kind, block, index in outs],
        scratch_shapes=scratch,
        compiler_params=pltpu.CompilerParams(
            vmem_limit_bytes=VMEM_BYTES, dimension_semantics=("arbitrary",) * len(grid)
        ),
        name=name,
    )(*arrays)


def on_device(
    images,
    labels,
    resolution,
    class_weight,
    column_master,
    column_first,
    column_second,
    column_average,
    row_master,
    row_first,
    row_second,
    row_average,
    head_master,
    head_first,
    head_second,
    head_average,
    route_master,
    route_first,
    route_second,
    route_average,
):
    chans, places = lax.axis_size("chan"), lax.axis_size("xy")
    core, place, layer = lax.axis_index("core"), lax.axis_index("xy"), lax.axis_index("chan")
    first_core = core == 0
    batch = images.shape[0] // chans
    slots = MAP * MAP
    rows = slots * batch
    wide = column_master.shape[1] * chans
    height = column_master.shape[1] // places
    begin = C0 + 2 * TAPS + SE
    tile = 3 * LANES
    tiles = wide // tile

    def fixed(array):
        return (array, None, None)

    def whole(array, grid=1):
        zeros = (0,) * array.ndim
        return (array, array.shape, lambda *ids: zeros, pl.Buffered(1))

    column, row = column_master.T, row_master
    column_parts = [column[:, :C0]]
    column_parts += two_parts(column[:, C0 : C0 + 2 * TAPS])
    small_left = jnp.concatenate([part.astype(BF16) for part in column_parts], 1)
    small_left = jnp.pad(small_left, ((0, 0), (0, 2 * C0 - small_left.shape[1])))
    small_right = jnp.concatenate(
        [row[:, :C0].astype(BF16)]
        + two_parts(column[:, C0 + 2 * TAPS : begin])
        + two_parts(row[:, C0 : C0 + SE]),
        1,
    )
    small = jnp.concatenate(own_order(jnp.where(first_core, small_left, small_right), height), 0)
    small = gather(small, "chan").reshape(chans, places, height, 2 * C0)
    small = small.transpose(1, 0, 2, 3).reshape(wide, 2 * C0)
    small_far = swap(small, "core", 1)
    left = jnp.where(first_core, small, small_far)
    right = jnp.where(first_core, small_far, small)

    expand_own = lax.dynamic_slice(
        column, (place * height, begin + core * HALF * C0), (height, HALF * C0)
    ).astype(BF16)
    expand_own = gather(gather(expand_own, "chan"), "xy")
    expand_far = swap(expand_own, "core", 1)
    project_own = lax.dynamic_slice(
        row, (place * height, C0 + SE + core * HALF * C2), (height, HALF * C2)
    ).astype(BF16)
    project_own = gather(gather(project_own, "chan"), "xy")
    project_far = swap(project_own, "core", 1)
    head_own = gather(gather(head_master.T.astype(BF16), "chan"), "xy")
    head_far = swap(head_own, "core", 1)

    def both(values, at, width):
        upper = values[:, at : at + width].astype(F32)
        return upper + values[:, at + width : at + 2 * width].astype(F32)

    def tap_rows(values):
        return jnp.broadcast_to(values.T[:, None, :], (TAPS, 8, wide))

    taps = both(left, C0, 2 * TAPS)
    first_taps, second_taps = tap_rows(taps[:, :TAPS]), tap_rows(taps[:, TAPS:])
    excite_out = both(right, C0, SE)
    excite_in = both(right, C0 + 2 * SE, SE)
    route_in, route_out = route_master[:C0], route_master[C0:]
    route_in = jnp.where(first_core, route_in, jnp.roll(route_in, HALF, axis=1))

    mine = lax.all_to_all(images, "chan", 0, 0, tiled=True)
    mine = mine.reshape(chans, batch, slots // chans, C0).transpose(0, 2, 1, 3)
    label = lax.dynamic_slice_in_dim(labels, layer * batch, batch, 0)
    side = lax.dynamic_slice_in_dim(resolution, layer * batch, batch, 0)
    spots = jnp.arange(slots, dtype=jnp.int32)
    inside = ((spots // MAP)[:, None] < side[None, :]) & ((spots % MAP)[:, None] < side[None, :])
    inside = inside.reshape(rows, 1)
    x = jnp.where(inside, mine.reshape(rows, C0), 0)
    mask = jnp.broadcast_to(inside.astype(F32), (rows, LANES))
    count = jnp.broadcast_to((side * side).astype(F32)[:, None], (batch, LANES))

    def tiled(array):
        return (array, (tile, array.shape[1]), lambda i: (i, 0))

    def across(array):
        return (array, (array.shape[0], tile), lambda i: (0, i))

    def tap_tile(array):
        return (array, (TAPS, 8, tile), lambda i: (0, 0, i))

    def out_full(shape, kind):
        zeros = (0,) * len(shape)
        return (shape, kind, shape, lambda *ids: zeros)

    def out_across(height_, kind):
        return ((height_, wide), kind, (height_, tile), lambda i: (0, i))

    def out_tiled(width, kind):
        return ((wide, width), kind, (tile, width), lambda i: (i, 0))

    conv_one, mixed_in, twice_one, mean_one, gate_one, gates_one, gates_mid = call(
        first_forward,
        (tiles,),
        [
            whole(x), tiled(left), tiled(right), tap_tile(first_taps), whole(mask), whole(count),
            whole(route_in),
        ],
        [
            out_across(rows, F32),
            out_full((rows, NE * C0), BF16),
            out_full((rows, 2 * C0), BF16),
            out_full((batch, C0), F32),
            out_full((batch, NE), F32),
            out_full((HALF, batch, 2 * C0), F32),
            out_full((HALF, batch, 2 * C2), F32),
        ],
        [
            pltpu.VMEM((rows, tile), F32), pltpu.VMEM((rows, tile), BF16),
            pltpu.VMEM((rows, C0), F32),
        ],
        "first_forward",
    )

    mixed_two, conv_two, mean_two, units, scale = call(
        second_forward,
        (tiles,),
        [
            whole(mixed_in), tiled(expand_own), tiled(expand_far), tap_tile(second_taps),
            whole(mask), whole(count), tiled(excite_in), whole(excite_out),
        ],
        [
            out_across(rows, F32),
            out_across(rows, F32),
            out_across(batch, F32),
            out_full((batch, SE), F32),
            out_full((batch, wide), F32),
        ],
        [pltpu.VMEM((rows, tile), F32)],
        "second_forward",
    )

    each, twice_two, mixed_head, mean_three, gate_two, gates_two = call(
        project,
        (),
        [
            fixed(conv_two), fixed(scale), fixed(project_own), fixed(project_far), fixed(mask),
            fixed(count), fixed(gates_mid), fixed(route_out),
        ],
        [
            ((rows, NE * C2), BF16, None, None),
            ((rows, 2 * C2), BF16, None, None),
            ((rows, NE * C2), BF16, None, None),
            ((batch, C2), F32, None, None),
            ((batch, NE), F32, None, None),
            ((HALF, batch, 2 * C2), F32, None, None),
        ],
        [pltpu.VMEM((rows, wide), BF16)],
        "project",
    )

    half = head_own.shape[0]
    blocks = 5
    part = NE * C2 // blocks
    expert_grad, class_grad, losses, hidden_two, route_grad_out = call(
        head,
        (2 * blocks,),
        [
            whole(mixed_head), whole(twice_two), whole(head_own), whole(head_far), whole(mask),
            whole(count), whole(label[:, None]), whole(class_weight[None, :]), whole(gates_two),
            whole(gate_two), whole(mean_three), whole(route_out),
        ],
        [
            (
                (2, half, NE * C2), F32, (1, half, part),
                lambda i: (1 - i // blocks, 0, i % blocks),
            ),
            out_full((2, half, CLASSES), F32),
            out_full((batch, 2), F32),
            out_full((rows, 2 * C2), BF16),
            out_full((C2, NE), F32),
        ],
        [
            pltpu.VMEM((rows, 2 * half), F32), pltpu.VMEM((rows, 2 * half), BF16),
            pltpu.VMEM((2 * half, rows), BF16), pltpu.VMEM((batch, 2 * half), F32),
            pltpu.VMEM((rows, C2), F32),
        ],
        "head",
    )
    rows_head = head_master.shape[1]
    expert_shard = reduce_shard(expert_grad[0], expert_grad[1], rows_head)
    class_shard = reduce_shard(class_grad[0], class_grad[1], rows_head)

    deep_grad, project_grad_own, project_grad_far, gate_sums, unit_grad, excite_grad = call(
        project_back,
        (tiles,),
        [
            whole(hidden_two), whole(gates_mid), whole(each), tiled(project_own),
            tiled(project_far), across(conv_two), across(scale), whole(mask), whole(scale),
            whole(units), whole(mean_two), whole(excite_out),
        ],
        [
            out_across(rows, F32),
            out_tiled(HALF * C2, F32),
            out_tiled(HALF * C2, F32),
            out_full((HALF, batch, 2 * C2), F32),
            out_full((batch, SE), F32),
            out_full((wide, 2 * SE), F32),
        ],
        [
            pltpu.VMEM((rows, NE * C2), BF16), pltpu.VMEM((rows, tile), BF16),
            pltpu.VMEM((batch, wide), F32),
        ],
        "project_back",
    )
    project_shard = reduce_shard(project_grad_own, project_grad_far, height)

    expand_grad_own, expand_grad_far, tap_grad_two, hidden_one, route_grad_in = call(
        second_back,
        (tiles,),
        [
            across(deep_grad), across(scale), whole(unit_grad), tiled(excite_in), whole(count),
            whole(mask), across(conv_two), across(mixed_two), tap_tile(second_taps),
            whole(mixed_in), tiled(expand_own), tiled(expand_far), whole(twice_one),
            whole(gates_one), whole(gate_one), whole(gate_sums), whole(route_in), whole(mean_one),
        ],
        [
            out_tiled(HALF * C0, F32),
            out_tiled(HALF * C0, F32),
            out_across(TAPS, F32),
            out_full((rows, C0), BF16),
            out_full((C0, NE), F32),
        ],
        [
            pltpu.VMEM((rows, tile), F32), pltpu.VMEM((rows, tile), F32),
            pltpu.VMEM((rows, wide), BF16), pltpu.VMEM((wide, HALF * C0), BF16),
            pltpu.VMEM((wide, HALF * C0), BF16),
        ],
        "second_back",
    )
    expand_shard = reduce_shard(expand_grad_own, expand_grad_far, height)

    weight_grad, tap_grad_one = call(
        first_back,
        (tiles,),
        [
            whole(x), tiled(left), tiled(right), tap_tile(first_taps), whole(mask),
            across(conv_one), whole(hidden_one),
        ],
        [out_tiled(2 * C0, F32), out_across(TAPS, F32)],
        [
            pltpu.VMEM((rows, tile), F32), pltpu.VMEM((rows, tile), F32),
            pltpu.VMEM((rows, tile), F32), pltpu.VMEM((rows, tile), BF16),
        ],
        "first_back",
    )
    small_width = C0 + 2 * SE
    tap_grads = jnp.concatenate([tap_grad_one, tap_grad_two], 0).T
    left_grad = jnp.concatenate([weight_grad[:, :C0], tap_grads], 1)
    left_grad = jnp.pad(left_grad, ((0, 0), (0, small_width - left_grad.shape[1])))
    right_grad = jnp.concatenate([weight_grad[:, C0:], excite_grad], 1)
    small_shard = reduce_shard(
        jnp.where(first_core, left_grad, right_grad),
        jnp.where(first_core, right_grad, left_grad),
        height,
    )

    shards = (expert_shard, class_shard, project_shard, expand_shard, small_shard)
    squares = sum(jnp.sum(shard * shard) for shard in shards)
    route_grad_in = jnp.where(first_core, route_grad_in, jnp.roll(route_grad_in, HALF, axis=1))
    route_grad = jnp.concatenate([route_grad_in, route_grad_out], 0)
    scalars = jnp.concatenate([squares[None], jnp.sum(losses, 0)])
    packed = jnp.concatenate([route_grad.reshape(-1, LANES), jnp.pad(scalars, (0, LANES - 3))[None]])
    packed = total_sum(packed)
    route_sum = packed[:-1].reshape(route_grad.shape)
    square_sum, loss_total, weight_total = packed[-1, 0], packed[-1, 1], packed[-1, 2]
    clip_norm = jnp.sqrt(square_sum + jnp.sum(route_sum * route_sum)) / weight_total
    factor = jnp.minimum(1.0, CLIP / (clip_norm + 1e-06)) / weight_total
    scalar = factor[None]

    project_mine, project_other = spread_back(project_shard)
    expand_mine, expand_other = spread_back(expand_shard)
    small_mine, small_other = spread_back(small_shard)

    def ordered(mine_, other):
        return jnp.where(first_core, mine_, other), jnp.where(first_core, other, mine_)

    project_low, project_up = ordered(project_mine, project_other)
    expand_low, expand_up = ordered(expand_mine, expand_other)
    small_low, small_up = ordered(small_mine, small_other)
    squeeze_grad = small_up[:, C0 + SE :]
    column_out = adamw(
        scalar,
        [small_low, small_up[:, C0 : C0 + SE], expand_low, expand_up],
        [C0 + 2 * TAPS, SE, HALF * C0, HALF * C0],
        column,
        column_first.T,
        column_second.T,
        column_average.T,
    )
    row_out = adamw(
        scalar,
        [small_up, squeeze_grad, project_low, project_up],
        [C0, SE, HALF * C2, HALF * C2],
        row_master,
        row_first,
        row_second,
        row_average,
    )
    head_out = adamw(
        scalar,
        [expert_shard, class_shard],
        [NE * C2, CLASSES],
        head_master.T,
        head_first.T,
        head_second.T,
        head_average.T,
    )
    route_out_new = adamw_values(
        route_master, route_first, route_second, route_average, route_sum * factor
    )
    return (
        *[value.T for value in column_out],
        *row_out,
        *[value.T for value in head_out],
        *route_out_new,
        loss_total,
        weight_total,
        clip_norm,
    )


def solution(mesh):
    groups = mesh.devices.shape[0] // 2
    fine = Mesh(
        mesh.devices.reshape(groups, 2, mesh.devices.shape[1]), ("xy", "core", "chan")
    )
    dp = ("xy", "core")
    every = ("xy", "core", "chan")
    column, row, head_spec = P(None, "chan"), P("chan", None), P(None, every)
    return jax.shard_map(
        on_device,
        mesh=fine,
        in_specs=(P(dp, "chan", None), P(dp), P(dp), P())
        + (column,) * 4
        + (row,) * 4
        + (head_spec,) * 4
        + (P(),) * 4,
        out_specs=(column,) * 5 + (row,) * 5 + (head_spec,) * 5 + (P(),) * 8,
        check_vma=False,
    )
```

```python
import functools
import math

import jax
import jax.numpy as jnp
from jax import lax
from jax.experimental import pallas as pl
from jax.experimental.pallas import tpu as pltpu
from jax.sharding import Mesh
from jax.sharding import PartitionSpec as P

C0 = 192
C2 = 320
SE = 48
CLASSES = 1000
NE = 8
HALF = NE // 2
KERNEL = 5
TAPS = KERNEL * KERNEL
MAP = 8
STEP = 10
LANES = 128

HIGH = lax.Precision.HIGHEST
BETA_ONE = 0.9
BETA_TWO = 0.999
EPSILON = 1e-08
DECAY = 0.05
RATE = 0.05
CLIP = 0.02
SMOOTH = 0.9

F32 = jnp.float32
BF16 = jnp.bfloat16
FLOPS_A_MICRO = 1.1e9
VMEM_BYTES = 60 * 1024 * 1024


def nn(left, right):
    return jnp.dot(left, right, preferred_element_type=F32)


def nt(left, right):
    return lax.dot_general(left, right, (((1,), (1,)), ((), ())), preferred_element_type=F32)


def high_nn(left, right):
    return jnp.dot(left, right, precision=HIGH, preferred_element_type=F32)


def high_nt(left, right):
    return lax.dot_general(
        left, right, (((1,), (1,)), ((), ())), precision=HIGH, preferred_element_type=F32
    )


def high_tn(left, right):
    return lax.dot_general(
        left, right, (((0,), (0,)), ((), ())), precision=HIGH, preferred_element_type=F32
    )


def sig(values):
    return 0.5 * jnp.tanh(0.5 * values) + 0.5


def slope(values, gate):
    return gate * (1.0 + values * (1.0 - gate))


def loop(count, body):
    def step(index, carry):
        body(index)
        return carry

    lax.fori_loop(0, count, step, 0)


def rows_at(index, count):
    return pl.ds(pl.multiple_of(index * count, count), count)


def lanes_at(index):
    return pl.ds(pl.multiple_of(index * LANES, LANES), LANES)


def depthwise(source, taps, lanes, batch, flip, emit):
    parts = batch // 8
    weights = [taps[TAPS - 1 - t if flip else t, :, lanes] for t in range(TAPS)]
    for down in range(MAP):
        total = {}
        for step_y in range(-2, 3):
            line = down + step_y
            if not 0 <= line < MAP:
                continue
            for spot in range(MAP):
                for part in range(parts):
                    value = source[pl.ds((line * MAP + spot) * batch + 8 * part, 8), lanes]
                    for step_x in range(-2, 3):
                        place = spot - step_x
                        if not 0 <= place < MAP:
                            continue
                        term = value * weights[(step_y + 2) * KERNEL + step_x + 2]
                        key = (place, part)
                        total[key] = total[key] + term if key in total else term
        for (place, part), value in total.items():
            emit((down * MAP + place) * batch + 8 * part, value)


def depthwise_weight(source, grad, lanes, batch, store):
    parts = batch // 8
    total = {}
    for down in range(MAP):
        slopes = {
            (spot, part): grad[pl.ds((down * MAP + spot) * batch + 8 * part, 8), lanes]
            for spot in range(MAP)
            for part in range(parts)
        }
        for step_y in range(-2, 3):
            line = down + step_y
            if not 0 <= line < MAP:
                continue
            for spot in range(MAP):
                for part in range(parts):
                    value = source[pl.ds((line * MAP + spot) * batch + 8 * part, 8), lanes]
                    for step_x in range(-2, 3):
                        place = spot - step_x
                        if not 0 <= place < MAP:
                            continue
                        tap = (step_y + 2) * KERNEL + step_x + 2
                        term = value * slopes[(place, part)]
                        total[tap] = total[tap] + term if tap in total else term
    for tap in range(TAPS):
        store(tap, jnp.sum(total[tap], axis=0, keepdims=True))


def pair_gates(gates, width):
    batch = gates.shape[0]
    spots = lax.broadcasted_iota(jnp.int32, (batch, 2 * width), 1)
    out = []
    for pair in range(HALF):
        left = jnp.broadcast_to(gates[:, 2 * pair : 2 * pair + 1], (batch, 2 * width))
        right = jnp.broadcast_to(gates[:, 2 * pair + 1 : 2 * pair + 2], (batch, 2 * width))
        out.append(jnp.where(spots < width, left, right))
    return out


def split_sums(values, width):
    columns = []
    for value in values:
        spots = lax.broadcasted_iota(jnp.int32, value.shape, 1)
        columns.append(jnp.sum(jnp.where(spots < width, value, 0.0), axis=1, keepdims=True))
        columns.append(jnp.sum(jnp.where(spots < width, 0.0, value), axis=1, keepdims=True))
    return jnp.concatenate(columns, axis=1)


def grouped(values, batch):
    return values.reshape(values.shape[0] // batch, batch, values.shape[1])


def flat(values):
    return values.reshape(values.shape[0] * values.shape[1], values.shape[2])


def first_forward(
    x_ref, left_ref, right_ref, taps_ref, mask_ref, count_ref, route_ref,
    conv_ref, wide_ref, twice_ref, mean_ref, gate_ref, small_gates_ref, large_gates_ref,
    act, deep, total,
):
    batch, tile = count_ref.shape[0], act.shape[1]
    line = MAP * batch
    step = pl.program_id(0)

    def expand(index):
        rows = rows_at(index, line)
        value = nt(x_ref[rows, :], left_ref[:, :C0])
        for part in range(tile // LANES):
            here = value[:, part * LANES : (part + 1) * LANES]
            act[rows, part * LANES : (part + 1) * LANES] = here * sig(here) * mask_ref[rows, :]

    loop(MAP, expand)

    def conv(index):
        lanes = lanes_at(index)

        def emit(row, value):
            conv_ref[pl.ds(row, 8), lanes] = value

        depthwise(act, taps_ref, lanes, batch, False, emit)

    loop(tile // LANES, conv)

    def activate(index):
        rows = rows_at(index, line)
        for part in range(tile // LANES):
            lanes = slice(part * LANES, (part + 1) * LANES)
            here = conv_ref[rows, lanes]
            deep[rows, lanes] = (here * sig(here) * mask_ref[rows, :]).astype(BF16)

    loop(MAP, activate)
    part_sum = nn(deep[...], right_ref[:, :C0])

    @pl.when(step == 0)
    def _():
        total[...] = part_sum

    @pl.when(step > 0)
    def _():
        total[...] += part_sum

    @pl.when(step == pl.num_programs(0) - 1)
    def _():
        mean_ref[...] = jnp.zeros_like(mean_ref)

        def finish(index):
            rows = rows_at(index, line)
            value = x_ref[rows, :].astype(F32) + total[rows, :]
            low = value.astype(BF16)
            twice_ref[rows, :C0] = low
            twice_ref[rows, C0:] = low
            for part in range(2):
                lanes = slice(0, LANES) if part == 0 else slice(LANES, C0)
                kept = value[:, lanes] * mask_ref[rows, : lanes.stop - lanes.start]
                mean_ref[:, lanes] += jnp.sum(grouped(kept, batch), axis=0)

        loop(MAP, finish)
        mean_ref[...] = mean_ref[...] / count_ref[:, :1]
        gates = jax.nn.sigmoid(high_nn(mean_ref[...], route_ref[...]))
        gate_ref[...] = gates
        for pair, value in enumerate(pair_gates(gates, C0)):
            small_gates_ref[pair] = value
        for pair, value in enumerate(pair_gates(gates, C2)):
            large_gates_ref[pair] = value

        def widen(index):
            rows = rows_at(index, line)
            value = grouped(twice_ref[rows, :].astype(F32), batch)
            for pair in range(HALF):
                lanes = slice(pair * 2 * C0, (pair + 1) * 2 * C0)
                wide_ref[rows, lanes] = flat(value * small_gates_ref[pair][None]).astype(BF16)

        loop(MAP, widen)


def second_forward(
    wide_ref, own_ref, far_ref, taps_ref, mask_ref, count_ref, squeeze_ref, excite_ref,
    mixed_ref, conv_ref, mean_ref, units_ref, scale_ref,
    act,
):
    batch, tile = count_ref.shape[0], act.shape[1]
    line = MAP * batch
    step = pl.program_id(0)
    half = own_ref.shape[1]

    def expand(index):
        rows = rows_at(index, 2 * line)
        mixed_ref[rows, :] = nt(wide_ref[rows, :half], own_ref[...]) + nt(
            wide_ref[rows, half:], far_ref[...]
        )

    loop(MAP // 2, expand)

    def activate(index):
        rows = rows_at(index, line)
        for part in range(tile // LANES):
            lanes = slice(part * LANES, (part + 1) * LANES)
            here = mixed_ref[rows, lanes]
            act[rows, lanes] = here * sig(here) * mask_ref[rows, :]

    loop(MAP, activate)

    def conv(index):
        lanes = lanes_at(index)

        def emit(row, value):
            conv_ref[pl.ds(row, 8), lanes] = value

        depthwise(act, taps_ref, lanes, batch, False, emit)

    loop(tile // LANES, conv)
    mean_ref[...] = jnp.zeros_like(mean_ref)

    def pool(index):
        rows = rows_at(index, line)
        for part in range(tile // LANES):
            lanes = slice(part * LANES, (part + 1) * LANES)
            here = conv_ref[rows, lanes]
            kept = here * sig(here) * mask_ref[rows, :]
            mean_ref[:, lanes] += jnp.sum(grouped(kept, batch), axis=0)

    loop(MAP, pool)
    mean_ref[...] = mean_ref[...] / count_ref[:, :1]
    units = high_nn(mean_ref[...], squeeze_ref[...])

    @pl.when(step == 0)
    def _():
        units_ref[...] = units

    @pl.when(step > 0)
    def _():
        units_ref[...] += units

    @pl.when(step == pl.num_programs(0) - 1)
    def _():
        value = units_ref[...]
        scale_ref[...] = jax.nn.sigmoid(high_nt(value * jax.nn.sigmoid(value), excite_ref[...]))


def project(
    conv_ref, scale_ref, own_ref, far_ref, mask_ref, count_ref, gates_ref, route_ref,
    each_ref, twice_ref, wide_ref, mean_ref, gate_ref, head_gates_ref,
    scaled,
):
    batch = count_ref.shape[0]
    line = MAP * batch
    width = scaled.shape[1]

    def activate(index):
        rows = rows_at(index, line)
        for part in range(width // LANES):
            lanes = slice(part * LANES, (part + 1) * LANES)
            here = conv_ref[rows, lanes]
            kept = grouped(here * sig(here) * mask_ref[rows, :], batch)
            scaled[rows, lanes] = flat(kept * scale_ref[:, lanes][None]).astype(BF16)

    loop(MAP, activate)
    mean_ref[...] = jnp.zeros_like(mean_ref)
    pairs = HALF // 2

    def mix(index):
        rows = rows_at(index, 2 * line)
        value = scaled[rows, :]
        total = None
        for pair in range(HALF):
            weights = own_ref if pair < pairs else far_ref
            inner = slice((pair % pairs) * 2 * C2, (pair % pairs + 1) * 2 * C2)
            each = nn(value, weights[:, inner])
            each_ref[rows, pair * 2 * C2 : (pair + 1) * 2 * C2] = each.astype(BF16)
            term = grouped(each, batch) * gates_ref[pair][None]
            total = term if total is None else total + term
        total = flat(total)
        value = total[:, :C2] + total[:, C2:]
        low = value.astype(BF16)
        twice_ref[rows, :C2] = low
        twice_ref[rows, C2:] = low
        kept = grouped(value * mask_ref[rows, :1], batch)
        mean_ref[...] += jnp.sum(kept, axis=0)

    loop(MAP // 2, mix)
    mean_ref[...] = mean_ref[...] / count_ref[:, :1]
    gates = jax.nn.sigmoid(high_nn(mean_ref[...], route_ref[...]))
    gate_ref[...] = gates
    for pair, value in enumerate(pair_gates(gates, C2)):
        head_gates_ref[pair] = value

    def widen(index):
        rows = rows_at(index, line)
        value = grouped(twice_ref[rows, :].astype(F32), batch)
        for pair in range(HALF):
            lanes = slice(pair * 2 * C2, (pair + 1) * 2 * C2)
            wide_ref[rows, lanes] = flat(value * head_gates_ref[pair][None]).astype(BF16)

    loop(MAP, widen)


def head(
    wide_ref, twice_ref, own_ref, far_ref, mask_ref, count_ref, label_ref, class_ref,
    gates_ref, gate_ref, mean_ref, route_ref,
    own_grad_ref, far_grad_ref, loss_ref, hidden_grad_ref, route_grad_ref,
    mixed, slopes, turned, pooled, total, means, logit_slopes,
):
    batch = count_ref.shape[0]
    line = MAP * batch
    step = pl.program_id(0)
    half = own_ref.shape[0]
    experts = NE * C2
    columns = own_grad_ref.shape[1]
    sides = (own_ref, far_ref)

    @pl.when(step == 0)
    def _():
        pooled[...] = jnp.zeros_like(pooled)
        for side, weights in enumerate(sides):

            def expand(index, side=side, weights=weights):
                rows = rows_at(index, 2 * line)
                mixed[rows, side * half : (side + 1) * half] = nt(
                    wide_ref[rows, :], weights[:, :experts]
                )

            loop(MAP // 2, expand)

        def pool(index):
            rows = rows_at(index, line)
            for part in range(2 * half // LANES):
                lanes = slice(part * LANES, (part + 1) * LANES)
                here = mixed[rows, lanes]
                kept = here * sig(here) * mask_ref[rows, :]
                pooled[:, lanes] += jnp.sum(grouped(kept, batch), axis=0)

        loop(MAP, pool)
        mean = (pooled[...] / count_ref[:, :1]).astype(BF16)
        logits = nn(mean[:, :half], own_ref[:, experts : experts + CLASSES]) + nn(mean[:, half:], far_ref[:, experts : experts + CLASSES])
        spots = lax.broadcasted_iota(jnp.int32, logits.shape, 1)
        onehot = (spots == label_ref[...]).astype(F32)
        weight = jnp.sum(onehot * class_ref[...], axis=1, keepdims=True)
        top = jnp.max(logits, axis=1, keepdims=True)
        powers = jnp.exp(logits - top)
        summed = jnp.sum(powers, axis=1, keepdims=True)
        loss = weight * (top + jnp.log(summed) - jnp.sum(logits * onehot, axis=1, keepdims=True))
        loss_ref[...] = jnp.concatenate([loss, weight], axis=1)
        logit_grad = (weight * (powers / summed - onehot)).astype(BF16)
        means[...] = mean
        logit_slopes[...] = jnp.zeros_like(logit_slopes)
        logit_slopes[:, :CLASSES] = logit_grad
        for side, weights in enumerate(sides):
            place = slice(side * half, (side + 1) * half)
            pooled[:, place] = nt(logit_grad, weights[:, experts : experts + CLASSES]) / count_ref[:, :1]

        def back(index):
            rows = rows_at(index, line)
            for part in range(2 * half // LANES):
                lanes = slice(part * LANES, (part + 1) * LANES)
                here = mixed[rows, lanes]
                value = grouped(mask_ref[rows, :] * slope(here, sig(here)), batch)
                slopes[rows, lanes] = flat(value * pooled[:, lanes][None]).astype(BF16)

        loop(MAP, back)
        for part in range(2 * half // LANES):
            turned[part * LANES : (part + 1) * LANES, :] = slopes[
                :, part * LANES : (part + 1) * LANES
            ].T

    blocks = pl.num_programs(0) // 2
    side = 1 - step // blocks
    block = step % blocks
    place = pl.ds(pl.multiple_of(side * half, half), half)

    def weight_grad(out):
        @pl.when(block < experts // columns)
        def _():
            out[...] = nn(
                turned[place, :],
                wide_ref[:, pl.ds(pl.multiple_of(block * columns, columns), columns)],
            ).astype(out.dtype)

        @pl.when(block >= experts // columns)
        def _():
            begin = pl.multiple_of(block * columns - experts, columns)
            out[...] = lax.dot_general(
                means[:, place], logit_slopes[:, pl.ds(begin, columns)],
                (((0,), (0,)), ((), ())), preferred_element_type=F32,
            ).astype(out.dtype)

    @pl.when(side == 1)
    def _():
        weight_grad(far_grad_ref)

    @pl.when(side == 0)
    def _():
        weight_grad(own_grad_ref)

    @pl.when(step == pl.num_programs(0) - 1)
    def _():
        sums = [jnp.zeros((batch, 2 * C2), F32)] * HALF

        def pull(index, sums):
            rows = rows_at(index, 2 * line)
            left, right = (slopes[rows, :half], slopes[rows, half:])
            hidden = grouped(twice_ref[rows, :].astype(F32), batch)
            summed = None
            sums = list(sums)
            for pair in range(HALF):
                lanes = slice(pair * 2 * C2, (pair + 1) * 2 * C2)
                each = grouped(nn(left, own_ref[:, lanes]) + nn(right, far_ref[:, lanes]), batch)
                sums[pair] = sums[pair] + jnp.sum(each * hidden, axis=0)
                term = each * gates_ref[pair][None]
                summed = term if summed is None else summed + term
            summed = flat(summed)
            total[rows, :] = summed[:, :C2] + summed[:, C2:]
            return tuple(sums)

        sums = lax.fori_loop(0, MAP // 2, pull, tuple(sums))
        gates = gate_ref[...]
        logit = split_sums(sums, C2) * gates * (1.0 - gates)
        route_grad_ref[...] = high_tn(mean_ref[...], logit)
        back_rows = high_nt(logit, route_ref[...]) / count_ref[:, :1]

        def finish(index):
            rows = rows_at(index, line)
            value = grouped(total[rows, :], batch) + back_rows[None] * grouped(
                jnp.broadcast_to(mask_ref[rows, :1], (line, C2)), batch
            )
            low = flat(value).astype(BF16)
            hidden_grad_ref[rows, :C2] = low
            hidden_grad_ref[rows, C2:] = low

        loop(MAP, finish)


def project_back(
    hidden_ref, gates_ref, each_ref, own_ref, far_ref, conv_ref, scale_ref, mask_ref,
    full_scale_ref, units_ref, mean_ref, excite_ref,
    grad_ref, own_grad_ref, far_grad_ref, gate_sum_ref, unit_grad_ref, small_ref,
    spread, scaled, sums,
):
    batch, tile = scale_ref.shape
    line = MAP * batch
    step = pl.program_id(0)
    half = own_ref.shape[1]

    @pl.when(step == 0)
    def _():
        gate_sum_ref[...] = jnp.zeros_like(gate_sum_ref)

        def widen(index):
            rows = rows_at(index, line)
            value = grouped(hidden_ref[rows, :].astype(F32), batch)
            for pair in range(HALF):
                lanes = slice(pair * 2 * C2, (pair + 1) * 2 * C2)
                spread[rows, lanes] = flat(value * gates_ref[pair][None]).astype(BF16)
                each = grouped(each_ref[rows, lanes].astype(F32), batch)
                gate_sum_ref[pair] += jnp.sum(each * value, axis=0)

        loop(MAP, widen)

    def pull(index):
        rows = rows_at(index, 2 * line)
        grad_ref[rows, :] = nt(spread[rows, :half], own_ref[...]) + nt(
            spread[rows, half:], far_ref[...]
        )

    loop(MAP // 2, pull)
    place = pl.ds(pl.multiple_of(step * tile, tile), tile)
    sums[:, place] = jnp.zeros((batch, tile), F32)

    def activate(index):
        rows = rows_at(index, line)
        for part in range(tile // LANES):
            lanes = slice(part * LANES, (part + 1) * LANES)
            here = conv_ref[rows, lanes]
            kept = here * sig(here) * mask_ref[rows, :]
            scaled[rows, lanes] = flat(grouped(kept, batch) * scale_ref[:, lanes][None]).astype(BF16)
            added = jnp.sum(grouped(grad_ref[rows, lanes] * kept, batch), axis=0)
            sums[:, pl.ds(pl.multiple_of(step * tile + part * LANES, LANES), LANES)] += added

    loop(MAP, activate)
    turned = scaled[...].T
    far_grad_ref[...] = nn(turned, spread[:, half:])
    own_grad_ref[...] = nn(turned, spread[:, :half])

    @pl.when(step == pl.num_programs(0) - 1)
    def _():
        scale = full_scale_ref[...]
        pre = sums[...] * scale * (1.0 - scale)
        units = units_ref[...]
        gate = jax.nn.sigmoid(units)
        unit_grad = high_nn(pre, excite_ref[...]) * slope(units, gate)
        unit_grad_ref[...] = unit_grad
        small_ref[:, :SE] = high_tn(pre, units * gate)
        small_ref[:, SE:] = high_tn(mean_ref[...], unit_grad)


def second_back(
    grad_ref, scale_ref, unit_grad_ref, squeeze_ref, count_ref, mask_ref, conv_ref, mixed_ref,
    taps_ref, wide_ref, own_ref, far_ref, twice_ref, gates_ref, gate_ref, gate_sum_ref,
    route_ref, mean_ref,
    own_grad_ref, far_grad_ref, tap_grad_ref, hidden_grad_ref, route_grad_ref,
    act, inner, slopes, own_all, far_all,
):
    batch, tile = scale_ref.shape
    line = MAP * batch
    step = pl.program_id(0)
    half = own_ref.shape[1]
    place = pl.ds(pl.multiple_of(step * tile, tile), tile)
    own_all[place, :] = own_ref[...]
    far_all[place, :] = far_ref[...]
    pool_grad = high_nt(unit_grad_ref[...], squeeze_ref[...]) / count_ref[:, :1]

    def activate(index):
        rows = rows_at(index, line)
        for part in range(tile // LANES):
            lanes = slice(part * LANES, (part + 1) * LANES)
            mask = mask_ref[rows, :]
            here = mixed_ref[rows, lanes]
            act[rows, lanes] = here * sig(here) * mask
            here = conv_ref[rows, lanes]
            value = grouped(grad_ref[rows, lanes], batch) * scale_ref[:, lanes][None]
            value = flat(value + pool_grad[:, lanes][None])
            inner[rows, lanes] = value * mask * slope(here, sig(here))

    loop(MAP, activate)

    def conv(index):
        lanes = lanes_at(index)

        def store(tap, value):
            tap_grad_ref[tap : tap + 1, lanes] = value

        depthwise_weight(act, inner, lanes, batch, store)

        def emit(row, value):
            act[pl.ds(row, 8), lanes] = value

        depthwise(inner, taps_ref, lanes, batch, True, emit)

    loop(tile // LANES, conv)

    def deactivate(index):
        rows = rows_at(index, line)
        for part in range(tile // LANES):
            lanes = slice(part * LANES, (part + 1) * LANES)
            here = mixed_ref[rows, lanes]
            value = act[rows, lanes] * mask_ref[rows, :] * slope(here, sig(here))
            slopes[rows, pl.ds(pl.multiple_of(step * tile + part * LANES, LANES), LANES)] = (
                value.astype(BF16)
            )

    loop(MAP, deactivate)
    turned = slopes[:, place].T
    far_grad_ref[...] = nn(turned, wide_ref[:, half:])
    own_grad_ref[...] = nn(turned, wide_ref[:, :half])

    @pl.when(step == pl.num_programs(0) - 1)
    def _():
        sums = [jnp.zeros((batch, 2 * C0), F32)] * HALF
        pairs = HALF // 2

        def pull(index, sums):
            rows = rows_at(index, 2 * line)
            value = slopes[rows, :]
            hidden = grouped(twice_ref[rows, :].astype(F32), batch)
            summed = None
            sums = list(sums)
            for pair in range(HALF):
                weights = own_all if pair < pairs else far_all
                lanes = slice((pair % pairs) * 2 * C0, (pair % pairs + 1) * 2 * C0)
                each = grouped(nn(value, weights[:, lanes]), batch)
                sums[pair] = sums[pair] + jnp.sum(each * hidden, axis=0)
                term = each * gates_ref[pair][None]
                summed = term if summed is None else summed + term
            act[rows, : 2 * C0] = flat(summed)
            return tuple(sums)

        sums = lax.fori_loop(0, MAP // 2, pull, tuple(sums))
        gates = gate_ref[...]
        logit = split_sums(sums, C0) + split_sums([gate_sum_ref[k] for k in range(HALF)], C2)
        logit = logit * gates * (1.0 - gates)
        route_grad_ref[...] = high_tn(mean_ref[...], logit)
        back_rows = high_nt(logit, route_ref[...]) / count_ref[:, :1]

        def finish(index):
            rows = rows_at(index, line)
            summed = act[rows, : 2 * C0]
            value = grouped(summed[:, :C0] + summed[:, C0:], batch) + back_rows[None] * grouped(
                jnp.broadcast_to(mask_ref[rows, :1], (line, C0)), batch
            )
            hidden_grad_ref[rows, :] = flat(value).astype(BF16)

        loop(MAP, finish)


def first_back(
    x_ref, left_ref, right_ref, taps_ref, mask_ref, conv_ref, hidden_ref,
    weight_grad_ref, tap_grad_ref,
    act, inner, wide, deep,
):
    tile = act.shape[1]
    batch = x_ref.shape[0] // (MAP * MAP)
    line = MAP * batch

    def expand(index):
        rows = rows_at(index, line)
        value = nt(x_ref[rows, :], left_ref[:, :C0])
        grad = nt(hidden_ref[rows, :], right_ref[:, :C0])
        for part in range(tile // LANES):
            lanes = slice(part * LANES, (part + 1) * LANES)
            mask = mask_ref[rows, :]
            here = value[:, lanes]
            gate = sig(here)
            act[rows, lanes] = here * gate * mask
            wide[rows, lanes] = slope(here, gate) * mask
            here = conv_ref[rows, lanes]
            gate = sig(here)
            deep[rows, lanes] = (here * gate * mask).astype(BF16)
            inner[rows, lanes] = grad[:, lanes] * mask * slope(here, gate)

    loop(MAP, expand)
    weight_grad_ref[:, C0:] = nn(deep[...].T, hidden_ref[...])

    def conv(index):
        lanes = lanes_at(index)

        def store(tap, value):
            tap_grad_ref[tap : tap + 1, lanes] = value

        depthwise_weight(act, inner, lanes, batch, store)

        def emit(row, value):
            act[pl.ds(row, 8), lanes] = value

        depthwise(inner, taps_ref, lanes, batch, True, emit)

    loop(tile // LANES, conv)

    def deactivate(index):
        rows = rows_at(index, line)
        for part in range(tile // LANES):
            lanes = slice(part * LANES, (part + 1) * LANES)
            deep[rows, lanes] = (act[rows, lanes] * wide[rows, lanes]).astype(BF16)

    loop(MAP, deactivate)
    weight_grad_ref[:, :C0] = nn(deep[...].T, x_ref[...])


def adamw_values(master, first, second, average, grad):
    first = BETA_ONE * first + (1.0 - BETA_ONE) * grad
    second = BETA_TWO * second + (1.0 - BETA_TWO) * grad * grad
    ratio = first / (1.0 - BETA_ONE**STEP) / (jnp.sqrt(second / (1.0 - BETA_TWO**STEP)) + EPSILON)
    master = master - RATE * (ratio + DECAY * master)
    average = SMOOTH * average + (1.0 - SMOOTH) * master
    return (first, second, master, average, master.astype(BF16))


def adamw_kernel(segments, arrays, place_ref, factor_ref, *refs):
    pieces = refs[: 2 * arrays]
    master, first, second, average = refs[2 * arrays : 2 * arrays + 4]
    outs = refs[2 * arrays + 4 : 2 * arrays + 9]
    whole = refs[-1]

    def fill(core):
        at = 0
        for side, array, begin, width in segments:
            source = pieces[2 * array + (side ^ core)]
            whole[:, at : at + width] = source[:, begin : begin + width].astype(F32)
            at += width

    for core in range(2):

        @pl.when(place_ref[1] == core)
        def _(core=core):
            fill(core)

    grad = whole[...] * factor_ref[0]
    values = adamw_values(master[...], first[...], second[...], average[...], grad)
    for out, value in zip(outs, values):
        out[...] = value


def adamw(factor, spot, rows, pieces, segments, master, first, second, average):
    height, width = master.shape
    specs = [
        pl.BlockSpec((rows, piece.shape[1]), lambda i, place: (i ^ place[0], 0)) for piece in pieces
    ]
    full = pl.BlockSpec((rows, width), lambda i, place: (i, 0))
    types = (F32, F32, F32, F32, BF16)
    return pl.pallas_call(
        functools.partial(adamw_kernel, segments, len(pieces) // 2),
        grid_spec=pltpu.PrefetchScalarGridSpec(
            num_scalar_prefetch=1,
            grid=(height // rows,),
            in_specs=[pl.BlockSpec(memory_space=pltpu.SMEM)] + specs + [full] * 4,
            out_specs=[full] * 5,
            scratch_shapes=[pltpu.VMEM((rows, width), F32)],
        ),
        out_shape=[jax.ShapeDtypeStruct((height, width), kind) for kind in types],
        compiler_params=pltpu.CompilerParams(vmem_limit_bytes=VMEM_BYTES),
        name="adamw",
    )(spot, factor, *pieces, master, first, second, average)


def adamw_head_kernel(factor_ref, grad, master, first, second, average, *outs):
    grad = grad[...] * factor_ref[0]
    values = adamw_values(master[...], first[...], second[...], average[...], grad)
    for out, value in zip(outs, values):
        out[...] = value


def adamw_head(factor, grad, *state):
    height, width = state[0].shape
    part = 4 * LANES
    block = pl.BlockSpec((height, part), lambda i: (0, i))
    types = (F32, F32, F32, F32, BF16)
    return pl.pallas_call(
        adamw_head_kernel,
        grid=(pl.cdiv(width, part),),
        in_specs=[pl.BlockSpec(memory_space=pltpu.SMEM)] + [block] * 5,
        out_specs=[block] * 5,
        out_shape=[jax.ShapeDtypeStruct((height, width), kind) for kind in types],
        compiler_params=pltpu.CompilerParams(vmem_limit_bytes=VMEM_BYTES),
        name="adamw_head",
    )(factor, grad, *state)


def swap(values, axis, distance):
    size = lax.axis_size(axis)
    return lax.ppermute(values, axis, [(i, i ^ distance) for i in range(size)])


def meet(*values):
    return lax.optimization_barrier(values)


def copies(values, axis):
    return [values] + [swap(values, axis, k) for k in range(1, lax.axis_size(axis))]


def joined(parts):
    return jnp.concatenate(parts, axis=0)


def pair_sum(own, came, parts):
    rows = own.shape[0] // parts
    return [own[k * rows : (k + 1) * rows] + came[k * rows : (k + 1) * rows] for k in range(parts)]


def exchange(blocks, axis):
    return [blocks[0]] + [swap(block.astype(BF16), axis, k) for k, block in enumerate(blocks) if k]


def added(parts):
    total = parts[0]
    for value in parts[1:]:
        total = total + value.astype(F32)
    return total


def split(values, parts):
    rows = values.shape[0] // parts
    return [values[k * rows : (k + 1) * rows] for k in range(parts)]


def total_sum(values):
    for axis in ("core", "xy", "chan"):
        distance = 1
        while distance < lax.axis_size(axis):
            values = values + swap(values, axis, distance)
            distance *= 2
    return values


def own_order(values, rows):
    place = lax.axis_index("xy")
    return [
        lax.dynamic_slice_in_dim(values, (place ^ k) * rows, rows, 0)
        for k in range(lax.axis_size("xy"))
    ]


def in_order(parts):
    place = lax.axis_index("xy")
    stack = jnp.stack(parts)
    return joined(
        [lax.dynamic_index_in_dim(stack, place ^ k, 0, keepdims=False) for k in range(len(parts))]
    )


def two_parts(values):
    upper = lax.reduce_precision(values, 8, 7)
    return [upper.astype(BF16), (values - upper).astype(BF16)]


def call(kernel, grid, ins, outs, scratch, name, micros):
    def spec(shape, block, index):
        if block is None:
            return pl.BlockSpec(memory_space=pltpu.VMEM)
        return pl.BlockSpec(block, index)

    in_specs = []
    arrays = []
    for entry in ins:
        array, block, index, *mode = entry
        arrays.append(array)
        if mode:
            in_specs.append(pl.BlockSpec(block, index, pipeline_mode=mode[0]))
        else:
            in_specs.append(spec(array.shape, block, index))
    return pl.pallas_call(
        kernel,
        grid=grid,
        in_specs=in_specs,
        out_specs=[spec(shape, block, index) for shape, kind, block, index in outs],
        out_shape=[jax.ShapeDtypeStruct(shape, kind) for shape, kind, block, index in outs],
        scratch_shapes=scratch,
        compiler_params=pltpu.CompilerParams(
            vmem_limit_bytes=VMEM_BYTES, dimension_semantics=("arbitrary",) * len(grid)
        ),
        cost_estimate=pl.CostEstimate(
            flops=int(micros * FLOPS_A_MICRO), bytes_accessed=1 << 20, transcendentals=0
        ),
        name=name,
    )(*arrays)


def on_device(
    images,
    labels,
    resolution,
    class_weight,
    column_master,
    column_first,
    column_second,
    column_average,
    row_master,
    row_first,
    row_second,
    row_average,
    head_master,
    head_first,
    head_second,
    head_average,
    route_master,
    route_first,
    route_second,
    route_average,
):
    chans, places = lax.axis_size("chan"), lax.axis_size("xy")
    core, place, layer = lax.axis_index("core"), lax.axis_index("xy"), lax.axis_index("chan")
    first_core = core == 0
    batch = images.shape[0] // chans
    slots = MAP * MAP
    rows = slots * batch
    wide = column_master.shape[1] * chans
    height = column_master.shape[1] // places
    begin = C0 + 2 * TAPS + SE
    tile = 3 * LANES
    tiles = wide // tile

    def fixed(array):
        return (array, None, None)

    def whole(array, grid=1):
        zeros = (0,) * array.ndim
        return (array, array.shape, lambda *ids: zeros, pl.Buffered(1))

    column, row = column_master.T, row_master
    column_parts = [column[:, :C0]]
    column_parts += two_parts(column[:, C0 : C0 + 2 * TAPS])
    small_left = jnp.concatenate([part.astype(BF16) for part in column_parts], 1)
    small_left = jnp.pad(small_left, ((0, 0), (0, 2 * C0 - small_left.shape[1])))
    small_right = jnp.concatenate(
        [row[:, :C0].astype(BF16)]
        + two_parts(column[:, C0 + 2 * TAPS : begin])
        + two_parts(row[:, C0 : C0 + SE]),
        1,
    )
    small = joined(own_order(jnp.where(first_core, small_left, small_right), height))
    expand_own = lax.dynamic_slice(
        column, (place * height, begin + core * HALF * C0), (height, HALF * C0)
    ).astype(BF16)
    project_own = lax.dynamic_slice(
        row, (place * height, C0 + SE + core * HALF * C2), (height, HALF * C2)
    ).astype(BF16)
    part = 4 * LANES
    blocks = pl.cdiv(NE * C2 + CLASSES, part)
    lanes = blocks * part
    head_own = jnp.pad(head_master.T.astype(BF16), ((0, 0), (0, lanes - NE * C2 - CLASSES)))
    mine = lax.all_to_all(images, "chan", 0, 0, tiled=True)
    small, expand_own, project_own, head_own, mine = meet(
        copies(small, "chan"), expand_own, project_own, head_own, mine
    )
    small = joined(small).reshape(chans, places, height, 2 * C0)
    small = small.transpose(1, 0, 2, 3).reshape(wide, 2 * C0)
    small_far = swap(small, "core", 1)
    expand_own = copies(expand_own, "chan")
    project_own = joined([project_own, swap(project_own, "chan", 1)])
    head_own = lax.all_gather(head_own, "chan", axis=0, tiled=True)
    expand_own = joined(expand_own)
    left = jnp.where(first_core, small, small_far)
    right = jnp.where(first_core, small_far, small)
    expand_own = copies(expand_own, "xy")
    distance = 2
    project_own = [project_own]
    while distance < chans:
        held = joined(project_own)
        project_own = [held, swap(held, "chan", distance)]
        distance *= 2

    def both(values, at, width):
        upper = values[:, at : at + width].astype(F32)
        return upper + values[:, at + width : at + 2 * width].astype(F32)

    def tap_rows(values):
        return jnp.broadcast_to(values.T[:, None, :], (TAPS, 8, wide))

    taps = both(left, C0, 2 * TAPS)
    first_taps, second_taps = tap_rows(taps[:, :TAPS]), tap_rows(taps[:, TAPS:])
    excite_out = both(right, C0, SE)
    excite_in = both(right, C0 + 2 * SE, SE)
    route_in, route_out = route_master[:C0], route_master[C0:]
    route_in = jnp.where(first_core, route_in, jnp.roll(route_in, HALF, axis=1))

    mine = mine.reshape(chans, batch, slots // chans, C0).transpose(0, 2, 1, 3)
    label = lax.dynamic_slice_in_dim(labels, layer * batch, batch, 0)
    side = lax.dynamic_slice_in_dim(resolution, layer * batch, batch, 0)
    spots = jnp.arange(slots, dtype=jnp.int32)
    inside = ((spots // MAP)[:, None] < side[None, :]) & ((spots % MAP)[:, None] < side[None, :])
    inside = inside.reshape(rows, 1)
    x = jnp.where(inside, mine.reshape(rows, C0), 0)
    mask = jnp.broadcast_to(inside.astype(F32), (rows, LANES))
    count = jnp.broadcast_to((side * side).astype(F32)[:, None], (batch, LANES))

    def tiled(array):
        return (array, (tile, array.shape[1]), lambda i: (i, 0))

    def across(array):
        return (array, (array.shape[0], tile), lambda i: (0, i))

    def tap_tile(array):
        return (array, (TAPS, 8, tile), lambda i: (0, 0, i))

    def out_full(shape, kind):
        zeros = (0,) * len(shape)
        return (shape, kind, shape, lambda *ids: zeros)

    def out_across(height_, kind):
        return ((height_, wide), kind, (height_, tile), lambda i: (0, i))

    def out_tiled(width, kind):
        return ((wide, width), kind, (tile, width), lambda i: (i, 0))

    first_out = call(
        first_forward,
        (tiles,),
        [
            whole(x), tiled(left), tiled(right), tap_tile(first_taps), whole(mask), whole(count),
            whole(route_in),
        ],
        [
            out_across(rows, F32),
            out_full((rows, NE * C0), BF16),
            out_full((rows, 2 * C0), BF16),
            out_full((batch, C0), F32),
            out_full((batch, NE), F32),
            out_full((HALF, batch, 2 * C0), F32),
            out_full((HALF, batch, 2 * C2), F32),
        ],
        [
            pltpu.VMEM((rows, tile), F32), pltpu.VMEM((rows, tile), BF16),
            pltpu.VMEM((rows, C0), F32),
        ],
        "first_forward",
        20,
    )

    (conv_one, mixed_in, twice_one, mean_one, gate_one, gates_one, gates_mid) = first_out
    mixed_in, expand_own, project_own, head_own = meet(mixed_in, expand_own, project_own, head_own)
    expand_own, project_own = joined(expand_own), joined(project_own)
    head_own = lax.all_gather(head_own, "xy", axis=0, tiled=True)
    expand_far = swap(expand_own, "core", 1)
    project_own = copies(project_own, "xy")

    mixed_two, conv_two, mean_two, units, scale = call(
        second_forward,
        (tiles,),
        [
            whole(mixed_in), tiled(expand_own), tiled(expand_far), tap_tile(second_taps),
            whole(mask), whole(count), tiled(excite_in), whole(excite_out),
        ],
        [
            out_across(rows, F32),
            out_across(rows, F32),
            out_across(batch, F32),
            out_full((batch, SE), F32),
            out_full((batch, wide), F32),
        ],
        [pltpu.VMEM((rows, tile), F32)],
        "second_forward",
        22,
    )

    conv_two, project_own = meet(conv_two, project_own)
    project_own = joined(project_own)
    project_far = swap(project_own, "core", 1)

    each, twice_two, mixed_head, mean_three, gate_two, gates_two = call(
        project,
        (),
        [
            fixed(conv_two), fixed(scale), fixed(project_own), fixed(project_far), fixed(mask),
            fixed(count), fixed(gates_mid), fixed(route_out),
        ],
        [
            ((rows, NE * C2), BF16, None, None),
            ((rows, 2 * C2), BF16, None, None),
            ((rows, NE * C2), BF16, None, None),
            ((batch, C2), F32, None, None),
            ((batch, NE), F32, None, None),
            ((HALF, batch, 2 * C2), F32, None, None),
        ],
        [pltpu.VMEM((rows, wide), BF16)],
        "project",
        20,
    )

    mixed_head, head_own = meet(mixed_head, head_own)
    head_far = swap(head_own, "core", 1)
    half = head_own.shape[0]
    head_grad_own, head_grad_far, losses, hidden_two, route_grad_out = call(
        head,
        (2 * blocks,),
        [
            whole(mixed_head), whole(twice_two), whole(head_own), whole(head_far), whole(mask),
            whole(count), whole(label[:, None]), whole(class_weight[None, :]), whole(gates_two),
            whole(gate_two), whole(mean_three), whole(route_out),
        ],
        [
            ((half, lanes), BF16, (half, part), lambda i: (0, jnp.maximum(i - blocks, 0))),
            ((half, lanes), BF16, (half, part), lambda i: (0, jnp.minimum(i, blocks - 1))),
            out_full((batch, 2), F32),
            out_full((rows, 2 * C2), BF16),
            out_full((C2, NE), F32),
        ],
        [
            pltpu.VMEM((rows, 2 * half), F32), pltpu.VMEM((rows, 2 * half), BF16),
            pltpu.VMEM((2 * half, rows), BF16), pltpu.VMEM((batch, 2 * half), F32),
            pltpu.VMEM((rows, C2), F32), pltpu.VMEM((batch, 2 * half), BF16),
            pltpu.VMEM((batch, lanes - NE * C2), BF16),
        ],
        "head",
        45,
    )
    head_came = swap(head_grad_far, "core", 1)

    deep_grad, project_grad_own, project_grad_far, gate_sums, unit_grad, excite_grad = call(
        project_back,
        (tiles,),
        [
            whole(hidden_two), whole(gates_mid), whole(each), tiled(project_own),
            tiled(project_far), across(conv_two), across(scale), whole(mask), whole(scale),
            whole(units), whole(mean_two), whole(excite_out),
        ],
        [
            out_across(rows, F32),
            out_tiled(HALF * C2, F32),
            out_tiled(HALF * C2, F32),
            out_full((HALF, batch, 2 * C2), F32),
            out_full((batch, SE), F32),
            out_full((wide, 2 * SE), F32),
        ],
        [
            pltpu.VMEM((rows, NE * C2), BF16), pltpu.VMEM((rows, tile), BF16),
            pltpu.VMEM((batch, wide), F32),
        ],
        "project_back",
        29,
    )
    deep_grad, head_came = meet(deep_grad, head_came)
    high_rows = half // places
    head_blocks = [
        lax.dynamic_slice_in_dim(head_grad_own, (place ^ k) * high_rows, high_rows, 0).astype(F32)
        + lax.dynamic_slice_in_dim(head_came, (place ^ k) * high_rows, high_rows, 0).astype(F32)
        for k in range(places)
    ]
    head_parts = exchange(head_blocks, "xy")
    project_came = swap(project_grad_far, "core", 1)

    expand_grad_own, expand_grad_far, tap_grad_two, hidden_one, route_grad_in = call(
        second_back,
        (tiles,),
        [
            across(deep_grad), across(scale), whole(unit_grad), tiled(excite_in), whole(count),
            whole(mask), across(conv_two), across(mixed_two), tap_tile(second_taps),
            whole(mixed_in), tiled(expand_own), tiled(expand_far), whole(twice_one),
            whole(gates_one), whole(gate_one), whole(gate_sums), whole(route_in), whole(mean_one),
        ],
        [
            out_tiled(HALF * C0, F32),
            out_tiled(HALF * C0, F32),
            out_across(TAPS, F32),
            out_full((rows, C0), BF16),
            out_full((C0, NE), F32),
        ],
        [
            pltpu.VMEM((rows, tile), F32), pltpu.VMEM((rows, tile), F32),
            pltpu.VMEM((rows, wide), BF16), pltpu.VMEM((wide, HALF * C0), BF16),
            pltpu.VMEM((wide, HALF * C0), BF16),
        ],
        "second_back",
        43,
    )
    hidden_one, project_came, head_parts = meet(hidden_one, project_came, head_parts)
    head_shard = lax.psum_scatter(added(head_parts), "chan", scatter_dimension=0, tiled=True)
    project_parts = exchange(pair_sum(project_grad_own, project_came, places), "xy")
    expand_came = swap(expand_grad_far, "core", 1)

    def first_back_tiles(start, count_, hidden_one):
        def shifted(array):
            return (array, (tile, array.shape[1]), lambda i: (i + start, 0))

        return call(
            first_back,
            (count_,),
            [
                whole(x), shifted(left), shifted(right),
                (first_taps, (TAPS, 8, tile), lambda i: (0, 0, i + start)), whole(mask),
                (conv_one, (rows, tile), lambda i: (0, i + start)), whole(hidden_one),
            ],
            [
                ((count_ * tile, 2 * C0), F32, (tile, 2 * C0), lambda i: (i, 0)),
                ((TAPS, count_ * tile), F32, (TAPS, tile), lambda i: (0, i)),
            ],
            [
                pltpu.VMEM((rows, tile), F32), pltpu.VMEM((rows, tile), F32),
                pltpu.VMEM((rows, tile), F32), pltpu.VMEM((rows, tile), BF16),
            ],
            "first_back",
            12 * count_,
        )

    start_grad, tap_grad_start = first_back_tiles(0, tiles - 1, hidden_one)
    start_grad, hidden_one, project_parts, expand_came = meet(
        start_grad, hidden_one, project_parts, expand_came
    )
    expand_parts = exchange(pair_sum(expand_grad_own, expand_came, places), "xy")
    project_parts = exchange(split(added(project_parts), chans), "chan")
    end_grad, tap_grad_end = first_back_tiles(tiles - 1, 1, hidden_one)
    end_grad, expand_parts, project_parts = meet(end_grad, expand_parts, project_parts)
    weight_grad = joined([start_grad, end_grad])
    tap_grad_one = jnp.concatenate([tap_grad_start, tap_grad_end], 1)

    small_width = 3 * LANES
    tap_grads = jnp.concatenate([tap_grad_one, tap_grad_two], 0).T
    left_grad = jnp.concatenate([weight_grad[:, :C0], tap_grads], 1)
    left_grad = jnp.pad(left_grad, ((0, 0), (0, small_width - left_grad.shape[1])))
    right_grad = jnp.concatenate([weight_grad[:, C0:], excite_grad], 1)
    right_grad = jnp.pad(right_grad, ((0, 0), (0, small_width - right_grad.shape[1])))
    small_own = jnp.where(first_core, left_grad, right_grad)
    small_came = swap(jnp.where(first_core, right_grad, left_grad), "core", 1)
    small_came, project_parts, head_shard = meet(small_came, project_parts, head_shard)
    small_parts = exchange(pair_sum(small_own, small_came, places), "xy")
    project_shard = added(project_parts)
    small_middle = added(small_parts)
    mixed_middle = jnp.concatenate([small_middle, added(expand_parts)], 1)
    mixed_parts = exchange(split(mixed_middle, chans), "chan")
    project_low = copies(project_shard.astype(BF16), "xy")
    mixed_parts, project_low = meet(mixed_parts, project_low)
    mixed_shard = added(mixed_parts)
    mixed_low = copies(mixed_shard.astype(BF16), "xy")

    shards = (head_shard, project_shard, mixed_shard)
    squares = sum(jnp.sum(shard * shard) for shard in shards)
    route_grad_in = jnp.where(first_core, route_grad_in, jnp.roll(route_grad_in, HALF, axis=1))
    route_grad = jnp.concatenate([route_grad_in, route_grad_out], 0)
    scalars = jnp.concatenate([squares[None], jnp.sum(losses, 0)])
    packed = jnp.concatenate([route_grad.reshape(-1, LANES), jnp.pad(scalars, (0, LANES - 3))[None]])
    packed = total_sum(packed)
    route_sum = packed[:-1].reshape(route_grad.shape)
    square_sum, loss_total, weight_total = packed[-1, 0], packed[-1, 1], packed[-1, 2]
    clip_norm = jnp.sqrt(square_sum + jnp.sum(route_sum * route_sum)) / weight_total
    factor = jnp.minimum(1.0, CLIP / (clip_norm + 1e-06)) / weight_total
    scalar = factor[None]

    if height % 8 == 0:
        line, spot = height, jnp.stack([place, core])
        project_mine, mixed_mine = joined(project_low), joined(mixed_low)
    else:
        line, spot = column.shape[0], jnp.stack([jnp.zeros_like(place), core])
        project_mine, mixed_mine = in_order(project_low), in_order(mixed_low)
    project_pair = [project_mine, swap(project_mine, "core", 1)]
    mixed_pair = [mixed_mine, swap(mixed_mine, "core", 1)]
    column_out = adamw(
        scalar,
        spot,
        line,
        mixed_pair,
        (
            (0, 0, 0, C0 + 2 * TAPS),
            (1, 0, C0, SE),
            (0, 0, small_width, HALF * C0),
            (1, 0, small_width, HALF * C0),
        ),
        column,
        column_first.T,
        column_second.T,
        column_average.T,
    )
    row_out = adamw(
        scalar,
        spot,
        line,
        mixed_pair + project_pair,
        ((1, 0, 0, C0), (1, 0, C0 + SE, SE), (0, 1, 0, HALF * C2), (1, 1, 0, HALF * C2)),
        row_master,
        row_first,
        row_second,
        row_average,
    )
    head_out = adamw_head(
        scalar, head_shard, head_master.T, head_first.T, head_second.T, head_average.T
    )
    route_out_new = adamw_values(
        route_master, route_first, route_second, route_average, route_sum * factor
    )
    return (
        *[value.T for value in column_out],
        *row_out,
        *[value.T for value in head_out],
        *route_out_new,
        loss_total,
        weight_total,
        clip_norm,
    )


def solution(mesh):
    groups = mesh.devices.shape[0] // 2
    fine = Mesh(
        mesh.devices.reshape(groups, 2, mesh.devices.shape[1]), ("xy", "core", "chan")
    )
    dp = ("xy", "core")
    every = ("xy", "core", "chan")
    column, row, head_spec = P(None, "chan"), P("chan", None), P(None, every)
    return jax.shard_map(
        on_device,
        mesh=fine,
        in_specs=(P(dp, "chan", None), P(dp), P(dp), P())
        + (column,) * 4
        + (row,) * 4
        + (head_spec,) * 4
        + (P(),) * 4,
        out_specs=(column,) * 5 + (row,) * 5 + (head_spec,) * 5 + (P(),) * 8,
        check_vma=False,
    )
```

```python
import functools
import math

import jax
import jax.numpy as jnp
from jax import lax
from jax.experimental import pallas as pl
from jax.experimental.pallas import tpu as pltpu
from jax.sharding import Mesh
from jax.sharding import PartitionSpec as P

C0 = 192
C2 = 320
SE = 48
CLASSES = 1000
NE = 8
HALF = NE // 2
KERNEL = 5
TAPS = KERNEL * KERNEL
MAP = 8
STEP = 10
LANES = 128

HIGH = lax.Precision.HIGHEST
BETA_ONE = 0.9
BETA_TWO = 0.999
EPSILON = 1e-08
DECAY = 0.05
RATE = 0.05
CLIP = 0.02
SMOOTH = 0.9

F32 = jnp.float32
BF16 = jnp.bfloat16
FLOPS_A_MICRO = 1.1e9
HBM = "hbm"
VMEM_BYTES = 60 * 1024 * 1024


def nn(left, right):
    return jnp.dot(left, right, preferred_element_type=F32)


def nt(left, right):
    return lax.dot_general(left, right, (((1,), (1,)), ((), ())), preferred_element_type=F32)


def high_nn(left, right):
    return jnp.dot(left, right, precision=HIGH, preferred_element_type=F32)


def high_nt(left, right):
    return lax.dot_general(
        left, right, (((1,), (1,)), ((), ())), precision=HIGH, preferred_element_type=F32
    )


def high_tn(left, right):
    return lax.dot_general(
        left, right, (((0,), (0,)), ((), ())), precision=HIGH, preferred_element_type=F32
    )


def turn(values):
    return values.T


def sig(values):
    return 0.5 * jnp.tanh(0.5 * values) + 0.5


def slope(values, gate):
    return gate * (1.0 + values * (1.0 - gate))


def loop(count, body):
    def step(index, carry):
        body(index)
        return carry

    lax.fori_loop(0, count, step, 0)


def rows_at(index, count):
    return pl.ds(pl.multiple_of(index * count, count), count)


def lanes_at(index):
    return pl.ds(pl.multiple_of(index * LANES, LANES), LANES)


def depthwise(source, taps, lanes, batch, flip, emit):
    parts = batch // 8
    weights = [taps[TAPS - 1 - t if flip else t, :, lanes] for t in range(TAPS)]
    for down in range(MAP):
        total = {}
        for step_y in range(-2, 3):
            line = down + step_y
            if not 0 <= line < MAP:
                continue
            for spot in range(MAP):
                for part in range(parts):
                    value = source[pl.ds((line * MAP + spot) * batch + 8 * part, 8), lanes]
                    for step_x in range(-2, 3):
                        place = spot - step_x
                        if not 0 <= place < MAP:
                            continue
                        term = value * weights[(step_y + 2) * KERNEL + step_x + 2]
                        key = (place, part)
                        total[key] = total[key] + term if key in total else term
        for (place, part), value in total.items():
            emit((down * MAP + place) * batch + 8 * part, value)


def depthwise_weight(source, grad, lanes, batch, store):
    parts = batch // 8
    for step_y in range(-2, 3):
        total = {}
        for down in range(MAP):
            line = down + step_y
            if not 0 <= line < MAP:
                continue
            for part in range(parts):
                slopes = [
                    grad[pl.ds((down * MAP + spot) * batch + 8 * part, 8), lanes]
                    for spot in range(MAP)
                ]
                for spot in range(MAP):
                    value = source[pl.ds((line * MAP + spot) * batch + 8 * part, 8), lanes]
                    for step_x in range(-2, 3):
                        place = spot - step_x
                        if not 0 <= place < MAP:
                            continue
                        key = (step_x, spot % 2)
                        term = value * slopes[place]
                        total[key] = total[key] + term if key in total else term
        for step_x in range(-2, 3):
            value = total[(step_x, 0)] + total[(step_x, 1)]
            store((step_y + 2) * KERNEL + step_x + 2, jnp.sum(value, axis=0, keepdims=True))


def pair_gates(gates, width):
    batch = gates.shape[0]
    spots = lax.broadcasted_iota(jnp.int32, (batch, 2 * width), 1)
    out = []
    for pair in range(HALF):
        left = jnp.broadcast_to(gates[:, 2 * pair : 2 * pair + 1], (batch, 2 * width))
        right = jnp.broadcast_to(gates[:, 2 * pair + 1 : 2 * pair + 2], (batch, 2 * width))
        out.append(jnp.where(spots < width, left, right))
    return out


def split_sums(values, width):
    columns = []
    for value in values:
        spots = lax.broadcasted_iota(jnp.int32, value.shape, 1)
        columns.append(jnp.sum(jnp.where(spots < width, value, 0.0), axis=1, keepdims=True))
        columns.append(jnp.sum(jnp.where(spots < width, 0.0, value), axis=1, keepdims=True))
    return jnp.concatenate(columns, axis=1)


def grouped(values, batch):
    return values.reshape(values.shape[0] // batch, batch, values.shape[1])


def flat(values):
    return values.reshape(values.shape[0] * values.shape[1], values.shape[2])


def first_forward(
    x_ref, left_ref, right_ref, taps_ref, mask_ref, count_ref, route_ref,
    conv_ref, wide_ref, twice_ref, mean_ref, gate_ref, small_gates_ref, large_gates_ref,
    act, deep, total,
):
    batch, tile = count_ref.shape[0], act.shape[1]
    line = MAP * batch
    step = pl.program_id(0)

    act[...] = nt(x_ref[...], left_ref[:, :C0])

    def expand(index):
        rows = rows_at(index, line)
        for part in range(tile // LANES):
            lanes = slice(part * LANES, (part + 1) * LANES)
            here = act[rows, lanes]
            act[rows, lanes] = here * sig(here) * mask_ref[rows, :]

    loop(MAP, expand)

    def conv(index):
        lanes = lanes_at(index)

        def emit(row, value):
            conv_ref[pl.ds(row, 8), lanes] = value

        depthwise(act, taps_ref, lanes, batch, False, emit)

    loop(tile // LANES, conv)

    def activate(index):
        rows = rows_at(index, line)
        for part in range(tile // LANES):
            lanes = slice(part * LANES, (part + 1) * LANES)
            here = conv_ref[rows, lanes]
            deep[rows, lanes] = (here * sig(here) * mask_ref[rows, :]).astype(BF16)

    loop(MAP, activate)
    part_sum = nn(deep[...], right_ref[:, :C0])

    @pl.when(step == 0)
    def _():
        total[...] = part_sum

    @pl.when(step > 0)
    def _():
        total[...] += part_sum

    @pl.when(step == pl.num_programs(0) - 1)
    def _():
        mean_ref[...] = jnp.zeros_like(mean_ref)

        def finish(index):
            rows = rows_at(index, line)
            value = x_ref[rows, :].astype(F32) + total[rows, :]
            low = value.astype(BF16)
            twice_ref[rows, :C0] = low
            twice_ref[rows, C0:] = low
            for part in range(2):
                lanes = slice(0, LANES) if part == 0 else slice(LANES, C0)
                kept = value[:, lanes] * mask_ref[rows, : lanes.stop - lanes.start]
                mean_ref[:, lanes] += jnp.sum(grouped(kept, batch), axis=0)

        loop(MAP, finish)
        mean_ref[...] = mean_ref[...] / count_ref[:, :1]
        gates = jax.nn.sigmoid(high_nn(mean_ref[...], route_ref[...]))
        gate_ref[...] = gates
        for pair, value in enumerate(pair_gates(gates, C0)):
            small_gates_ref[pair] = value
        for pair, value in enumerate(pair_gates(gates, C2)):
            large_gates_ref[pair] = value

        def widen(index):
            rows = rows_at(index, line)
            value = grouped(twice_ref[rows, :].astype(F32), batch)
            for pair in range(HALF):
                lanes = slice(pair * 2 * C0, (pair + 1) * 2 * C0)
                wide_ref[rows, lanes] = flat(value * small_gates_ref[pair][None]).astype(BF16)

        loop(MAP, widen)


def second_forward(
    wide_ref, own_ref, far_ref, taps_ref, mask_ref, count_ref, squeeze_ref, excite_ref,
    mixed_ref, conv_ref, mean_ref, units_ref, scale_ref,
    act,
):
    batch, tile = count_ref.shape[0], act.shape[1]
    line = MAP * batch
    step = pl.program_id(0)
    half = own_ref.shape[1]

    def expand(index):
        rows = rows_at(index, 4 * line)
        mixed_ref[rows, :] = nt(wide_ref[rows, :half], own_ref[...]) + nt(
            wide_ref[rows, half:], far_ref[...]
        )

    loop(MAP // 4, expand)

    def activate(index):
        rows = rows_at(index, line)
        for part in range(tile // LANES):
            lanes = slice(part * LANES, (part + 1) * LANES)
            here = mixed_ref[rows, lanes]
            act[rows, lanes] = here * sig(here) * mask_ref[rows, :]

    loop(MAP, activate)

    def conv(index):
        lanes = lanes_at(index)

        def emit(row, value):
            conv_ref[pl.ds(row, 8), lanes] = value

        depthwise(act, taps_ref, lanes, batch, False, emit)

    loop(tile // LANES, conv)
    mean_ref[...] = jnp.zeros_like(mean_ref)

    def pool(index):
        rows = rows_at(index, line)
        for part in range(tile // LANES):
            lanes = slice(part * LANES, (part + 1) * LANES)
            here = conv_ref[rows, lanes]
            kept = here * sig(here) * mask_ref[rows, :]
            mean_ref[:, lanes] += jnp.sum(grouped(kept, batch), axis=0)

    loop(MAP, pool)
    mean_ref[...] = mean_ref[...] / count_ref[:, :1]
    units = high_nn(mean_ref[...], squeeze_ref[...])

    @pl.when(step == 0)
    def _():
        units_ref[...] = units

    @pl.when(step > 0)
    def _():
        units_ref[...] += units

    @pl.when(step == pl.num_programs(0) - 1)
    def _():
        value = units_ref[...]
        scale_ref[...] = jax.nn.sigmoid(high_nt(value * jax.nn.sigmoid(value), excite_ref[...]))


def project(
    conv_ref, scale_ref, own_ref, far_ref, mask_ref, count_ref, gates_ref, route_ref,
    each_ref, twice_ref, mean_ref, gate_ref, head_gates_ref,
    scaled,
):
    batch = count_ref.shape[0]
    line = MAP * batch
    block, width = scaled.shape
    step = pl.program_id(0)

    def activate(index):
        rows = rows_at(index, line)
        for part in range(width // LANES):
            lanes = slice(part * LANES, (part + 1) * LANES)
            here = conv_ref[rows, lanes]
            kept = grouped(here * sig(here) * mask_ref[rows, :], batch)
            scaled[rows, lanes] = flat(kept * scale_ref[:, lanes][None]).astype(BF16)

    loop(block // line, activate)
    pairs = HALF // 2

    @pl.when(step == 0)
    def _():
        mean_ref[...] = jnp.zeros_like(mean_ref)

    value = scaled[...]
    total = None
    for pair in range(HALF):
        weights = own_ref if pair < pairs else far_ref
        inner = slice((pair % pairs) * 2 * C2, (pair % pairs + 1) * 2 * C2)
        each = nn(value, weights[:, inner])
        each_ref[:, pair * 2 * C2 : (pair + 1) * 2 * C2] = each.astype(BF16)
        term = grouped(each, batch) * gates_ref[pair][None]
        total = term if total is None else total + term
    total = flat(total)
    value = total[:, :C2] + total[:, C2:]
    low = value.astype(BF16)
    twice_ref[:, :C2] = low
    twice_ref[:, C2:] = low
    kept = grouped(value * mask_ref[:, :1], batch)
    mean_ref[...] += jnp.sum(kept, axis=0)

    @pl.when(step == pl.num_programs(0) - 1)
    def _():
        mean_ref[...] = mean_ref[...] / count_ref[:, :1]
        gates = jax.nn.sigmoid(high_nn(mean_ref[...], route_ref[...]))
        gate_ref[...] = gates
        for pair, value in enumerate(pair_gates(gates, C2)):
            head_gates_ref[pair] = value


def head(
    twice_ref, near_ref, distant_ref, mask_ref, count_ref, label_ref, class_ref,
    gates_ref, gate_ref, mean_ref, route_ref,
    own_grad_ref, far_grad_ref, loss_ref, hidden_grad_ref, route_grad_ref,
    weights, wide_ref, mixed, slopes, turned, pooled, total, means, logit_slopes, arrivals,
):
    batch = count_ref.shape[0]
    line = MAP * batch
    step = pl.program_id(0)
    half = near_ref.shape[0]
    experts = NE * C2
    columns = own_grad_ref.shape[1]

    @pl.when(step == 0)
    def _():
        loads = [
            pltpu.make_async_copy(
                source, weights.at[pl.ds(side * half, half), :], arrivals.at[side]
            )
            for side, source in enumerate((near_ref, distant_ref))
        ]
        for load in loads:
            load.start()
        pooled[...] = jnp.zeros_like(pooled)

        def widen(index):
            rows = rows_at(index, line)
            value = grouped(twice_ref[rows, :].astype(F32), batch)
            for pair in range(HALF):
                lanes = slice(pair * 2 * C2, (pair + 1) * 2 * C2)
                wide_ref[rows, lanes] = flat(value * gates_ref[pair][None]).astype(BF16)

        loop(MAP, widen)
        for load in loads:
            load.wait()

        def expand(index):
            rows = rows_at(index, 4 * line)
            mixed[rows, :] = nt(wide_ref[rows, :], weights[:, :experts])

        loop(MAP // 4, expand)

        def pool(index):
            rows = rows_at(index, line)
            for part in range(2 * half // LANES):
                lanes = slice(part * LANES, (part + 1) * LANES)
                here = mixed[rows, lanes]
                kept = here * sig(here) * mask_ref[rows, :]
                pooled[:, lanes] += jnp.sum(grouped(kept, batch), axis=0)

        loop(MAP, pool)
        mean = (pooled[...] / count_ref[:, :1]).astype(BF16)
        logits = nn(mean, weights[:, experts : experts + CLASSES])
        spots = lax.broadcasted_iota(jnp.int32, logits.shape, 1)
        onehot = (spots == label_ref[...]).astype(F32)
        weight = jnp.sum(onehot * class_ref[...], axis=1, keepdims=True)
        top = jnp.max(logits, axis=1, keepdims=True)
        powers = jnp.exp(logits - top)
        summed = jnp.sum(powers, axis=1, keepdims=True)
        loss = weight * (top + jnp.log(summed) - jnp.sum(logits * onehot, axis=1, keepdims=True))
        loss_ref[...] = jnp.concatenate([loss, weight], axis=1)
        logit_grad = (weight * (powers / summed - onehot)).astype(BF16)
        means[...] = mean
        logit_slopes[...] = jnp.zeros_like(logit_slopes)
        logit_slopes[:, :CLASSES] = logit_grad
        pooled[...] = nt(logit_grad, weights[:, experts : experts + CLASSES]) / count_ref[:, :1]

        def back(index):
            rows = rows_at(index, line)
            for part in range(2 * half // LANES):
                lanes = slice(part * LANES, (part + 1) * LANES)
                here = mixed[rows, lanes]
                value = grouped(mask_ref[rows, :] * slope(here, sig(here)), batch)
                slopes[rows, lanes] = flat(value * pooled[:, lanes][None]).astype(BF16)

        loop(MAP, back)
        for part in range(2 * half // LANES):
            lanes = slice(part * LANES, (part + 1) * LANES)
            turned[lanes, :] = turn(slopes[:, lanes])

    blocks = pl.num_programs(0) // 2
    side = 1 - step // blocks
    block = step % blocks
    place = pl.ds(pl.multiple_of(side * half, half), half)

    def weight_grad(out):
        for index in range(2):

            @pl.when(block == index)
            def _(index=index):
                begin = index * columns
                width = min(columns, experts - begin)
                out[:, :width] = nn(turned[place, :], wide_ref[:, begin : begin + width]).astype(
                    out.dtype
                )
                if width < columns:
                    out[:, width:] = lax.dot_general(
                        means[:, place], logit_slopes[...],
                        (((0,), (0,)), ((), ())), preferred_element_type=F32,
                    ).astype(out.dtype)

    @pl.when(side == 1)
    def _():
        weight_grad(far_grad_ref)

    @pl.when(side == 0)
    def _():
        weight_grad(own_grad_ref)

    @pl.when(step == pl.num_programs(0) - 1)
    def _():
        sums = [jnp.zeros((batch, 2 * C2), F32)] * HALF

        def pull(index, sums):
            rows = rows_at(index, 2 * line)
            value = slopes[rows, :]
            hidden = grouped(twice_ref[rows, :].astype(F32), batch)
            summed = None
            sums = list(sums)
            for pair in range(HALF):
                if pair % 2 == 0:
                    begin = pair * 2 * C2
                    both = nn(value, weights[:, begin : begin + 4 * C2])
                each = grouped(both[:, 2 * C2 * (pair % 2) : 2 * C2 * (pair % 2 + 1)], batch)
                sums[pair] = sums[pair] + jnp.sum(each * hidden, axis=0)
                term = each * gates_ref[pair][None]
                summed = term if summed is None else summed + term
            summed = flat(summed)
            total[rows, :] = summed[:, :C2] + summed[:, C2:]
            return tuple(sums)

        sums = lax.fori_loop(0, MAP // 2, pull, tuple(sums))
        gates = gate_ref[...]
        logit = split_sums(sums, C2) * gates * (1.0 - gates)
        route_grad_ref[...] = high_tn(mean_ref[...], logit)
        back_rows = high_nt(logit, route_ref[...]) / count_ref[:, :1]

        def finish(index):
            rows = rows_at(index, line)
            value = grouped(total[rows, :], batch) + back_rows[None] * grouped(
                jnp.broadcast_to(mask_ref[rows, :1], (line, C2)), batch
            )
            low = flat(value).astype(BF16)
            hidden_grad_ref[rows, :C2] = low
            hidden_grad_ref[rows, C2:] = low

        loop(MAP, finish)


def project_back(
    hidden_ref, gates_ref, far_each_ref, own_ref, far_ref, conv_ref, scale_ref, mask_ref,
    full_scale_ref, units_ref, mean_ref, excite_ref,
    grad_ref, own_grad_ref, far_grad_ref, gate_sum_ref, unit_grad_ref, small_ref,
    spread, scaled, sums, each_ref, arrival,
):
    batch, tile = scale_ref.shape
    line = MAP * batch
    step = pl.program_id(0)
    half = own_ref.shape[1]
    arriving = pltpu.make_async_copy(far_each_ref, each_ref, arrival)

    @pl.when(step == 0)
    def _():
        arriving.start()

        def widen(index):
            rows = rows_at(index, line)
            value = grouped(hidden_ref[rows, :].astype(F32), batch)
            for pair in range(HALF):
                lanes = slice(pair * 2 * C2, (pair + 1) * 2 * C2)
                spread[rows, lanes] = flat(value * gates_ref[pair][None]).astype(BF16)

        loop(MAP, widen)

    def pull(index):
        rows = rows_at(index, 4 * line)
        grad_ref[rows, :] = nt(spread[rows, :half], own_ref[...]) + nt(
            spread[rows, half:], far_ref[...]
        )

    loop(MAP // 4, pull)
    place = pl.ds(pl.multiple_of(step * tile, tile), tile)
    sums[:, place] = jnp.zeros((batch, tile), F32)

    def activate(index):
        rows = rows_at(index, line)
        for part in range(tile // LANES):
            lanes = slice(part * LANES, (part + 1) * LANES)
            here = conv_ref[rows, lanes]
            kept = here * sig(here) * mask_ref[rows, :]
            scaled[rows, lanes] = flat(grouped(kept, batch) * scale_ref[:, lanes][None]).astype(BF16)
            added = jnp.sum(grouped(grad_ref[rows, lanes] * kept, batch), axis=0)
            sums[:, pl.ds(pl.multiple_of(step * tile + part * LANES, LANES), LANES)] += added

    loop(MAP, activate)
    turned = turn(scaled[...])
    far_grad_ref[...] = nn(turned, spread[:, half:])
    own_grad_ref[...] = nn(turned, spread[:, :half])

    @pl.when(step == pl.num_programs(0) - 1)
    def _():
        arriving.wait()
        gate_sum_ref[...] = jnp.zeros_like(gate_sum_ref)

        def weigh(index):
            rows = rows_at(index, line)
            value = grouped(hidden_ref[rows, :].astype(F32), batch)
            for pair in range(HALF):
                lanes = slice(pair * 2 * C2, (pair + 1) * 2 * C2)
                each = grouped(each_ref[rows, lanes].astype(F32), batch)
                gate_sum_ref[pair] += jnp.sum(each * value, axis=0)

        loop(MAP, weigh)
        scale = full_scale_ref[...]
        pre = sums[...] * scale * (1.0 - scale)
        units = units_ref[...]
        gate = jax.nn.sigmoid(units)
        unit_grad = high_nn(pre, excite_ref[...]) * slope(units, gate)
        unit_grad_ref[...] = unit_grad
        small_ref[:, :SE] = high_tn(pre, units * gate)
        small_ref[:, SE:] = high_tn(mean_ref[...], unit_grad)


def second_back(
    grad_ref, scale_ref, unit_grad_ref, squeeze_ref, count_ref, mask_ref, conv_ref, mixed_ref,
    taps_ref, wide_ref, own_ref, far_ref, twice_ref, gates_ref, gate_ref, gate_sum_ref,
    route_ref, mean_ref,
    own_grad_ref, far_grad_ref, tap_grad_ref, hidden_grad_ref, route_grad_ref,
    act, inner, slopes, own_all, far_all,
):
    batch, tile = scale_ref.shape
    line = MAP * batch
    step = pl.program_id(0)
    half = own_ref.shape[1]
    place = pl.ds(pl.multiple_of(step * tile, tile), tile)
    own_all[place, :] = own_ref[...]
    far_all[place, :] = far_ref[...]
    pool_grad = high_nt(unit_grad_ref[...], squeeze_ref[...]) / count_ref[:, :1]

    def activate(index):
        rows = rows_at(index, line)
        for part in range(tile // LANES):
            lanes = slice(part * LANES, (part + 1) * LANES)
            mask = mask_ref[rows, :]
            here = mixed_ref[rows, lanes]
            act[rows, lanes] = here * sig(here) * mask
            here = conv_ref[rows, lanes]
            value = grouped(grad_ref[rows, lanes], batch) * scale_ref[:, lanes][None]
            value = flat(value + pool_grad[:, lanes][None])
            inner[rows, lanes] = value * mask * slope(here, sig(here))

    loop(MAP, activate)

    def conv(index):
        lanes = lanes_at(index)

        def store(tap, value):
            tap_grad_ref[tap : tap + 1, lanes] = value

        depthwise_weight(act, inner, lanes, batch, store)

        def emit(row, value):
            act[pl.ds(row, 8), lanes] = value

        depthwise(inner, taps_ref, lanes, batch, True, emit)

    loop(tile // LANES, conv)

    def deactivate(index):
        rows = rows_at(index, line)
        for part in range(tile // LANES):
            lanes = slice(part * LANES, (part + 1) * LANES)
            here = mixed_ref[rows, lanes]
            value = act[rows, lanes] * mask_ref[rows, :] * slope(here, sig(here))
            slopes[rows, pl.ds(pl.multiple_of(step * tile + part * LANES, LANES), LANES)] = (
                value.astype(BF16)
            )

    loop(MAP, deactivate)
    turned = turn(slopes[:, place])
    far_grad_ref[...] = nn(turned, wide_ref[:, half:])
    own_grad_ref[...] = nn(turned, wide_ref[:, :half])

    @pl.when(step == pl.num_programs(0) - 1)
    def _():
        sums = [jnp.zeros((batch, 2 * C0), F32)] * HALF
        pairs = HALF // 2

        def pull(index, sums):
            rows = rows_at(index, 2 * line)
            value = slopes[rows, :]
            hidden = grouped(twice_ref[rows, :].astype(F32), batch)
            summed = None
            sums = list(sums)
            for pair in range(HALF):
                weights = own_all if pair < pairs else far_all
                lanes = slice((pair % pairs) * 2 * C0, (pair % pairs + 1) * 2 * C0)
                each = grouped(nn(value, weights[:, lanes]), batch)
                sums[pair] = sums[pair] + jnp.sum(each * hidden, axis=0)
                term = each * gates_ref[pair][None]
                summed = term if summed is None else summed + term
            act[rows, : 2 * C0] = flat(summed)
            return tuple(sums)

        sums = lax.fori_loop(0, MAP // 2, pull, tuple(sums))
        gates = gate_ref[...]
        logit = split_sums(sums, C0) + split_sums([gate_sum_ref[k] for k in range(HALF)], C2)
        logit = logit * gates * (1.0 - gates)
        route_grad_ref[...] = high_tn(mean_ref[...], logit)
        back_rows = high_nt(logit, route_ref[...]) / count_ref[:, :1]

        def finish(index):
            rows = rows_at(index, line)
            summed = act[rows, : 2 * C0]
            value = grouped(summed[:, :C0] + summed[:, C0:], batch) + back_rows[None] * grouped(
                jnp.broadcast_to(mask_ref[rows, :1], (line, C0)), batch
            )
            hidden_grad_ref[rows, :] = flat(value).astype(BF16)

        loop(MAP, finish)


def first_back(
    x_ref, left_ref, right_ref, taps_ref, mask_ref, conv_ref, hidden_ref,
    weight_grad_ref, tap_grad_ref,
    act, inner, wide, deep,
):
    tile = act.shape[1]
    batch = x_ref.shape[0] // (MAP * MAP)
    line = MAP * batch

    def expand(index):
        rows = rows_at(index, line)
        for part in range(tile // LANES):
            lanes = slice(part * LANES, (part + 1) * LANES)
            mask = mask_ref[rows, :]
            here = act[rows, lanes]
            gate = sig(here)
            act[rows, lanes] = here * gate * mask
            wide[rows, lanes] = slope(here, gate) * mask
            here = conv_ref[rows, lanes]
            gate = sig(here)
            deep[rows, lanes] = (here * gate * mask).astype(BF16)
            inner[rows, lanes] = inner[rows, lanes] * mask * slope(here, gate)

    act[...] = nt(x_ref[...], left_ref[:, :C0])
    inner[...] = nt(hidden_ref[...], right_ref[:, :C0])
    loop(MAP, expand)
    weight_grad_ref[:, C0:] = nn(turn(deep[...]), hidden_ref[...])

    def conv(index):
        lanes = lanes_at(index)

        def store(tap, value):
            tap_grad_ref[tap : tap + 1, lanes] = value

        depthwise_weight(act, inner, lanes, batch, store)

        def emit(row, value):
            act[pl.ds(row, 8), lanes] = value

        depthwise(inner, taps_ref, lanes, batch, True, emit)

    loop(tile // LANES, conv)

    def deactivate(index):
        rows = rows_at(index, line)
        for part in range(tile // LANES):
            lanes = slice(part * LANES, (part + 1) * LANES)
            deep[rows, lanes] = (act[rows, lanes] * wide[rows, lanes]).astype(BF16)

    loop(MAP, deactivate)
    weight_grad_ref[:, :C0] = nn(turn(deep[...]), x_ref[...])


def adamw_values(master, first, second, average, grad):
    first = BETA_ONE * first + (1.0 - BETA_ONE) * grad
    second = BETA_TWO * second + (1.0 - BETA_TWO) * grad * grad
    ratio = first / (1.0 - BETA_ONE**STEP) / (jnp.sqrt(second / (1.0 - BETA_TWO**STEP)) + EPSILON)
    master = master - RATE * (ratio + DECAY * master)
    average = SMOOTH * average + (1.0 - SMOOTH) * master
    return (first, second, master, average, master.astype(BF16))


def clipped(total):
    routers = total[: total.shape[0] - 1]
    squares, weight = total[total.shape[0] - 1 :, :1], total[total.shape[0] - 1 :, 2:3]
    norm = jnp.sqrt(squares + jnp.sum(routers * routers, keepdims=True)) / weight
    return norm, jnp.minimum(1.0, CLIP / (norm + 1e-06)) / weight


def adamw_kernel(segments, arrays, place_ref, factor_ref, *refs):
    pieces = refs[: 2 * arrays]
    master, first, second, average = refs[2 * arrays : 2 * arrays + 4]
    outs = refs[2 * arrays + 4 : 2 * arrays + 9]
    whole = refs[-1]

    def fill(core):
        at = 0
        for side, array, begin, width in segments:
            source = pieces[2 * array + (side ^ core)]
            whole[:, at : at + width] = source[:, begin : begin + width].astype(F32)
            at += width

    for core in range(2):

        @pl.when(place_ref[1] == core)
        def _(core=core):
            fill(core)

    grad = whole[...] * factor_ref[0, 1]
    values = adamw_values(master[...], first[...], second[...], average[...], grad)
    for out, value in zip(outs, values):
        out[...] = value


def adamw(factor, spot, rows, pieces, segments, master, first, second, average):
    height, width = master.shape
    specs = [
        pl.BlockSpec((rows, piece.shape[1]), lambda i, place: (i ^ place[0], 0)) for piece in pieces
    ]
    full = pl.BlockSpec((rows, width), lambda i, place: (i, 0))
    types = (F32, F32, F32, F32, BF16)
    return pl.pallas_call(
        functools.partial(adamw_kernel, segments, len(pieces) // 2),
        grid_spec=pltpu.PrefetchScalarGridSpec(
            num_scalar_prefetch=1,
            grid=(height // rows,),
            in_specs=[pl.BlockSpec(memory_space=pltpu.SMEM)] + specs + [full] * 4,
            out_specs=[full] * 5,
            scratch_shapes=[pltpu.VMEM((rows, width), F32)],
        ),
        out_shape=[jax.ShapeDtypeStruct((height, width), kind) for kind in types],
        compiler_params=pltpu.CompilerParams(vmem_limit_bytes=VMEM_BYTES),
        name="adamw",
    )(spot, factor, *pieces, master, first, second, average)


def adamw_head_kernel(total_ref, grad, master, first, second, average, *outs):
    norm, factor = clipped(total_ref[...])
    outs[5][...] = jnp.concatenate([norm, factor], axis=1)
    values = adamw_values(master[...], first[...], second[...], average[...], grad[...] * factor)
    for out, value in zip(outs, values):
        out[...] = value


def adamw_head(total, grad, *state):
    height, width = state[0].shape
    part = 14 * LANES
    block = pl.BlockSpec((height, part), lambda i: (0, i))
    types = (F32, F32, F32, F32, BF16)
    return pl.pallas_call(
        adamw_head_kernel,
        grid=(pl.cdiv(width, part),),
        in_specs=[pl.BlockSpec(total.shape, lambda i: (0, 0))] + [block] * 5,
        out_specs=[block] * 5 + [pl.BlockSpec((1, 2), lambda i: (0, 0))],
        out_shape=[jax.ShapeDtypeStruct((height, width), kind) for kind in types]
        + [jax.ShapeDtypeStruct((1, 2), F32)],
        compiler_params=pltpu.CompilerParams(vmem_limit_bytes=VMEM_BYTES),
        name="adamw_head",
    )(total, grad, *state)


def swap(values, axis, distance):
    size = lax.axis_size(axis)
    return lax.ppermute(values, axis, [(i, i ^ distance) for i in range(size)])


def meet(*values):
    return lax.optimization_barrier(values)


def copies(values, axis):
    return [values] + [swap(values, axis, k) for k in range(1, lax.axis_size(axis))]


def joined(parts):
    return jnp.concatenate(parts, axis=0)


def pair_sum(own, came, parts):
    rows = own.shape[0] // parts
    return [own[k * rows : (k + 1) * rows] + came[k * rows : (k + 1) * rows] for k in range(parts)]


def exchange(blocks, axis):
    return [blocks[0]] + [swap(block.astype(BF16), axis, k) for k, block in enumerate(blocks) if k]


def added(parts):
    total = parts[0]
    for value in parts[1:]:
        total = total + value.astype(F32)
    return total


def split(values, parts):
    rows = values.shape[0] // parts
    return [values[k * rows : (k + 1) * rows] for k in range(parts)]


def total_sum(values):
    for axis in ("core", "xy", "chan"):
        distance = 1
        while distance < lax.axis_size(axis):
            values = values + swap(values, axis, distance)
            distance *= 2
    return values


def own_order(values, rows):
    place = lax.axis_index("xy")
    return [
        lax.dynamic_slice_in_dim(values, (place ^ k) * rows, rows, 0)
        for k in range(lax.axis_size("xy"))
    ]


def in_order(parts):
    place = lax.axis_index("xy")
    stack = jnp.stack(parts)
    return joined(
        [lax.dynamic_index_in_dim(stack, place ^ k, 0, keepdims=False) for k in range(len(parts))]
    )


def two_parts(values):
    upper = lax.reduce_precision(values, 8, 7)
    return [upper.astype(BF16), (values - upper).astype(BF16)]


def call(kernel, grid, ins, outs, scratch, name, micros):
    def spec(shape, block, index):
        if block is HBM:
            return pl.BlockSpec(memory_space=pl.ANY)
        if block is None:
            return pl.BlockSpec(memory_space=pltpu.VMEM)
        return pl.BlockSpec(block, index)

    in_specs = []
    arrays = []
    for entry in ins:
        array, block, index, *mode = entry
        arrays.append(array)
        if mode:
            in_specs.append(pl.BlockSpec(block, index, pipeline_mode=mode[0]))
        else:
            in_specs.append(spec(array.shape, block, index))
    return pl.pallas_call(
        kernel,
        grid=grid,
        in_specs=in_specs,
        out_specs=[spec(shape, block, index) for shape, kind, block, index in outs],
        out_shape=[jax.ShapeDtypeStruct(shape, kind) for shape, kind, block, index in outs],
        scratch_shapes=scratch,
        compiler_params=pltpu.CompilerParams(
            vmem_limit_bytes=VMEM_BYTES, dimension_semantics=("arbitrary",) * len(grid)
        ),
        cost_estimate=pl.CostEstimate(
            flops=int(micros * FLOPS_A_MICRO), bytes_accessed=1 << 20, transcendentals=0
        ),
        name=name,
    )(*arrays)


def on_device(
    images,
    labels,
    resolution,
    class_weight,
    column_master,
    column_first,
    column_second,
    column_average,
    row_master,
    row_first,
    row_second,
    row_average,
    head_master,
    head_first,
    head_second,
    head_average,
    route_master,
    route_first,
    route_second,
    route_average,
):
    chans, places = lax.axis_size("chan"), lax.axis_size("xy")
    core, place, layer = lax.axis_index("core"), lax.axis_index("xy"), lax.axis_index("chan")
    first_core = core == 0
    batch = images.shape[0] // chans
    slots = MAP * MAP
    rows = slots * batch
    wide = column_master.shape[1] * chans
    height = column_master.shape[1] // places
    begin = C0 + 2 * TAPS + SE
    tile = 3 * LANES
    tiles = wide // tile

    def fixed(array):
        return (array, None, None)

    def whole(array, grid=1):
        zeros = (0,) * array.ndim
        return (array, array.shape, lambda *ids: zeros, pl.Buffered(1))

    column, row = column_master.T, row_master
    column_parts = [column[:, :C0]]
    column_parts += two_parts(column[:, C0 : C0 + 2 * TAPS])
    small_left = jnp.concatenate([part.astype(BF16) for part in column_parts], 1)
    small_left = jnp.pad(small_left, ((0, 0), (0, 2 * C0 - small_left.shape[1])))
    small_right = jnp.concatenate(
        [row[:, :C0].astype(BF16)]
        + two_parts(column[:, C0 + 2 * TAPS : begin])
        + two_parts(row[:, C0 : C0 + SE]),
        1,
    )
    small = joined(own_order(jnp.where(first_core, small_left, small_right), height))
    expand_own = lax.dynamic_slice(
        column, (place * height, begin + core * HALF * C0), (height, HALF * C0)
    ).astype(BF16)
    project_own = lax.dynamic_slice(
        row, (place * height, C0 + SE + core * HALF * C2), (height, HALF * C2)
    ).astype(BF16)
    blocks = 2
    part = pl.cdiv(NE * C2 + CLASSES, blocks * LANES) * LANES
    lanes = blocks * part
    head_own = jnp.pad(head_master.T.astype(BF16), ((0, 0), (0, lanes - NE * C2 - CLASSES)))
    mine = lax.all_to_all(images, "chan", 0, 0, tiled=True)
    small, expand_own, project_own, mine = meet(
        copies(small, "chan"), expand_own, project_own, mine
    )
    small = joined(small).reshape(chans, places, height, 2 * C0)
    small = small.transpose(1, 0, 2, 3).reshape(wide, 2 * C0)
    small_far = swap(small, "core", 1)
    expand_own = copies(expand_own, "chan")
    project_own = joined([project_own, swap(project_own, "chan", 1)])
    expand_own = joined(expand_own)
    left = jnp.where(first_core, small, small_far)
    right = jnp.where(first_core, small_far, small)
    expand_own = copies(expand_own, "xy")
    distance = 2
    project_own = [project_own]
    while distance < chans:
        held = joined(project_own)
        project_own = [held, swap(held, "chan", distance)]
        distance *= 2

    def both(values, at, width):
        upper = values[:, at : at + width].astype(F32)
        return upper + values[:, at + width : at + 2 * width].astype(F32)

    def tap_rows(values):
        return jnp.broadcast_to(values.T[:, None, :], (TAPS, 8, wide))

    taps = both(left, C0, 2 * TAPS)
    first_taps, second_taps = tap_rows(taps[:, :TAPS]), tap_rows(taps[:, TAPS:])
    excite_out = both(right, C0, SE)
    excite_in = both(right, C0 + 2 * SE, SE)
    route_in, route_out = route_master[:C0], route_master[C0:]
    route_in = jnp.where(first_core, route_in, jnp.roll(route_in, HALF, axis=1))

    mine = mine.reshape(chans, batch, slots // chans, C0).transpose(0, 2, 1, 3)
    label = lax.dynamic_slice_in_dim(labels, layer * batch, batch, 0)
    side = lax.dynamic_slice_in_dim(resolution, layer * batch, batch, 0)
    spots = jnp.arange(slots, dtype=jnp.int32)
    inside = ((spots // MAP)[:, None] < side[None, :]) & ((spots % MAP)[:, None] < side[None, :])
    inside = inside.reshape(rows, 1)
    x = jnp.where(inside, mine.reshape(rows, C0), 0)
    x, expand_own, project_own, head_own = meet(x, expand_own, project_own, head_own)
    expand_own, project_own = joined(expand_own), joined(project_own)
    head_own = lax.all_gather(head_own, "chan", axis=0, tiled=True)
    expand_far = swap(expand_own, "core", 1)
    project_own = copies(project_own, "xy")
    mask = jnp.broadcast_to(inside.astype(F32), (rows, LANES))
    count = jnp.broadcast_to((side * side).astype(F32)[:, None], (batch, LANES))

    def tiled(array):
        return (array, (tile, array.shape[1]), lambda i: (i, 0))

    def across(array):
        return (array, (array.shape[0], tile), lambda i: (0, i))

    def tap_tile(array):
        return (array, (TAPS, 8, tile), lambda i: (0, 0, i))

    def out_full(shape, kind):
        zeros = (0,) * len(shape)
        return (shape, kind, shape, lambda *ids: zeros)

    def out_across(height_, kind):
        return ((height_, wide), kind, (height_, tile), lambda i: (0, i))

    def out_tiled(width, kind):
        return ((wide, width), kind, (tile, width), lambda i: (i, 0))

    first_out = call(
        first_forward,
        (tiles,),
        [
            whole(x), tiled(left), tiled(right), tap_tile(first_taps), whole(mask), whole(count),
            whole(route_in),
        ],
        [
            out_across(rows, F32),
            out_full((rows, NE * C0), BF16),
            out_full((rows, 2 * C0), BF16),
            out_full((batch, C0), F32),
            out_full((batch, NE), F32),
            out_full((HALF, batch, 2 * C0), F32),
            out_full((HALF, batch, 2 * C2), F32),
        ],
        [
            pltpu.VMEM((rows, tile), F32), pltpu.VMEM((rows, tile), BF16),
            pltpu.VMEM((rows, C0), F32),
        ],
        "first_forward",
        17,
    )

    (conv_one, mixed_in, twice_one, mean_one, gate_one, gates_one, gates_mid) = first_out
    mixed_in, expand_far, project_own, head_own = meet(
        mixed_in, expand_far, project_own, head_own
    )
    project_own = joined(project_own)
    project_far = swap(project_own, "core", 1)
    head_own = lax.all_gather(head_own, "xy", axis=0, tiled=True)

    mixed_two, conv_two, mean_two, units, scale = call(
        second_forward,
        (tiles,),
        [
            whole(mixed_in), tiled(expand_own), tiled(expand_far), tap_tile(second_taps),
            whole(mask), whole(count), tiled(excite_in), whole(excite_out),
        ],
        [
            out_across(rows, F32),
            out_across(rows, F32),
            out_across(batch, F32),
            out_full((batch, SE), F32),
            out_full((batch, wide), F32),
        ],
        [pltpu.VMEM((rows, tile), F32)],
        "second_forward",
        21,
    )

    conv_two, project_far = meet(conv_two, project_far)

    line = rows // 4

    def out_rows(width, kind):
        return ((rows, width), kind, (line, width), lambda i: (i, 0))

    def by_rows(array):
        return (array, (line, array.shape[1]), lambda i: (i, 0))

    each, twice_two, mean_three, gate_two, gates_two = call(
        project,
        (rows // line,),
        [
            by_rows(conv_two), whole(scale), whole(project_own), whole(project_far),
            by_rows(mask), whole(count), whole(gates_mid), whole(route_out),
        ],
        [
            out_rows(NE * C2, BF16),
            out_rows(2 * C2, BF16),
            out_full((batch, C2), F32),
            out_full((batch, NE), F32),
            out_full((HALF, batch, 2 * C2), F32),
        ],
        [pltpu.VMEM((line, wide), BF16)],
        "project",
        16,
    )

    twice_two, head_own = meet(twice_two, head_own)
    head_far = swap(head_own, "core", 1)
    half = head_own.shape[0]
    head_grad_own, head_grad_far, losses, hidden_two, route_grad_out = call(
        head,
        (2 * blocks,),
        [
            whole(twice_two), (head_own, HBM, None), (head_far, HBM, None), whole(mask),
            whole(count), whole(label[:, None]), whole(class_weight[None, :]), whole(gates_two),
            whole(gate_two), whole(mean_three), whole(route_out),
        ],
        [
            ((half, lanes), BF16, (half, part), lambda i: (0, jnp.maximum(i - blocks, 0))),
            ((half, lanes), BF16, (half, part), lambda i: (0, jnp.minimum(i, blocks - 1))),
            out_full((batch, 2), F32),
            out_full((rows, 2 * C2), BF16),
            out_full((C2, NE), F32),
        ],
        [
            pltpu.VMEM((2 * half, lanes), BF16), pltpu.VMEM((rows, NE * C2), BF16),
            pltpu.VMEM((rows, 2 * half), F32), pltpu.VMEM((rows, 2 * half), BF16),
            pltpu.VMEM((2 * half, rows), BF16), pltpu.VMEM((batch, 2 * half), F32),
            pltpu.VMEM((rows, C2), F32), pltpu.VMEM((batch, 2 * half), BF16),
            pltpu.VMEM((batch, lanes - NE * C2), BF16), pltpu.SemaphoreType.DMA((2,)),
        ],
        "head",
        39,
    )
    head_came = swap(head_grad_far, "core", 1)

    deep_grad, project_grad_own, project_grad_far, gate_sums, unit_grad, excite_grad = call(
        project_back,
        (tiles,),
        [
            whole(hidden_two), whole(gates_mid), (each, HBM, None), tiled(project_own),
            tiled(project_far), across(conv_two), across(scale), whole(mask), whole(scale),
            whole(units), whole(mean_two), whole(excite_out),
        ],
        [
            out_across(rows, F32),
            out_tiled(HALF * C2, F32),
            out_tiled(HALF * C2, F32),
            out_full((HALF, batch, 2 * C2), F32),
            out_full((batch, SE), F32),
            out_full((wide, 2 * SE), F32),
        ],
        [
            pltpu.VMEM((rows, NE * C2), BF16), pltpu.VMEM((rows, tile), BF16),
            pltpu.VMEM((batch, wide), F32), pltpu.VMEM((rows, NE * C2), BF16),
            pltpu.SemaphoreType.DMA(()),
        ],
        "project_back",
        26,
    )
    deep_grad, head_came = meet(deep_grad, head_came)
    high_rows = half // places
    head_blocks = [
        lax.dynamic_slice_in_dim(head_grad_own, (place ^ k) * high_rows, high_rows, 0).astype(F32)
        + lax.dynamic_slice_in_dim(head_came, (place ^ k) * high_rows, high_rows, 0).astype(F32)
        for k in range(places)
    ]
    head_parts = exchange(head_blocks, "xy")
    project_came = swap(project_grad_far, "core", 1)

    expand_grad_own, expand_grad_far, tap_grad_two, hidden_one, route_grad_in = call(
        second_back,
        (tiles,),
        [
            across(deep_grad), across(scale), whole(unit_grad), tiled(excite_in), whole(count),
            whole(mask), across(conv_two), across(mixed_two), tap_tile(second_taps),
            whole(mixed_in), tiled(expand_own), tiled(expand_far), whole(twice_one),
            whole(gates_one), whole(gate_one), whole(gate_sums), whole(route_in), whole(mean_one),
        ],
        [
            out_tiled(HALF * C0, F32),
            out_tiled(HALF * C0, F32),
            out_across(TAPS, F32),
            out_full((rows, C0), BF16),
            out_full((C0, NE), F32),
        ],
        [
            pltpu.VMEM((rows, tile), F32), pltpu.VMEM((rows, tile), F32),
            pltpu.VMEM((rows, wide), BF16), pltpu.VMEM((wide, HALF * C0), BF16),
            pltpu.VMEM((wide, HALF * C0), BF16),
        ],
        "second_back",
        38,
    )
    hidden_one, project_came, head_parts = meet(hidden_one, project_came, head_parts)
    head_shard = lax.psum_scatter(added(head_parts), "chan", scatter_dimension=0, tiled=True)
    project_parts = exchange(pair_sum(project_grad_own, project_came, places), "xy")
    expand_came = swap(expand_grad_far, "core", 1)

    def first_back_tiles(start, count_, hidden_one):
        def shifted(array):
            return (array, (tile, array.shape[1]), lambda i: (i + start, 0))

        return call(
            first_back,
            (count_,),
            [
                whole(x), shifted(left), shifted(right),
                (first_taps, (TAPS, 8, tile), lambda i: (0, 0, i + start)), whole(mask),
                (conv_one, (rows, tile), lambda i: (0, i + start)), whole(hidden_one),
            ],
            [
                ((count_ * tile, 2 * C0), F32, (tile, 2 * C0), lambda i: (i, 0)),
                ((TAPS, count_ * tile), F32, (TAPS, tile), lambda i: (0, i)),
            ],
            [
                pltpu.VMEM((rows, tile), F32), pltpu.VMEM((rows, tile), F32),
                pltpu.VMEM((rows, tile), F32), pltpu.VMEM((rows, tile), BF16),
            ],
            "first_back",
            10 * count_,
        )

    start_grad, tap_grad_start = first_back_tiles(0, tiles - 1, hidden_one)
    start_grad, tap_grad_start, hidden_one, project_parts, expand_came = meet(
        start_grad, tap_grad_start, hidden_one, project_parts, expand_came
    )
    expand_parts = exchange(pair_sum(expand_grad_own, expand_came, places), "xy")
    project_middle = added(project_parts)
    end_grad, tap_grad_end = first_back_tiles(tiles - 1, 1, hidden_one)
    end_grad, tap_grad_end, expand_parts = meet(end_grad, tap_grad_end, expand_parts)
    weight_grad = joined([start_grad, end_grad])
    tap_grad_one = jnp.concatenate([tap_grad_start, tap_grad_end], 1)

    small_width = 3 * LANES
    tap_grads = jnp.concatenate([tap_grad_one, tap_grad_two], 0).T
    left_grad = jnp.concatenate([weight_grad[:, :C0], tap_grads], 1)
    left_grad = jnp.pad(left_grad, ((0, 0), (0, small_width - left_grad.shape[1])))
    right_grad = jnp.concatenate([weight_grad[:, C0:], excite_grad], 1)
    right_grad = jnp.pad(right_grad, ((0, 0), (0, small_width - right_grad.shape[1])))
    small_own = jnp.where(first_core, left_grad, right_grad)
    small_came = swap(jnp.where(first_core, right_grad, left_grad), "core", 1)
    small_came, head_shard = meet(small_came, head_shard)
    small_parts = exchange(pair_sum(small_own, small_came, places), "xy")
    project_parts = exchange(split(project_middle, chans), "chan")
    small_parts, project_parts = meet(small_parts, project_parts)
    project_shard = added(project_parts)
    small_middle = added(small_parts)
    mixed_middle = jnp.concatenate([small_middle, added(expand_parts)], 1)
    mixed_parts = exchange(split(mixed_middle, chans), "chan")
    project_low = copies(project_shard.astype(BF16), "xy")
    mixed_parts, project_low = meet(mixed_parts, project_low)
    mixed_shard = added(mixed_parts)
    mixed_low = copies(mixed_shard.astype(BF16), "xy")

    shards = (head_shard, project_shard, mixed_shard)
    squares = sum(jnp.sum(shard * shard) for shard in shards)
    route_grad_in = jnp.where(first_core, route_grad_in, jnp.roll(route_grad_in, HALF, axis=1))
    route_grad = jnp.concatenate([route_grad_in, route_grad_out], 0)
    scalars = jnp.concatenate([squares[None], jnp.sum(losses, 0)])
    packed = jnp.concatenate([route_grad.reshape(-1, LANES), jnp.pad(scalars, (0, LANES - 3))[None]])
    packed = total_sum(packed)
    route_sum = packed[:-1].reshape(route_grad.shape)
    loss_total, weight_total = packed[-1, 1], packed[-1, 2]
    *head_out, clip_pair = adamw_head(
        packed, head_shard, head_master.T, head_first.T, head_second.T, head_average.T
    )
    clip_norm, factor = clip_pair[0, 0], clip_pair[0, 1]

    if height % 8 == 0:
        line, spot = height, jnp.stack([place, core])
        project_mine, mixed_mine = joined(project_low), joined(mixed_low)
    else:
        line, spot = column.shape[0], jnp.stack([jnp.zeros_like(place), core])
        project_mine, mixed_mine = in_order(project_low), in_order(mixed_low)
    project_pair = [project_mine, swap(project_mine, "core", 1)]
    mixed_pair = [mixed_mine, swap(mixed_mine, "core", 1)]
    column_out = adamw(
        clip_pair,
        spot,
        line,
        mixed_pair,
        (
            (0, 0, 0, C0 + 2 * TAPS),
            (1, 0, C0, SE),
            (0, 0, small_width, HALF * C0),
            (1, 0, small_width, HALF * C0),
        ),
        column,
        column_first.T,
        column_second.T,
        column_average.T,
    )
    row_out = adamw(
        clip_pair,
        spot,
        line,
        mixed_pair + project_pair,
        ((1, 0, 0, C0), (1, 0, C0 + SE, SE), (0, 1, 0, HALF * C2), (1, 1, 0, HALF * C2)),
        row_master,
        row_first,
        row_second,
        row_average,
    )
    route_out_new = adamw_values(
        route_master, route_first, route_second, route_average, route_sum * factor
    )
    return (
        *[value.T for value in column_out],
        *row_out,
        *[value.T for value in head_out],
        *route_out_new,
        loss_total,
        weight_total,
        clip_norm,
    )


def solution(mesh):
    groups = mesh.devices.shape[0] // 2
    fine = Mesh(
        mesh.devices.reshape(groups, 2, mesh.devices.shape[1]), ("xy", "core", "chan")
    )
    dp = ("xy", "core")
    every = ("xy", "core", "chan")
    column, row, head_spec = P(None, "chan"), P("chan", None), P(None, every)
    return jax.shard_map(
        on_device,
        mesh=fine,
        in_specs=(P(dp, "chan", None), P(dp), P(dp), P())
        + (column,) * 4
        + (row,) * 4
        + (head_spec,) * 4
        + (P(),) * 4,
        out_specs=(column,) * 5 + (row,) * 5 + (head_spec,) * 5 + (P(),) * 8,
        check_vma=False,
    )
```

```python
import functools
import math

import jax
import jax.numpy as jnp
from jax import lax
from jax.experimental import pallas as pl
from jax.experimental.pallas import tpu as pltpu
from jax.sharding import Mesh
from jax.sharding import PartitionSpec as P

C0 = 192
C2 = 320
SE = 48
CLASSES = 1000
NE = 8
HALF = NE // 2
KERNEL = 5
TAPS = KERNEL * KERNEL
MAP = 8
STEP = 10
LANES = 128

HIGH = lax.Precision.HIGHEST
BETA_ONE = 0.9
BETA_TWO = 0.999
EPSILON = 1e-08
DECAY = 0.05
RATE = 0.05
CLIP = 0.02
SMOOTH = 0.9

F32 = jnp.float32
BF16 = jnp.bfloat16
FLOPS_A_MICRO = 1.1e9
HBM = "hbm"
VMEM_BYTES = 60 * 1024 * 1024


def nn(left, right):
    return jnp.dot(left, right, preferred_element_type=F32)


def nt(left, right):
    return lax.dot_general(left, right, (((1,), (1,)), ((), ())), preferred_element_type=F32)


def high_nn(left, right):
    return jnp.dot(left, right, precision=HIGH, preferred_element_type=F32)


def high_nt(left, right):
    return lax.dot_general(
        left, right, (((1,), (1,)), ((), ())), precision=HIGH, preferred_element_type=F32
    )


def high_tn(left, right):
    return lax.dot_general(
        left, right, (((0,), (0,)), ((), ())), precision=HIGH, preferred_element_type=F32
    )


def turn(values):
    return values.T


def sig(values):
    return 0.5 * jnp.tanh(0.5 * values) + 0.5


def slope(values, gate):
    return gate * (1.0 + values * (1.0 - gate))


def loop(count, body):
    def step(index, carry):
        body(index)
        return carry

    lax.fori_loop(0, count, step, 0)


def rows_at(index, count):
    return pl.ds(pl.multiple_of(index * count, count), count)


def lanes_at(index):
    return pl.ds(pl.multiple_of(index * LANES, LANES), LANES)


def depthwise(source, taps, lanes, batch, flip, emit):
    parts = batch // 8
    weights = [taps[TAPS - 1 - t if flip else t, :, lanes] for t in range(TAPS)]
    for down in range(MAP):
        total = {}
        for step_y in range(-2, 3):
            line = down + step_y
            if not 0 <= line < MAP:
                continue
            for spot in range(MAP):
                for part in range(parts):
                    value = source[pl.ds((line * MAP + spot) * batch + 8 * part, 8), lanes]
                    for step_x in range(-2, 3):
                        place = spot - step_x
                        if not 0 <= place < MAP:
                            continue
                        term = value * weights[(step_y + 2) * KERNEL + step_x + 2]
                        key = (place, part)
                        total[key] = total[key] + term if key in total else term
        for (place, part), value in total.items():
            emit((down * MAP + place) * batch + 8 * part, value)


def depthwise_weight(source, grad, lanes, batch, store):
    parts = batch // 8
    for step_y in range(-2, 3):
        total = {}
        for down in range(MAP):
            line = down + step_y
            if not 0 <= line < MAP:
                continue
            for part in range(parts):
                slopes = [
                    grad[pl.ds((down * MAP + spot) * batch + 8 * part, 8), lanes]
                    for spot in range(MAP)
                ]
                for spot in range(MAP):
                    value = source[pl.ds((line * MAP + spot) * batch + 8 * part, 8), lanes]
                    for step_x in range(-2, 3):
                        place = spot - step_x
                        if not 0 <= place < MAP:
                            continue
                        key = (step_x, spot % 2)
                        term = value * slopes[place]
                        total[key] = total[key] + term if key in total else term
        for step_x in range(-2, 3):
            value = total[(step_x, 0)] + total[(step_x, 1)]
            store((step_y + 2) * KERNEL + step_x + 2, jnp.sum(value, axis=0, keepdims=True))


def pair_gates(gates, width):
    batch = gates.shape[0]
    spots = lax.broadcasted_iota(jnp.int32, (batch, 2 * width), 1)
    out = []
    for pair in range(HALF):
        left = jnp.broadcast_to(gates[:, 2 * pair : 2 * pair + 1], (batch, 2 * width))
        right = jnp.broadcast_to(gates[:, 2 * pair + 1 : 2 * pair + 2], (batch, 2 * width))
        out.append(jnp.where(spots < width, left, right))
    return out


def split_sums(values, width):
    columns = []
    for value in values:
        spots = lax.broadcasted_iota(jnp.int32, value.shape, 1)
        columns.append(jnp.sum(jnp.where(spots < width, value, 0.0), axis=1, keepdims=True))
        columns.append(jnp.sum(jnp.where(spots < width, 0.0, value), axis=1, keepdims=True))
    return jnp.concatenate(columns, axis=1)


def grouped(values, batch):
    return values.reshape(values.shape[0] // batch, batch, values.shape[1])


def flat(values):
    return values.reshape(values.shape[0] * values.shape[1], values.shape[2])


def first_forward(
    x_ref, left_ref, right_ref, taps_ref, mask_ref, count_ref, route_ref,
    conv_ref, wide_ref, twice_ref, mean_ref, gate_ref, small_gates_ref, large_gates_ref,
    act, deep, total,
):
    batch, tile = count_ref.shape[0], act.shape[1]
    line = MAP * batch
    step = pl.program_id(0)

    act[...] = nt(x_ref[...], left_ref[:, :C0])

    def expand(index):
        rows = rows_at(index, line)
        for part in range(tile // LANES):
            lanes = slice(part * LANES, (part + 1) * LANES)
            here = act[rows, lanes]
            act[rows, lanes] = here * sig(here) * mask_ref[rows, :]

    loop(MAP, expand)

    def conv(index):
        lanes = lanes_at(index)

        def emit(row, value):
            conv_ref[pl.ds(row, 8), lanes] = value

        depthwise(act, taps_ref, lanes, batch, False, emit)

    loop(tile // LANES, conv)

    def activate(index):
        rows = rows_at(index, line)
        for part in range(tile // LANES):
            lanes = slice(part * LANES, (part + 1) * LANES)
            here = conv_ref[rows, lanes]
            deep[rows, lanes] = (here * sig(here) * mask_ref[rows, :]).astype(BF16)

    loop(MAP, activate)
    part_sum = nn(deep[...], right_ref[:, :C0])

    @pl.when(step == 0)
    def _():
        total[...] = part_sum

    @pl.when(step > 0)
    def _():
        total[...] += part_sum

    @pl.when(step == pl.num_programs(0) - 1)
    def _():
        mean_ref[...] = jnp.zeros_like(mean_ref)

        def finish(index):
            rows = rows_at(index, line)
            value = x_ref[rows, :].astype(F32) + total[rows, :]
            low = value.astype(BF16)
            twice_ref[rows, :C0] = low
            twice_ref[rows, C0:] = low
            for part in range(2):
                lanes = slice(0, LANES) if part == 0 else slice(LANES, C0)
                kept = value[:, lanes] * mask_ref[rows, : lanes.stop - lanes.start]
                mean_ref[:, lanes] += jnp.sum(grouped(kept, batch), axis=0)

        loop(MAP, finish)
        mean_ref[...] = mean_ref[...] / count_ref[:, :1]
        gates = jax.nn.sigmoid(high_nn(mean_ref[...], route_ref[...]))
        gate_ref[...] = gates
        for pair, value in enumerate(pair_gates(gates, C0)):
            small_gates_ref[pair] = value
        for pair, value in enumerate(pair_gates(gates, C2)):
            large_gates_ref[pair] = value

        def widen(index):
            rows = rows_at(index, line)
            value = grouped(twice_ref[rows, :].astype(F32), batch)
            for pair in range(HALF):
                lanes = slice(pair * 2 * C0, (pair + 1) * 2 * C0)
                wide_ref[rows, lanes] = flat(value * small_gates_ref[pair][None]).astype(BF16)

        loop(MAP, widen)


def second_forward(
    wide_ref, own_ref, far_ref, taps_ref, mask_ref, count_ref, squeeze_ref, excite_ref,
    mixed_ref, conv_ref, mean_ref, units_ref, scale_ref,
    act,
):
    batch, tile = count_ref.shape[0], act.shape[1]
    line = MAP * batch
    step = pl.program_id(0)
    half = own_ref.shape[1]

    def expand(index):
        rows = rows_at(index, 4 * line)
        mixed_ref[rows, :] = nt(wide_ref[rows, :half], own_ref[...]) + nt(
            wide_ref[rows, half:], far_ref[...]
        )

    loop(MAP // 4, expand)

    def activate(index):
        rows = rows_at(index, line)
        for part in range(tile // LANES):
            lanes = slice(part * LANES, (part + 1) * LANES)
            here = mixed_ref[rows, lanes]
            act[rows, lanes] = here * sig(here) * mask_ref[rows, :]

    loop(MAP, activate)

    def conv(index):
        lanes = lanes_at(index)

        def emit(row, value):
            conv_ref[pl.ds(row, 8), lanes] = value

        depthwise(act, taps_ref, lanes, batch, False, emit)

    loop(tile // LANES, conv)
    mean_ref[...] = jnp.zeros_like(mean_ref)

    def pool(index):
        rows = rows_at(index, line)
        for part in range(tile // LANES):
            lanes = slice(part * LANES, (part + 1) * LANES)
            here = conv_ref[rows, lanes]
            kept = here * sig(here) * mask_ref[rows, :]
            mean_ref[:, lanes] += jnp.sum(grouped(kept, batch), axis=0)

    loop(MAP, pool)
    mean_ref[...] = mean_ref[...] / count_ref[:, :1]
    units = high_nn(mean_ref[...], squeeze_ref[...])

    @pl.when(step == 0)
    def _():
        units_ref[...] = units

    @pl.when(step > 0)
    def _():
        units_ref[...] += units

    @pl.when(step == pl.num_programs(0) - 1)
    def _():
        value = units_ref[...]
        scale_ref[...] = jax.nn.sigmoid(high_nt(value * jax.nn.sigmoid(value), excite_ref[...]))


def project(
    conv_ref, scale_ref, own_ref, far_ref, mask_ref, count_ref, gates_ref, route_ref,
    each_ref, twice_ref, mean_ref, gate_ref, head_gates_ref,
    scaled,
):
    batch = count_ref.shape[0]
    line = MAP * batch
    block, width = scaled.shape
    step = pl.program_id(0)

    def activate(index):
        rows = rows_at(index, line)
        for part in range(width // LANES):
            lanes = slice(part * LANES, (part + 1) * LANES)
            here = conv_ref[rows, lanes]
            kept = grouped(here * sig(here) * mask_ref[rows, :], batch)
            scaled[rows, lanes] = flat(kept * scale_ref[:, lanes][None]).astype(BF16)

    loop(block // line, activate)
    pairs = HALF // 2

    @pl.when(step == 0)
    def _():
        mean_ref[...] = jnp.zeros_like(mean_ref)

    value = scaled[...]
    total = None
    for pair in range(HALF):
        weights = own_ref if pair < pairs else far_ref
        inner = slice((pair % pairs) * 2 * C2, (pair % pairs + 1) * 2 * C2)
        each = nn(value, weights[:, inner])
        each_ref[:, pair * 2 * C2 : (pair + 1) * 2 * C2] = each.astype(BF16)
        term = grouped(each, batch) * gates_ref[pair][None]
        total = term if total is None else total + term
    total = flat(total)
    value = total[:, :C2] + total[:, C2:]
    low = value.astype(BF16)
    twice_ref[:, :C2] = low
    twice_ref[:, C2:] = low
    kept = grouped(value * mask_ref[:, :1], batch)
    mean_ref[...] += jnp.sum(kept, axis=0)

    @pl.when(step == pl.num_programs(0) - 1)
    def _():
        mean_ref[...] = mean_ref[...] / count_ref[:, :1]
        gates = jax.nn.sigmoid(high_nn(mean_ref[...], route_ref[...]))
        gate_ref[...] = gates
        for pair, value in enumerate(pair_gates(gates, C2)):
            head_gates_ref[pair] = value


def head(
    twice_ref, near_ref, distant_ref, mask_ref, count_ref, label_ref, class_ref,
    gates_ref, gate_ref, mean_ref, route_ref,
    own_grad_ref, far_grad_ref, loss_ref, hidden_grad_ref, route_grad_ref,
    weights, wide_ref, mixed, slopes, turned, pooled, total, means, logit_slopes, arrivals,
):
    batch = count_ref.shape[0]
    line = MAP * batch
    step = pl.program_id(0)
    half = near_ref.shape[0]
    experts = NE * C2
    columns = own_grad_ref.shape[1]

    @pl.when(step == 0)
    def _():
        loads = [
            pltpu.make_async_copy(
                source, weights.at[pl.ds(side * half, half), :], arrivals.at[side]
            )
            for side, source in enumerate((near_ref, distant_ref))
        ]
        for load in loads:
            load.start()
        pooled[...] = jnp.zeros_like(pooled)

        def widen(index):
            rows = rows_at(index, line)
            value = grouped(twice_ref[rows, :].astype(F32), batch)
            for pair in range(HALF):
                lanes = slice(pair * 2 * C2, (pair + 1) * 2 * C2)
                wide_ref[rows, lanes] = flat(value * gates_ref[pair][None]).astype(BF16)

        loop(MAP, widen)
        for load in loads:
            load.wait()

        def expand(index):
            rows = rows_at(index, 4 * line)
            mixed[rows, :] = nt(wide_ref[rows, :], weights[:, :experts])

        loop(MAP // 4, expand)

        def pool(index):
            rows = rows_at(index, line)
            for part in range(2 * half // LANES):
                lanes = slice(part * LANES, (part + 1) * LANES)
                here = mixed[rows, lanes]
                kept = here * sig(here) * mask_ref[rows, :]
                pooled[:, lanes] += jnp.sum(grouped(kept, batch), axis=0)

        loop(MAP, pool)
        mean = (pooled[...] / count_ref[:, :1]).astype(BF16)
        logits = nn(mean, weights[:, experts : experts + CLASSES])
        spots = lax.broadcasted_iota(jnp.int32, logits.shape, 1)
        onehot = (spots == label_ref[...]).astype(F32)
        weight = jnp.sum(onehot * class_ref[...], axis=1, keepdims=True)
        top = jnp.max(logits, axis=1, keepdims=True)
        powers = jnp.exp(logits - top)
        summed = jnp.sum(powers, axis=1, keepdims=True)
        loss = weight * (top + jnp.log(summed) - jnp.sum(logits * onehot, axis=1, keepdims=True))
        loss_ref[...] = jnp.concatenate([loss, weight], axis=1)
        logit_grad = (weight * (powers / summed - onehot)).astype(BF16)
        means[...] = mean
        logit_slopes[...] = jnp.zeros_like(logit_slopes)
        logit_slopes[:, :CLASSES] = logit_grad
        pooled[...] = nt(logit_grad, weights[:, experts : experts + CLASSES]) / count_ref[:, :1]

        def back(index):
            rows = rows_at(index, line)
            for part in range(2 * half // LANES):
                lanes = slice(part * LANES, (part + 1) * LANES)
                here = mixed[rows, lanes]
                value = grouped(mask_ref[rows, :] * slope(here, sig(here)), batch)
                slopes[rows, lanes] = flat(value * pooled[:, lanes][None]).astype(BF16)

        loop(MAP, back)
        for part in range(2 * half // LANES):
            lanes = slice(part * LANES, (part + 1) * LANES)
            turned[lanes, :] = turn(slopes[:, lanes])

    blocks = pl.num_programs(0) // 2
    side = 1 - step // blocks
    block = step % blocks
    place = pl.ds(pl.multiple_of(side * half, half), half)

    def weight_grad(out):
        for index in range(2):

            @pl.when(block == index)
            def _(index=index):
                begin = index * columns
                width = min(columns, experts - begin)
                out[:, :width] = nn(turned[place, :], wide_ref[:, begin : begin + width]).astype(
                    out.dtype
                )
                if width < columns:
                    out[:, width:] = lax.dot_general(
                        means[:, place], logit_slopes[...],
                        (((0,), (0,)), ((), ())), preferred_element_type=F32,
                    ).astype(out.dtype)

    @pl.when(side == 1)
    def _():
        weight_grad(far_grad_ref)

    @pl.when(side == 0)
    def _():
        weight_grad(own_grad_ref)

    @pl.when(step == pl.num_programs(0) - 1)
    def _():
        sums = [jnp.zeros((batch, 2 * C2), F32)] * HALF

        def pull(index, sums):
            rows = rows_at(index, 2 * line)
            value = slopes[rows, :]
            hidden = grouped(twice_ref[rows, :].astype(F32), batch)
            summed = None
            sums = list(sums)
            for pair in range(HALF):
                if pair % 2 == 0:
                    begin = pair * 2 * C2
                    both = nn(value, weights[:, begin : begin + 4 * C2])
                each = grouped(both[:, 2 * C2 * (pair % 2) : 2 * C2 * (pair % 2 + 1)], batch)
                sums[pair] = sums[pair] + jnp.sum(each * hidden, axis=0)
                term = each * gates_ref[pair][None]
                summed = term if summed is None else summed + term
            summed = flat(summed)
            total[rows, :] = summed[:, :C2] + summed[:, C2:]
            return tuple(sums)

        sums = lax.fori_loop(0, MAP // 2, pull, tuple(sums))
        gates = gate_ref[...]
        logit = split_sums(sums, C2) * gates * (1.0 - gates)
        route_grad_ref[...] = high_tn(mean_ref[...], logit)
        back_rows = high_nt(logit, route_ref[...]) / count_ref[:, :1]

        def finish(index):
            rows = rows_at(index, line)
            value = grouped(total[rows, :], batch) + back_rows[None] * grouped(
                jnp.broadcast_to(mask_ref[rows, :1], (line, C2)), batch
            )
            low = flat(value).astype(BF16)
            hidden_grad_ref[rows, :C2] = low
            hidden_grad_ref[rows, C2:] = low

        loop(MAP, finish)


def project_back(
    hidden_ref, gates_ref, far_each_ref, own_ref, far_ref, conv_ref, scale_ref, mask_ref,
    full_scale_ref, units_ref, mean_ref, excite_ref,
    grad_ref, own_grad_ref, far_grad_ref, gate_sum_ref, unit_grad_ref, small_ref,
    spread, scaled, sums, each_ref, arrival,
):
    batch, tile = scale_ref.shape
    line = MAP * batch
    step = pl.program_id(0)
    half = own_ref.shape[1]
    arriving = pltpu.make_async_copy(far_each_ref, each_ref, arrival)

    @pl.when(step == 0)
    def _():
        arriving.start()

        def widen(index):
            rows = rows_at(index, line)
            value = grouped(hidden_ref[rows, :].astype(F32), batch)
            for pair in range(HALF):
                lanes = slice(pair * 2 * C2, (pair + 1) * 2 * C2)
                spread[rows, lanes] = flat(value * gates_ref[pair][None]).astype(BF16)

        loop(MAP, widen)

    def pull(index):
        rows = rows_at(index, 4 * line)
        grad_ref[rows, :] = nt(spread[rows, :half], own_ref[...]) + nt(
            spread[rows, half:], far_ref[...]
        )

    loop(MAP // 4, pull)
    place = pl.ds(pl.multiple_of(step * tile, tile), tile)
    sums[:, place] = jnp.zeros((batch, tile), F32)

    def activate(index):
        rows = rows_at(index, line)
        for part in range(tile // LANES):
            lanes = slice(part * LANES, (part + 1) * LANES)
            here = conv_ref[rows, lanes]
            kept = here * sig(here) * mask_ref[rows, :]
            scaled[rows, lanes] = flat(grouped(kept, batch) * scale_ref[:, lanes][None]).astype(BF16)
            added = jnp.sum(grouped(grad_ref[rows, lanes] * kept, batch), axis=0)
            sums[:, pl.ds(pl.multiple_of(step * tile + part * LANES, LANES), LANES)] += added

    loop(MAP, activate)
    turned = turn(scaled[...])
    far_grad_ref[...] = nn(turned, spread[:, half:])
    own_grad_ref[...] = nn(turned, spread[:, :half])

    @pl.when(step == pl.num_programs(0) - 1)
    def _():
        arriving.wait()
        gate_sum_ref[...] = jnp.zeros_like(gate_sum_ref)

        def weigh(index):
            rows = rows_at(index, line)
            value = grouped(hidden_ref[rows, :].astype(F32), batch)
            for pair in range(HALF):
                lanes = slice(pair * 2 * C2, (pair + 1) * 2 * C2)
                each = grouped(each_ref[rows, lanes].astype(F32), batch)
                gate_sum_ref[pair] += jnp.sum(each * value, axis=0)

        loop(MAP, weigh)
        scale = full_scale_ref[...]
        pre = sums[...] * scale * (1.0 - scale)
        units = units_ref[...]
        gate = jax.nn.sigmoid(units)
        unit_grad = high_nn(pre, excite_ref[...]) * slope(units, gate)
        unit_grad_ref[...] = unit_grad
        small_ref[:, :SE] = high_tn(pre, units * gate)
        small_ref[:, SE:] = high_tn(mean_ref[...], unit_grad)


def second_back(
    grad_ref, scale_ref, unit_grad_ref, squeeze_ref, count_ref, mask_ref, conv_ref, mixed_ref,
    taps_ref, wide_ref, own_ref, far_ref, twice_ref, gates_ref, gate_ref, gate_sum_ref,
    route_ref, mean_ref,
    own_grad_ref, far_grad_ref, tap_grad_ref, hidden_grad_ref, route_grad_ref,
    act, inner, slopes, own_all, far_all,
):
    batch, tile = scale_ref.shape
    line = MAP * batch
    step = pl.program_id(0)
    half = own_ref.shape[1]
    place = pl.ds(pl.multiple_of(step * tile, tile), tile)
    own_all[place, :] = own_ref[...]
    far_all[place, :] = far_ref[...]
    pool_grad = high_nt(unit_grad_ref[...], squeeze_ref[...]) / count_ref[:, :1]

    def activate(index):
        rows = rows_at(index, line)
        for part in range(tile // LANES):
            lanes = slice(part * LANES, (part + 1) * LANES)
            mask = mask_ref[rows, :]
            here = mixed_ref[rows, lanes]
            act[rows, lanes] = here * sig(here) * mask
            here = conv_ref[rows, lanes]
            value = grouped(grad_ref[rows, lanes], batch) * scale_ref[:, lanes][None]
            value = flat(value + pool_grad[:, lanes][None])
            inner[rows, lanes] = value * mask * slope(here, sig(here))

    loop(MAP, activate)

    def conv(index):
        lanes = lanes_at(index)

        def store(tap, value):
            tap_grad_ref[tap : tap + 1, lanes] = value

        depthwise_weight(act, inner, lanes, batch, store)

        def emit(row, value):
            act[pl.ds(row, 8), lanes] = value

        depthwise(inner, taps_ref, lanes, batch, True, emit)

    loop(tile // LANES, conv)

    def deactivate(index):
        rows = rows_at(index, line)
        for part in range(tile // LANES):
            lanes = slice(part * LANES, (part + 1) * LANES)
            here = mixed_ref[rows, lanes]
            value = act[rows, lanes] * mask_ref[rows, :] * slope(here, sig(here))
            slopes[rows, pl.ds(pl.multiple_of(step * tile + part * LANES, LANES), LANES)] = (
                value.astype(BF16)
            )

    loop(MAP, deactivate)
    turned = turn(slopes[:, place])
    far_grad_ref[...] = nn(turned, wide_ref[:, half:])
    own_grad_ref[...] = nn(turned, wide_ref[:, :half])

    @pl.when(step == pl.num_programs(0) - 1)
    def _():
        sums = [jnp.zeros((batch, 2 * C0), F32)] * HALF
        pairs = HALF // 2

        def pull(index, sums):
            rows = rows_at(index, 2 * line)
            value = slopes[rows, :]
            hidden = grouped(twice_ref[rows, :].astype(F32), batch)
            summed = None
            sums = list(sums)
            for pair in range(HALF):
                weights = own_all if pair < pairs else far_all
                lanes = slice((pair % pairs) * 2 * C0, (pair % pairs + 1) * 2 * C0)
                each = grouped(nn(value, weights[:, lanes]), batch)
                sums[pair] = sums[pair] + jnp.sum(each * hidden, axis=0)
                term = each * gates_ref[pair][None]
                summed = term if summed is None else summed + term
            act[rows, : 2 * C0] = flat(summed)
            return tuple(sums)

        sums = lax.fori_loop(0, MAP // 2, pull, tuple(sums))
        gates = gate_ref[...]
        logit = split_sums(sums, C0) + split_sums([gate_sum_ref[k] for k in range(HALF)], C2)
        logit = logit * gates * (1.0 - gates)
        route_grad_ref[...] = high_tn(mean_ref[...], logit)
        back_rows = high_nt(logit, route_ref[...]) / count_ref[:, :1]

        def finish(index):
            rows = rows_at(index, line)
            summed = act[rows, : 2 * C0]
            value = grouped(summed[:, :C0] + summed[:, C0:], batch) + back_rows[None] * grouped(
                jnp.broadcast_to(mask_ref[rows, :1], (line, C0)), batch
            )
            hidden_grad_ref[rows, :] = flat(value).astype(BF16)

        loop(MAP, finish)


def first_back(
    x_ref, left_ref, right_ref, taps_ref, mask_ref, conv_ref, hidden_ref,
    weight_grad_ref, tap_grad_ref,
    act, inner, wide, deep,
):
    tile = act.shape[1]
    batch = x_ref.shape[0] // (MAP * MAP)
    line = MAP * batch

    def expand(index):
        rows = rows_at(index, line)
        for part in range(tile // LANES):
            lanes = slice(part * LANES, (part + 1) * LANES)
            mask = mask_ref[rows, :]
            here = act[rows, lanes]
            gate = sig(here)
            act[rows, lanes] = here * gate * mask
            wide[rows, lanes] = slope(here, gate) * mask
            here = conv_ref[rows, lanes]
            gate = sig(here)
            deep[rows, lanes] = (here * gate * mask).astype(BF16)
            inner[rows, lanes] = inner[rows, lanes] * mask * slope(here, gate)

    act[...] = nt(x_ref[...], left_ref[:, :C0])
    inner[...] = nt(hidden_ref[...], right_ref[:, :C0])
    loop(MAP, expand)
    weight_grad_ref[:, C0:] = nn(turn(deep[...]), hidden_ref[...])

    def conv(index):
        lanes = lanes_at(index)

        def store(tap, value):
            tap_grad_ref[tap : tap + 1, lanes] = value

        depthwise_weight(act, inner, lanes, batch, store)

        def emit(row, value):
            act[pl.ds(row, 8), lanes] = value

        depthwise(inner, taps_ref, lanes, batch, True, emit)

    loop(tile // LANES, conv)

    def deactivate(index):
        rows = rows_at(index, line)
        for part in range(tile // LANES):
            lanes = slice(part * LANES, (part + 1) * LANES)
            deep[rows, lanes] = (act[rows, lanes] * wide[rows, lanes]).astype(BF16)

    loop(MAP, deactivate)
    weight_grad_ref[:, :C0] = nn(turn(deep[...]), x_ref[...])


def adamw_values(master, first, second, average, grad):
    first = BETA_ONE * first + (1.0 - BETA_ONE) * grad
    second = BETA_TWO * second + (1.0 - BETA_TWO) * grad * grad
    ratio = first / (1.0 - BETA_ONE**STEP) / (jnp.sqrt(second / (1.0 - BETA_TWO**STEP)) + EPSILON)
    master = master - RATE * (ratio + DECAY * master)
    average = SMOOTH * average + (1.0 - SMOOTH) * master
    return (first, second, master, average, master.astype(BF16))


def clipped(total):
    routers = total[: total.shape[0] - 1]
    squares, weight = total[total.shape[0] - 1 :, :1], total[total.shape[0] - 1 :, 2:3]
    norm = jnp.sqrt(squares + jnp.sum(routers * routers, keepdims=True)) / weight
    return norm, jnp.minimum(1.0, CLIP / (norm + 1e-06)) / weight


def adamw_kernel(segments, arrays, place_ref, factor_ref, *refs):
    pieces = refs[: 2 * arrays]
    master, first, second, average = refs[2 * arrays : 2 * arrays + 4]
    outs = refs[2 * arrays + 4 : 2 * arrays + 9]
    whole = refs[-1]

    def fill(core):
        at = 0
        for side, array, begin, width in segments:
            source = pieces[2 * array + (side ^ core)]
            whole[:, at : at + width] = source[:, begin : begin + width].astype(F32)
            at += width

    for core in range(2):

        @pl.when(place_ref[1] == core)
        def _(core=core):
            fill(core)

    grad = whole[...] * factor_ref[0, 1]
    values = adamw_values(master[...], first[...], second[...], average[...], grad)
    for out, value in zip(outs, values):
        out[...] = value


def adamw(factor, spot, rows, pieces, segments, master, first, second, average):
    height, width = master.shape
    specs = [
        pl.BlockSpec((rows, piece.shape[1]), lambda i, place: (i ^ place[0], 0)) for piece in pieces
    ]
    full = pl.BlockSpec((rows, width), lambda i, place: (i, 0))
    types = (F32, F32, F32, F32, BF16)
    return pl.pallas_call(
        functools.partial(adamw_kernel, segments, len(pieces) // 2),
        grid_spec=pltpu.PrefetchScalarGridSpec(
            num_scalar_prefetch=1,
            grid=(height // rows,),
            in_specs=[pl.BlockSpec(memory_space=pltpu.SMEM)] + specs + [full] * 4,
            out_specs=[full] * 5,
            scratch_shapes=[pltpu.VMEM((rows, width), F32)],
        ),
        out_shape=[jax.ShapeDtypeStruct((height, width), kind) for kind in types],
        compiler_params=pltpu.CompilerParams(vmem_limit_bytes=VMEM_BYTES),
        name="adamw",
    )(spot, factor, *pieces, master, first, second, average)


def adamw_head_kernel(total_ref, grad, master, first, second, average, *outs):
    norm, factor = clipped(total_ref[...])
    outs[5][...] = jnp.concatenate([norm, factor], axis=1)
    values = adamw_values(master[...], first[...], second[...], average[...], grad[...] * factor)
    for out, value in zip(outs, values):
        out[...] = value


def adamw_head(total, grad, *state):
    height, width = state[0].shape
    part = 14 * LANES
    block = pl.BlockSpec((height, part), lambda i: (0, i))
    types = (F32, F32, F32, F32, BF16)
    return pl.pallas_call(
        adamw_head_kernel,
        grid=(pl.cdiv(width, part),),
        in_specs=[pl.BlockSpec(total.shape, lambda i: (0, 0))] + [block] * 5,
        out_specs=[block] * 5 + [pl.BlockSpec((1, 2), lambda i: (0, 0))],
        out_shape=[jax.ShapeDtypeStruct((height, width), kind) for kind in types]
        + [jax.ShapeDtypeStruct((1, 2), F32)],
        compiler_params=pltpu.CompilerParams(vmem_limit_bytes=VMEM_BYTES),
        name="adamw_head",
    )(total, grad, *state)


def swap(values, axis, distance):
    size = lax.axis_size(axis)
    return lax.ppermute(values, axis, [(i, i ^ distance) for i in range(size)])


def meet(*values):
    return lax.optimization_barrier(values)


def copies(values, axis):
    return [values] + [swap(values, axis, k) for k in range(1, lax.axis_size(axis))]


def joined(parts):
    return jnp.concatenate(parts, axis=0)


def pair_sum(own, came, parts):
    rows = own.shape[0] // parts
    return [own[k * rows : (k + 1) * rows] + came[k * rows : (k + 1) * rows] for k in range(parts)]


def exchange(blocks, axis):
    return [blocks[0]] + [swap(block.astype(BF16), axis, k) for k, block in enumerate(blocks) if k]


def added(parts):
    total = parts[0]
    for value in parts[1:]:
        total = total + value.astype(F32)
    return total


def split(values, parts):
    rows = values.shape[0] // parts
    return [values[k * rows : (k + 1) * rows] for k in range(parts)]


def total_sum(values):
    for axis in ("core", "xy", "chan"):
        distance = 1
        while distance < lax.axis_size(axis):
            values = values + swap(values, axis, distance)
            distance *= 2
    return values


def in_order(parts):
    place = lax.axis_index("xy")
    stack = jnp.stack(parts)
    return joined(
        [lax.dynamic_index_in_dim(stack, place ^ k, 0, keepdims=False) for k in range(len(parts))]
    )


def two_parts(values):
    upper = lax.reduce_precision(values, 8, 7)
    return [upper.astype(BF16), (values - upper).astype(BF16)]


def call(kernel, grid, ins, outs, scratch, name, micros):
    def spec(shape, block, index):
        if block is HBM:
            return pl.BlockSpec(memory_space=pl.ANY)
        if block is None:
            return pl.BlockSpec(memory_space=pltpu.VMEM)
        return pl.BlockSpec(block, index)

    in_specs = []
    arrays = []
    for entry in ins:
        array, block, index, *mode = entry
        arrays.append(array)
        if mode:
            in_specs.append(pl.BlockSpec(block, index, pipeline_mode=mode[0]))
        else:
            in_specs.append(spec(array.shape, block, index))
    return pl.pallas_call(
        kernel,
        grid=grid,
        in_specs=in_specs,
        out_specs=[spec(shape, block, index) for shape, kind, block, index in outs],
        out_shape=[jax.ShapeDtypeStruct(shape, kind) for shape, kind, block, index in outs],
        scratch_shapes=scratch,
        compiler_params=pltpu.CompilerParams(
            vmem_limit_bytes=VMEM_BYTES, dimension_semantics=("arbitrary",) * len(grid)
        ),
        cost_estimate=pl.CostEstimate(
            flops=int(micros * FLOPS_A_MICRO), bytes_accessed=1 << 20, transcendentals=0
        ),
        name=name,
    )(*arrays)


def on_device(
    images,
    labels,
    resolution,
    class_weight,
    column_master,
    column_first,
    column_second,
    column_average,
    row_master,
    row_first,
    row_second,
    row_average,
    head_master,
    head_first,
    head_second,
    head_average,
    route_master,
    route_first,
    route_second,
    route_average,
):
    chans, places = lax.axis_size("chan"), lax.axis_size("xy")
    core, place, layer = lax.axis_index("core"), lax.axis_index("xy"), lax.axis_index("chan")
    first_core = core == 0
    batch = images.shape[0] // chans
    slots = MAP * MAP
    rows = slots * batch
    wide = column_master.shape[1] * chans
    height = column_master.shape[1] // places
    begin = C0 + 2 * TAPS + SE
    tile = 3 * LANES
    tiles = wide // tile

    def fixed(array):
        return (array, None, None)

    def whole(array, grid=1):
        zeros = (0,) * array.ndim
        return (array, array.shape, lambda *ids: zeros, pl.Buffered(1))

    column, row = column_master.T, row_master
    column_parts = [column[:, :C0]]
    column_parts += two_parts(column[:, C0 : C0 + 2 * TAPS])
    small_left = jnp.concatenate([part.astype(BF16) for part in column_parts], 1)
    small_left = jnp.pad(small_left, ((0, 0), (0, 2 * C0 - small_left.shape[1])))
    small_right = jnp.concatenate(
        [row[:, :C0].astype(BF16)]
        + two_parts(column[:, C0 + 2 * TAPS : begin])
        + two_parts(row[:, C0 : C0 + SE]),
        1,
    )
    small = lax.dynamic_slice_in_dim(
        jnp.where(first_core, small_left, small_right), place * height, height, 0
    )
    expand_own = lax.dynamic_slice(
        column, (place * height, begin + core * HALF * C0), (height, HALF * C0)
    ).astype(BF16)
    first_own = jnp.concatenate([expand_own, small], 1)
    project_own = lax.dynamic_slice(
        row, (place * height, C0 + SE + core * HALF * C2), (height, HALF * C2)
    ).astype(BF16)
    blocks = 2
    part = pl.cdiv(NE * C2 + CLASSES, blocks * LANES) * LANES
    lanes = blocks * part
    head_own = jnp.pad(head_master.T.astype(BF16), ((0, 0), (0, lanes - NE * C2 - CLASSES)))
    mine = lax.all_to_all(images, "chan", 0, 0, tiled=True)
    first_own, project_own, head_own = meet(
        copies(first_own, "chan"), [project_own, swap(project_own, "chan", 1)], head_own
    )
    first_own = copies(joined(first_own), "xy")
    head_own = lax.all_gather(head_own, "chan", axis=0, tiled=True)
    distance = 2
    while distance < chans:
        held = joined(project_own)
        project_own = [held, swap(held, "chan", distance)]
        distance *= 2
    mine = mine.reshape(chans, batch, slots // chans, C0).transpose(0, 2, 1, 3)
    mine, first_own, project_own, head_own = meet(mine, first_own, project_own, head_own)
    head_own = lax.all_gather(head_own, "xy", axis=0, tiled=True)
    first_own, project_own = joined(first_own), joined(project_own)
    first_far = swap(first_own, "core", 1)
    project_own = copies(project_own, "xy")
    small, small_far = first_own[:, HALF * C0 :], first_far[:, HALF * C0 :]
    left = jnp.where(first_core, small, small_far)
    right = jnp.where(first_core, small_far, small)

    def both(values, at, width):
        upper = values[:, at : at + width].astype(F32)
        return upper + values[:, at + width : at + 2 * width].astype(F32)

    def tap_rows(values):
        return jnp.broadcast_to(values.T[:, None, :], (TAPS, 8, wide))

    taps = both(left, C0, 2 * TAPS)
    first_taps, second_taps = tap_rows(taps[:, :TAPS]), tap_rows(taps[:, TAPS:])
    excite_out = both(right, C0, SE)
    excite_in = both(right, C0 + 2 * SE, SE)
    route_in, route_out = route_master[:C0], route_master[C0:]
    route_in = jnp.where(first_core, route_in, jnp.roll(route_in, HALF, axis=1))

    label = lax.dynamic_slice_in_dim(labels, layer * batch, batch, 0)
    side = lax.dynamic_slice_in_dim(resolution, layer * batch, batch, 0)
    spots = jnp.arange(slots, dtype=jnp.int32)
    inside = ((spots // MAP)[:, None] < side[None, :]) & ((spots % MAP)[:, None] < side[None, :])
    inside = inside.reshape(rows, 1)
    x = jnp.where(inside, mine.reshape(rows, C0), 0)
    mask = jnp.broadcast_to(inside.astype(F32), (rows, LANES))
    count = jnp.broadcast_to((side * side).astype(F32)[:, None], (batch, LANES))

    def tiled(array):
        return (array, (tile, array.shape[1]), lambda i: (i, 0))

    def experts(array):
        return (array, (tile, HALF * C0), lambda i: (i, 0))

    def across(array):
        return (array, (array.shape[0], tile), lambda i: (0, i))

    def tap_tile(array):
        return (array, (TAPS, 8, tile), lambda i: (0, 0, i))

    def out_full(shape, kind):
        zeros = (0,) * len(shape)
        return (shape, kind, shape, lambda *ids: zeros)

    def out_across(height_, kind):
        return ((height_, wide), kind, (height_, tile), lambda i: (0, i))

    def out_tiled(width, kind):
        return ((wide, width), kind, (tile, width), lambda i: (i, 0))

    first_out = call(
        first_forward,
        (tiles,),
        [
            whole(x), tiled(left), tiled(right), tap_tile(first_taps), whole(mask), whole(count),
            whole(route_in),
        ],
        [
            out_across(rows, F32),
            out_full((rows, NE * C0), BF16),
            out_full((rows, 2 * C0), BF16),
            out_full((batch, C0), F32),
            out_full((batch, NE), F32),
            out_full((HALF, batch, 2 * C0), F32),
            out_full((HALF, batch, 2 * C2), F32),
        ],
        [
            pltpu.VMEM((rows, tile), F32), pltpu.VMEM((rows, tile), BF16),
            pltpu.VMEM((rows, C0), F32),
        ],
        "first_forward",
        17,
    )

    (conv_one, mixed_in, twice_one, mean_one, gate_one, gates_one, gates_mid) = first_out

    mixed_two, conv_two, mean_two, units, scale = call(
        second_forward,
        (tiles,),
        [
            whole(mixed_in), experts(first_own), experts(first_far), tap_tile(second_taps),
            whole(mask), whole(count), tiled(excite_in), whole(excite_out),
        ],
        [
            out_across(rows, F32),
            out_across(rows, F32),
            out_across(batch, F32),
            out_full((batch, SE), F32),
            out_full((batch, wide), F32),
        ],
        [pltpu.VMEM((rows, tile), F32)],
        "second_forward",
        21,
    )

    conv_two, project_own = meet(conv_two, project_own)
    project_own = joined(project_own)
    project_far = swap(project_own, "core", 1)

    line = rows // 4

    def out_rows(width, kind):
        return ((rows, width), kind, (line, width), lambda i: (i, 0))

    def by_rows(array):
        return (array, (line, array.shape[1]), lambda i: (i, 0))

    each, twice_two, mean_three, gate_two, gates_two = call(
        project,
        (rows // line,),
        [
            by_rows(conv_two), whole(scale), whole(project_own), whole(project_far),
            by_rows(mask), whole(count), whole(gates_mid), whole(route_out),
        ],
        [
            out_rows(NE * C2, BF16),
            out_rows(2 * C2, BF16),
            out_full((batch, C2), F32),
            out_full((batch, NE), F32),
            out_full((HALF, batch, 2 * C2), F32),
        ],
        [pltpu.VMEM((line, wide), BF16)],
        "project",
        16,
    )

    twice_two, head_own = meet(twice_two, head_own)
    head_far = swap(head_own, "core", 1)
    half = head_own.shape[0]
    head_grad_own, head_grad_far, losses, hidden_two, route_grad_out = call(
        head,
        (2 * blocks,),
        [
            whole(twice_two), (head_own, HBM, None), (head_far, HBM, None), whole(mask),
            whole(count), whole(label[:, None]), whole(class_weight[None, :]), whole(gates_two),
            whole(gate_two), whole(mean_three), whole(route_out),
        ],
        [
            ((half, lanes), BF16, (half, part), lambda i: (0, jnp.maximum(i - blocks, 0))),
            ((half, lanes), BF16, (half, part), lambda i: (0, jnp.minimum(i, blocks - 1))),
            out_full((batch, 2), F32),
            out_full((rows, 2 * C2), BF16),
            out_full((C2, NE), F32),
        ],
        [
            pltpu.VMEM((2 * half, lanes), BF16), pltpu.VMEM((rows, NE * C2), BF16),
            pltpu.VMEM((rows, 2 * half), F32), pltpu.VMEM((rows, 2 * half), BF16),
            pltpu.VMEM((2 * half, rows), BF16), pltpu.VMEM((batch, 2 * half), F32),
            pltpu.VMEM((rows, C2), F32), pltpu.VMEM((batch, 2 * half), BF16),
            pltpu.VMEM((batch, lanes - NE * C2), BF16), pltpu.SemaphoreType.DMA((2,)),
        ],
        "head",
        39,
    )
    head_came = swap(head_grad_far, "core", 1)

    deep_grad, project_grad_own, project_grad_far, gate_sums, unit_grad, excite_grad = call(
        project_back,
        (tiles,),
        [
            whole(hidden_two), whole(gates_mid), (each, HBM, None), tiled(project_own),
            tiled(project_far), across(conv_two), across(scale), whole(mask), whole(scale),
            whole(units), whole(mean_two), whole(excite_out),
        ],
        [
            out_across(rows, F32),
            out_tiled(HALF * C2, F32),
            out_tiled(HALF * C2, F32),
            out_full((HALF, batch, 2 * C2), F32),
            out_full((batch, SE), F32),
            out_full((wide, 2 * SE), F32),
        ],
        [
            pltpu.VMEM((rows, NE * C2), BF16), pltpu.VMEM((rows, tile), BF16),
            pltpu.VMEM((batch, wide), F32), pltpu.VMEM((rows, NE * C2), BF16),
            pltpu.SemaphoreType.DMA(()),
        ],
        "project_back",
        26,
    )
    deep_grad, head_came = meet(deep_grad, head_came)
    high_rows = half // places
    head_blocks = [
        lax.dynamic_slice_in_dim(head_grad_own, (place ^ k) * high_rows, high_rows, 0).astype(F32)
        + lax.dynamic_slice_in_dim(head_came, (place ^ k) * high_rows, high_rows, 0).astype(F32)
        for k in range(places)
    ]
    head_parts = exchange(head_blocks, "xy")
    project_came = swap(project_grad_far, "core", 1)

    expand_grad_own, expand_grad_far, tap_grad_two, hidden_one, route_grad_in = call(
        second_back,
        (tiles,),
        [
            across(deep_grad), across(scale), whole(unit_grad), tiled(excite_in), whole(count),
            whole(mask), across(conv_two), across(mixed_two), tap_tile(second_taps),
            whole(mixed_in), experts(first_own), experts(first_far), whole(twice_one),
            whole(gates_one), whole(gate_one), whole(gate_sums), whole(route_in), whole(mean_one),
        ],
        [
            out_tiled(HALF * C0, F32),
            out_tiled(HALF * C0, F32),
            out_across(TAPS, F32),
            out_full((rows, C0), BF16),
            out_full((C0, NE), F32),
        ],
        [
            pltpu.VMEM((rows, tile), F32), pltpu.VMEM((rows, tile), F32),
            pltpu.VMEM((rows, wide), BF16), pltpu.VMEM((wide, HALF * C0), BF16),
            pltpu.VMEM((wide, HALF * C0), BF16),
        ],
        "second_back",
        38,
    )
    hidden_one, project_came, head_parts = meet(hidden_one, project_came, head_parts)
    head_shard = lax.psum_scatter(added(head_parts), "chan", scatter_dimension=0, tiled=True)
    project_parts = exchange(pair_sum(project_grad_own, project_came, places), "xy")
    expand_came = swap(expand_grad_far, "core", 1)

    def first_back_tiles(start, count_, hidden_one):
        def shifted(array):
            return (array, (tile, array.shape[1]), lambda i: (i + start, 0))

        return call(
            first_back,
            (count_,),
            [
                whole(x), shifted(left), shifted(right),
                (first_taps, (TAPS, 8, tile), lambda i: (0, 0, i + start)), whole(mask),
                (conv_one, (rows, tile), lambda i: (0, i + start)), whole(hidden_one),
            ],
            [
                ((count_ * tile, 2 * C0), F32, (tile, 2 * C0), lambda i: (i, 0)),
                ((TAPS, count_ * tile), F32, (TAPS, tile), lambda i: (0, i)),
            ],
            [
                pltpu.VMEM((rows, tile), F32), pltpu.VMEM((rows, tile), F32),
                pltpu.VMEM((rows, tile), F32), pltpu.VMEM((rows, tile), BF16),
            ],
            "first_back",
            10 * count_,
        )

    start_grad, tap_grad_start = first_back_tiles(0, tiles - 1, hidden_one)
    start_grad, tap_grad_start, hidden_one, project_parts, expand_came = meet(
        start_grad, tap_grad_start, hidden_one, project_parts, expand_came
    )
    expand_parts = exchange(pair_sum(expand_grad_own, expand_came, places), "xy")
    project_middle = added(project_parts)
    end_grad, tap_grad_end = first_back_tiles(tiles - 1, 1, hidden_one)
    end_grad, tap_grad_end, expand_parts = meet(end_grad, tap_grad_end, expand_parts)
    weight_grad = joined([start_grad, end_grad])
    tap_grad_one = jnp.concatenate([tap_grad_start, tap_grad_end], 1)

    small_width = 3 * LANES
    tap_grads = jnp.concatenate([tap_grad_one, tap_grad_two], 0).T
    left_grad = jnp.concatenate([weight_grad[:, :C0], tap_grads], 1)
    left_grad = jnp.pad(left_grad, ((0, 0), (0, small_width - left_grad.shape[1])))
    right_grad = jnp.concatenate([weight_grad[:, C0:], excite_grad], 1)
    right_grad = jnp.pad(right_grad, ((0, 0), (0, small_width - right_grad.shape[1])))
    small_own = jnp.where(first_core, left_grad, right_grad)
    small_came = swap(jnp.where(first_core, right_grad, left_grad), "core", 1)
    small_came, head_shard = meet(small_came, head_shard)
    small_parts = exchange(pair_sum(small_own, small_came, places), "xy")
    project_parts = exchange(split(project_middle, chans), "chan")
    small_parts, project_parts = meet(small_parts, project_parts)
    project_shard = added(project_parts)
    small_middle = added(small_parts)
    mixed_middle = jnp.concatenate([small_middle, added(expand_parts)], 1)
    mixed_parts = exchange(split(mixed_middle, chans), "chan")
    project_low = copies(project_shard.astype(BF16), "xy")
    mixed_parts, project_low = meet(mixed_parts, project_low)
    mixed_shard = added(mixed_parts)
    mixed_low = copies(mixed_shard.astype(BF16), "xy")

    shards = (head_shard, project_shard, mixed_shard)
    squares = sum(jnp.sum(shard * shard) for shard in shards)
    route_grad_in = jnp.where(first_core, route_grad_in, jnp.roll(route_grad_in, HALF, axis=1))
    route_grad = jnp.concatenate([route_grad_in, route_grad_out], 0)
    scalars = jnp.concatenate([squares[None], jnp.sum(losses, 0)])
    packed = jnp.concatenate([route_grad.reshape(-1, LANES), jnp.pad(scalars, (0, LANES - 3))[None]])
    packed = total_sum(packed)
    route_sum = packed[:-1].reshape(route_grad.shape)
    loss_total, weight_total = packed[-1, 1], packed[-1, 2]
    *head_out, clip_pair = adamw_head(
        packed, head_shard, head_master.T, head_first.T, head_second.T, head_average.T
    )
    clip_norm, factor = clip_pair[0, 0], clip_pair[0, 1]

    if height % 8 == 0:
        line, spot = height, jnp.stack([place, core])
        project_mine, mixed_mine = joined(project_low), joined(mixed_low)
    else:
        line, spot = column.shape[0], jnp.stack([jnp.zeros_like(place), core])
        project_mine, mixed_mine = in_order(project_low), in_order(mixed_low)
    project_pair = [project_mine, swap(project_mine, "core", 1)]
    mixed_pair = [mixed_mine, swap(mixed_mine, "core", 1)]
    column_out = adamw(
        clip_pair,
        spot,
        line,
        mixed_pair,
        (
            (0, 0, 0, C0 + 2 * TAPS),
            (1, 0, C0, SE),
            (0, 0, small_width, HALF * C0),
            (1, 0, small_width, HALF * C0),
        ),
        column,
        column_first.T,
        column_second.T,
        column_average.T,
    )
    row_out = adamw(
        clip_pair,
        spot,
        line,
        mixed_pair + project_pair,
        ((1, 0, 0, C0), (1, 0, C0 + SE, SE), (0, 1, 0, HALF * C2), (1, 1, 0, HALF * C2)),
        row_master,
        row_first,
        row_second,
        row_average,
    )
    route_out_new = adamw_values(
        route_master, route_first, route_second, route_average, route_sum * factor
    )
    return (
        *[value.T for value in column_out],
        *row_out,
        *[value.T for value in head_out],
        *route_out_new,
        loss_total,
        weight_total,
        clip_norm,
    )


def solution(mesh):
    groups = mesh.devices.shape[0] // 2
    fine = Mesh(
        mesh.devices.reshape(groups, 2, mesh.devices.shape[1]), ("xy", "core", "chan")
    )
    dp = ("xy", "core")
    every = ("xy", "core", "chan")
    column, row, head_spec = P(None, "chan"), P("chan", None), P(None, every)
    return jax.shard_map(
        on_device,
        mesh=fine,
        in_specs=(P(dp, "chan", None), P(dp), P(dp), P())
        + (column,) * 4
        + (row,) * 4
        + (head_spec,) * 4
        + (P(),) * 4,
        out_specs=(column,) * 5 + (row,) * 5 + (head_spec,) * 5 + (P(),) * 8,
        check_vma=False,
    )
```
